32 devices in a mesh: seq: 8 (over y, x, core), batch: 4 (over z).
Axes of the slice: x: 2, y: 2, z: 4, core: 2. Of those that a mesh axis runs over, the one named last changes fastest.
Arguments:
- inputs: bfloat16 [4, 6144, 512], P('batch', 'seq'), may hold values from -6 to 6
- cotangent: bfloat16 [4, 6144, 512], P('batch', 'seq'), may hold values from -12 to 12
- ln1_gain: float32 [512], replicated, may hold values from 0.1 to 1.9
- ln1_bias: float32 [512], replicated, may hold values from -3 to 3
- w_query: bfloat16 [512, 512], replicated, may hold values from -0.25 to 0.25
- w_key: bfloat16 [512, 512], replicated, may hold values from -0.25 to 0.25
- w_value: bfloat16 [512, 512], replicated, may hold values from -0.25 to 0.25
- conv_key: bfloat16 [3, 512, 512], replicated, may hold values from -0.15625 to 0.15625
- conv_value: bfloat16 [3, 512, 512], replicated, may hold values from -0.15625 to 0.15625
- w_out: bfloat16 [512, 512], replicated, may hold values from -6 to 6
- ln2_gain: float32 [512], replicated, may hold values from 0.1 to 1.9
- ln2_bias: float32 [512], replicated, may hold values from -3 to 3
- w_up: bfloat16 [512, 2048], replicated, may hold values from -0.25 to 0.25
- up_bias: float32 [2048], replicated, may hold values from -3 to 3
- w_down: bfloat16 [2048, 512], replicated, may hold values from -0.125 to 0.125
- down_bias: float32 [512], replicated, may hold values from -3 to 3
Outputs:
- outputs: bfloat16 [4, 6144, 512], P('batch', 'seq')
- grad_inputs: bfloat16 [4, 6144, 512], P('batch', 'seq')
- grad_ln1_gain: float32 [512], replicated
- grad_ln1_bias: float32 [512], replicated
- grad_w_query: float32 [512, 512], replicated
- grad_w_key: float32 [512, 512], replicated
- grad_w_value: float32 [512, 512], replicated
- grad_conv_key: float32 [3, 512, 512], replicated
- grad_conv_value: float32 [3, 512, 512], replicated
- grad_w_out: float32 [512, 512], replicated
- grad_ln2_gain: float32 [512], replicated
- grad_ln2_bias: float32 [512], replicated
- grad_w_up: float32 [512, 2048], replicated
- grad_up_bias: float32 [2048], replicated
- grad_w_down: float32 [2048, 512], replicated
- grad_down_bias: float32 [512], replicated
The draws below stay inside these ranges and needn't reach their ends.
All inputs are finite; a program needn't handle non-finite values.
Results may differ from the reference program's by a relative error of at most 0.017.
Values may be sent and summed in bfloat16 or wider, within the bound.
No kernel may reach another device: no remote copies, remote signals or barrier semaphores. Data moves between devices by JAX's collectives and lax.ppermute only.
A program may use at most 256 MiB of HBM per device.

```python
import jax
import jax.numpy as jnp
from jax import lax

D = 512
HEADS = 8
HEAD_DIM = 64
FF = 2048
TOK_DEV = 768
LENGTH = 6144
SEQS = 4


def draw_cotangent(key, part):
    key = jax.random.fold_in(key, 7)
    position = jnp.arange(LENGTH, dtype=jnp.float32) / LENGTH
    order = jnp.arange(SEQS, dtype=jnp.float32) / SEQS
    rising = (0.5 + position)[None, :, None] * (0.7 + 0.6 * order)[:, None, None]
    values = rising * jax.random.normal(key, (SEQS, LENGTH, D), dtype=jnp.float32)
    return jnp.clip(values, -12.0, 12.0).astype(jnp.bfloat16)


def block_levels(rng, dims, cuts, smallest, largest):
    loudness = 1.0
    for dim, parts in cuts:
        draws = jax.random.uniform(jax.random.fold_in(jax.random.fold_in(rng, 6), dim), (parts,), jnp.float32, smallest / len(cuts), largest / len(cuts))
        loudness = loudness * jnp.repeat(jnp.exp(draws), dims[dim] // parts).reshape((-1,) + (1,) * (len(dims) - 1 - dim))
    return loudness


def scatter_about(rng, shape, deviation, most, shards=(), kind=jnp.bfloat16):
    entries = jax.random.normal(rng, shape, jnp.float32) * deviation
    if len(shards) > 0:
        entries = block_levels(rng, shape, shards, -0.22, 0.18) * entries
    return jnp.clip(entries, min=-most, max=most).astype(kind)


def setup_inputs(seed: int = 0) -> dict:
    streams_of = jax.random.split(jax.random.key(seed), 17)
    inputs = scatter_about(streams_of[0], (SEQS, LENGTH, D), 1.0, 6.0, ((0, 4), (1, 8)))
    cotangent = draw_cotangent(jax.random.fold_in(streams_of[16], 71), 0)
    ln1_gain = jnp.clip(1.0 + 0.18 * jax.random.normal(streams_of[2], (D,), jnp.float32), 0.1, 1.9)
    ln1_bias = scatter_about(streams_of[3], (D,), 0.5, 3.0, (), jnp.float32)
    w_query = scatter_about(streams_of[4], (D, D), D ** -0.5, 0.25)
    w_key = scatter_about(streams_of[5], (D, D), D ** -0.5, 0.25)
    w_value = scatter_about(streams_of[6], (D, D), D ** -0.5, 0.25)
    conv_key = scatter_about(streams_of[7], (3, D, D), (3 * D) ** -0.5, 0.15625)
    conv_value = scatter_about(streams_of[8], (3, D, D), (3 * D) ** -0.5, 0.15625)
    w_out = scatter_about(streams_of[9], (D, D), 1 ** -0.5, 6.0)
    ln2_gain = jnp.clip(1.0 + 0.18 * jax.random.normal(streams_of[10], (D,), jnp.float32), 0.1, 1.9)
    ln2_bias = scatter_about(streams_of[11], (D,), 0.5, 3.0, (), jnp.float32)
    w_up = scatter_about(streams_of[12], (D, FF), D ** -0.5, 0.25)
    up_bias = scatter_about(streams_of[13], (FF,), 0.5, 3.0, (), jnp.float32)
    w_down = scatter_about(streams_of[14], (FF, D), FF ** -0.5, 0.125)
    down_bias = scatter_about(streams_of[15], (D,), 0.5, 3.0, (), jnp.float32)
    return {"inputs": inputs, "cotangent": cotangent, "ln1_gain": ln1_gain, "ln1_bias": ln1_bias, "w_query": w_query, "w_key": w_key, "w_value": w_value, "conv_key": conv_key, "conv_value": conv_value, "w_out": w_out, "ln2_gain": ln2_gain, "ln2_bias": ln2_bias, "w_up": w_up, "up_bias": up_bias, "w_down": w_down, "down_bias": down_bias}


@jax.custom_vjp
def low(v):
    return lax.optimization_barrier(v.astype(jnp.bfloat16)).astype(jnp.float32)

@jax.custom_vjp
def low_back(v):
    return v

def low_keep(v):
    return (low(v), None)

def low_pass(kept, grad):
    return (grad,)

def back_keep(v):
    return (v, None)

def back_low(kept, grad):
    return (low(grad),)
low.defvjp(low_keep, low_pass)
low_back.defvjp(back_keep, back_low)
epsilon = 1e-05
largest_score = lax.Precision.HIGHEST

def normed(values, scale_gain, offset):
    average = lax.optimization_barrier(jnp.mean(values, -1, keepdims=True))
    centred = values - average
    variance = lax.optimization_barrier(jnp.mean(centred * centred, -1, keepdims=True))
    return centred * lax.rsqrt(variance + epsilon) * scale_gain + offset

def product(operand, second):
    return jnp.dot(operand, second, precision=largest_score, preferred_element_type=jnp.float32)

def layer(tokens, weights):
    ln1_gain, ln1_bias, w_query, w_key, w_value, conv_key, conv_value, w_out, ln2_gain, ln2_bias, w_up, up_bias, w_down, down_bias = weights
    length, model_width = tokens.shape
    slot_total = length // 3
    score_scale = HEAD_DIM ** (-0.5)
    hidden = low(normed(tokens, ln1_gain, ln1_bias))
    queries = low(low_back(product(hidden, w_query)))
    token_keys = low(low_back(product(hidden, w_key)))
    token_values = low(low_back(product(hidden, w_value)))
    memory_keys = low(low_back(product(token_keys.reshape(slot_total, 3 * model_width), conv_key.reshape(3 * model_width, model_width))))
    memory_values = low(low_back(product(token_values.reshape(slot_total, 3 * model_width), conv_value.reshape(3 * model_width, model_width))))
    memory_key_triples = memory_keys.reshape(slot_total, HEADS, HEAD_DIM)
    memory_value_triples = memory_values.reshape(slot_total, HEADS, HEAD_DIM)
    slot_ends = 3 * jnp.arange(slot_total, dtype=jnp.int32) + 2

    def attend(pieces):
        query_block_rows, block_k, block_v, first_row = pieces
        positions = first_row + jnp.arange(TOK_DEV, dtype=jnp.int32)
        logit_scores = jnp.einsum('zbn,wbn->bzw', query_block_rows, memory_key_triples, precision=largest_score) * score_scale
        visible = (slot_ends[None, :] <= positions[:, None])[None]
        logit_scores = jnp.where(visible, logit_scores, -1e+30)
        own_scores = lax.optimization_barrier(jnp.sum(query_block_rows * block_k, -1)).T * score_scale
        combined = low_back(jnp.concatenate([logit_scores, own_scores[:, :, None]], -1))
        maxima = lax.optimization_barrier(jnp.max(combined, -1, keepdims=True))
        exponent = jnp.exp(combined - maxima)
        attention_weight = low(exponent / lax.optimization_barrier(jnp.sum(exponent, -1, keepdims=True)))
        blended_values = jnp.einsum('pxz,zpr->xpr', attention_weight[:, :, :-1], memory_value_triples, precision=largest_score)
        return blended_values + attention_weight[:, :, -1].T[:, :, None] * block_v
    blocks = length // TOK_DEV

    def split_rows(array):
        return array.reshape(blocks, TOK_DEV, HEADS, HEAD_DIM)
    starts = TOK_DEV * jnp.arange(blocks, dtype=jnp.int32)
    attended = lax.map(jax.checkpoint(attend), (split_rows(queries), split_rows(token_keys), split_rows(token_values), starts))
    attended = low(low_back(attended.reshape(length, model_width)))
    branch = low_back(product(attended, w_out))
    middle = tokens + branch
    hidden_two = low(normed(middle, ln2_gain, ln2_bias))
    upward = low_back(product(hidden_two, w_up) + up_bias)
    activated = low(jax.nn.gelu(upward, approximate=False))
    return middle + product(activated, w_down) + down_bias

def reference(inputs, cotangent, ln1_gain, ln1_bias, w_query, w_key, w_value, conv_key, conv_value, w_out, ln2_gain, ln2_bias, w_up, up_bias, w_down, down_bias):
    weights = tuple((item.astype(jnp.float32) for item in (ln1_gain, ln1_bias, w_query, w_key, w_value, conv_key, conv_value, w_out, ln2_gain, ln2_bias, w_up, up_bias, w_down, down_bias)))

    def one_sequence(running, pair):
        tokens, grad_output = pair
        result, pullback = jax.vjp(layer, tokens.astype(jnp.float32), weights)
        grad_tokens, grad_weights = pullback(grad_output.astype(jnp.float32))
        running = jax.tree.map(jnp.add, running, grad_weights)
        return (running, (result.astype(jnp.bfloat16), grad_tokens.astype(jnp.bfloat16)))
    initial = jax.tree.map(jnp.zeros_like, weights)
    totals, (outputs, grad_inputs) = lax.scan(one_sequence, initial, (inputs, cotangent))
    return (outputs, grad_inputs) + tuple(totals)
```

```python
import functools

import jax
import jax.numpy as jnp
import numpy as np
from jax import lax
from jax.experimental import pallas as pl
from jax.experimental.pallas import tpu as pltpu
from jax.sharding import PartitionSpec as P

HEADS = 8
HEAD_DIM = 64
PAIR = 2 * HEAD_DIM
TAPS = 3
TILE = 16

epsilon = 1e-05
narrow = jnp.bfloat16
single = jnp.float32
scale = HEAD_DIM ** (-0.5)

vmem = pl.BlockSpec(memory_space=pltpu.VMEM)
smem = pl.BlockSpec(memory_space=pltpu.SMEM)
params = pltpu.CompilerParams(vmem_limit_bytes=56 * 2**20)


def nn(a, b):
    return lax.dot_general(a, b, (((1,), (0,)), ((), ())), preferred_element_type=single)


def nt(a, b):
    return lax.dot_general(a, b, (((1,), (1,)), ((), ())), preferred_element_type=single)


def tn(a, b):
    return lax.dot_general(a, b, (((0,), (0,)), ((), ())), preferred_element_type=single)


def bit_masks(size):
    return [1 << b for b in range(size.bit_length() - 1)]


def seq_masks(size, core):
    masks = bit_masks(size)[1:]
    return masks if core == 0 else masks[::-1]


def seq_swap(size, stage):
    return [(i, i ^ seq_masks(size, i & 1)[stage]) for i in range(size)]


def gather_stages(seq_size):
    found = [("seq", seq_swap(seq_size, j)) for j in range(len(bit_masks(seq_size)) - 1)]
    return found + [("seq", [(i, i ^ 1) for i in range(seq_size)])]


def reduce_stages(seq_size, batch_size):
    found = [("seq", [(i, i ^ 1) for i in range(seq_size)])]
    found += [("seq", seq_swap(seq_size, j)) for j in range(len(bit_masks(seq_size)) - 1)]
    found += [("batch", [(i, i ^ m) for i in range(batch_size)]) for m in bit_masks(batch_size)]
    return found


def gather_origin(seq_size, me, block):
    count = len(bit_masks(seq_size)) - 1
    core_bit = (block >> count) & 1
    other = me ^ core_bit
    masks = seq_masks(seq_size, other & 1)
    for j in range(count):
        if (block >> j) & 1:
            other ^= masks[j]
    return other


def piece_of(seq_size, batch_size, split_bits, me_seq, me_batch, place):
    bits = [(place >> (split_bits - 1 - j)) & 1 for j in range(split_bits)]
    s = me_seq ^ bits[0]
    masks = seq_masks(seq_size, s & 1)
    z = me_batch
    for j, b in enumerate(bits[1:]):
        if j < len(masks):
            s ^= masks[j] * b
        else:
            z ^= (1 << (j - len(masks))) * b
    low_batch = z & ((1 << (split_bits - len(bit_masks(seq_size)))) - 1)
    return s + seq_size * low_batch


def plan_tables(seq_size, batch_size, split_bits):
    rows = []
    pieces = 1 << split_bits
    for s in range(seq_size):
        origins = [gather_origin(seq_size, s, k) for k in range(seq_size)]
        seen = [k for k in range(1, seq_size) if origins[k] < s]
        rest = [k for k in range(1, seq_size) if origins[k] > s]
        for z in range(batch_size):
            places = [piece_of(seq_size, batch_size, split_bits, s, z, k) for k in range(pieces)]
            inverse = [places.index(p) for p in range(pieces)]
            rows.append([len(seen)] + seen + rest + places + inverse)
    return np.asarray(rows, np.int32)


def reduce_scatter(buffer, stages, split_bits):
    for j, (axis, pairs) in enumerate(stages):
        if j < split_bits:
            half = (buffer.shape[0] - 1) // 2
            other = lax.ppermute(buffer[half:], axis, pairs)
            summed = [
                buffer[:half].astype(single) + other[:half].astype(single),
                buffer[2 * half :].astype(single) + other[half:].astype(single),
            ]
            buffer = jnp.concatenate(summed).astype(narrow)
        else:
            other = lax.ppermute(buffer, axis, pairs)
            buffer = (buffer.astype(single) + other.astype(single)).astype(narrow)
    return buffer


def gather(piece, stages):
    for axis, pairs in stages:
        piece = jnp.concatenate([piece, lax.ppermute(piece, axis, pairs)])
    return piece


def token_order(rows):
    slots = rows // TAPS
    r = lax.broadcasted_iota(jnp.int32, (rows, rows), 0)
    c = lax.broadcasted_iota(jnp.int32, (rows, rows), 1)
    return jnp.where(c == TAPS * (r % slots) + r // slots, 1.0, 0.0).astype(narrow)


def head_rows(width):
    r = lax.broadcasted_iota(jnp.int32, (HEADS, width), 0)
    c = lax.broadcasted_iota(jnp.int32, (HEADS, width), 1)
    return jnp.where(c // HEAD_DIM == r, 1.0, 0.0).astype(narrow)


def head_sums(values):
    marks = head_rows(values.shape[1])
    high = values.astype(narrow)
    rest = values - high.astype(single)
    middle = rest.astype(narrow)
    low = (rest - middle.astype(single)).astype(narrow)
    return nt(marks, high) + nt(marks, middle) + nt(marks, low)


def standardized(values):
    centred = values - jnp.mean(values, -1, keepdims=True)
    spread = lax.rsqrt(jnp.mean(centred * centred, -1, keepdims=True) + epsilon)
    return centred * spread, spread


def norm_back(grad, unit, spread, gain):
    inner = grad * gain
    return spread * (
        inner
        - jnp.mean(inner, -1, keepdims=True)
        - unit * jnp.mean(inner * unit, -1, keepdims=True)
    )


def front_kernel(x_ref, gain_ref, bias_ref, wk_ref, wv_ref, ck_ref, cv_ref, xp_ref, hid_ref, tk_ref, tv_ref, kv_ref):
    rows, width = x_ref.shape
    slots = rows // TAPS
    x = nn(token_order(rows), x_ref[...])
    xp_ref[...] = x.astype(narrow)
    unit, _ = standardized(x)
    hidden = (unit * gain_ref[...] + bias_ref[...]).astype(narrow)
    hid_ref[...] = hidden
    for w_ref, c_ref, t_ref, first in ((wk_ref, ck_ref, tk_ref, 0), (wv_ref, cv_ref, tv_ref, width)):
        t = nn(hidden, w_ref[...]).astype(narrow)
        t_ref[...] = t
        total = nn(t[:slots], c_ref[:width])
        for i in range(1, TAPS):
            total += nn(t[i * slots : (i + 1) * slots], c_ref[i * width : (i + 1) * width])
        kv_ref[:, first : first + width] = total.astype(narrow)


def query_kernel(hid_ref, wq_ref, g_ref, q_ref, gp_ref):
    q_ref[...] = nn(hid_ref[...], wq_ref[...]).astype(narrow)
    gp_ref[...] = nn(token_order(g_ref.shape[0]), g_ref[...]).astype(narrow)


def attend_kernel(tab_ref, q_ref, tk_ref, tv_ref, kv_ref, att_ref, lse_ref, own_ref, m_s, acc_s, qm_s):
    rows, width = q_ref.shape
    slots = kv_ref.shape[1]
    q = q_ref[...].astype(single)
    own = head_sums(q * tk_ref[...].astype(single)) * scale
    own_cols = own.T
    scaled = (q * scale).astype(narrow)
    lanes = lax.broadcasted_iota(jnp.int32, (rows, width), 1) % PAIR
    lane = lax.broadcasted_iota(jnp.int32, (1, PAIR), 1)
    nothing = jnp.zeros_like(scaled)
    qm_s[0] = jnp.where(lanes < HEAD_DIM, scaled, nothing)
    qm_s[1] = jnp.where(lanes >= HEAD_DIM, scaled, nothing)
    for h in range(HEADS):
        keep = (lane < HEAD_DIM) if h % 2 == 0 else (lane >= HEAD_DIM)
        m_s[h] = jnp.broadcast_to(own_cols[:, h : h + 1], (rows, PAIR))
        acc_s[h] = jnp.where(keep, tv_ref[:, PAIR * (h // 2) : PAIR * (h // 2 + 1)].astype(single), 1.0)

    def block(number, diagonal):
        for h in range(HEADS):
            cols = slice(PAIR * (h // 2), PAIR * (h // 2 + 1))
            keep = (lane < HEAD_DIM) if h % 2 == 0 else (lane >= HEAD_DIM)
            v = kv_ref[number, :, width + cols.start : width + cols.stop]
            v_ones = jnp.where(keep, v, jnp.ones_like(v))
            s = nt(qm_s[h % 2, :, cols], kv_ref[number, :, cols])
            if diagonal:
                slot = lax.broadcasted_iota(jnp.int32, s.shape, 1)
                row = lax.broadcasted_iota(jnp.int32, s.shape, 0)
                s = jnp.where(3 * slot + 2 <= 3 * (row % slots) + row // slots, s, -1e30)
            before = m_s[h]
            after = jnp.maximum(before, jnp.max(s, 1, keepdims=True))
            m_s[h] = after
            p = jnp.exp(s - jnp.concatenate([after] * (slots // PAIR), 1))
            acc_s[h] = acc_s[h] * jnp.exp(before - after) + nn(p.astype(narrow), v_ones)

    block(0, True)

    def step(i, carry):
        block(tab_ref[1 + i], False)
        return carry

    lax.fori_loop(0, tab_ref[0], step, 0)
    columns = []
    for p in range(HEADS // 2):
        first, second = acc_s[2 * p], acc_s[2 * p + 1]
        sums = pltpu.roll(jnp.where(lane < HEAD_DIM, second, first), HEAD_DIM, 1)
        att_ref[:, PAIR * p : PAIR * (p + 1)] = jnp.where(lane < HEAD_DIM, first, second) / sums
        columns.append(m_s[2 * p][:, :1] + jnp.log(first[:, HEAD_DIM : HEAD_DIM + 1]))
        columns.append(m_s[2 * p + 1][:, :1] + jnp.log(second[:, :1]))
    lse = jnp.concatenate(columns, 1).T
    lse_ref[...] = lse
    own_ref[...] = jnp.exp(own - lse)


def gelu_parts(u):
    bell = jnp.exp(-0.5 * (u * u))
    t = 1.0 / (1.0 + (0.3275911 * 0.5**0.5) * jnp.abs(u))
    series = t * (0.127414796 + t * (-0.142248368 + t * (0.7107068705 + t * (-0.7265760135 + t * 0.5307027145))))
    tail = series * bell
    below = jnp.where(u >= 0.0, 1.0 - tail, tail)
    return u * below, below + u * (bell * 0.3989422804014327)


def feed_kernel(
    tab_ref, x_ref, att_ref, g_ref, tv_ref, own_ref, wo_ref, gain_ref, bias_ref, wu_ref, ub_ref, wd_ref, db_ref,
    out_ref, gm_ref, ga_ref, delta_ref, ods_ref, buf_ref,
    mid_s, h_s, ht_s, out_s, gh_s, *, pieces, inverse_at,
):
    step = pl.program_id(0)
    rows, width = x_ref.shape
    hidden_rows = wd_ref.shape[0]
    steps = pl.num_programs(0)
    down_rows = hidden_rows * 4 // pieces
    down_tiles, up_tiles = down_rows // TILE, 4
    tiles = down_tiles + up_tiles + 1

    @pl.when(step == 0)
    def _():
        middle = x_ref[...].astype(single) + nn(att_ref[...].astype(narrow), wo_ref[...])
        mid_s[...] = middle
        unit, _ = standardized(middle)
        h = (unit * gain_ref[...] + bias_ref[...]).astype(narrow)
        h_s[...] = h
        ht_s[...] = h.T
        out_s[...] = middle + db_ref[...]
        gh_s[...] = jnp.zeros_like(gh_s)
        buf_ref[buf_ref.shape[0] - 1] = jnp.zeros((TILE, width), narrow)

    g = g_ref[...]
    act, slope = gelu_parts(nn(h_s[...], wu_ref[...]) + ub_ref[...])
    act = act.astype(narrow)
    out_s[...] += nn(act, wd_ref[...])
    gu = (nt(g, wd_ref[...]) * slope).astype(narrow)
    gh_s[...] += nt(gu, wu_ref[...])
    grad_down = tn(act, g).astype(narrow)
    here = hidden_rows // down_rows
    for j in range(here):
        at = tab_ref[inverse_at + step * here + j] * tiles
        for t in range(down_tiles):
            first = j * down_rows + t * TILE
            buf_ref[at + t] = grad_down[first : first + TILE]
    grad_up = nn(ht_s[...], gu).astype(narrow)
    for j in range(pieces):
        at = tab_ref[inverse_at + j] * tiles + down_tiles
        buf_ref[at + step] = grad_up[j * TILE : (j + 1) * TILE]
    small = buf_ref.shape[0] - 1
    up_bias = jnp.sum(gu.astype(single), 0, keepdims=True)
    place = lax.broadcasted_iota(jnp.int32, (TILE, width), 0)
    buf_ref[small] = jnp.where(place == 1 + step, up_bias, buf_ref[small].astype(single)).astype(narrow)

    @pl.when(step == steps - 1)
    def _():
        out_ref[...] = tn(token_order(rows), out_s[...].astype(narrow)).astype(narrow)
        unit, spread = standardized(mid_s[...])
        gh = gh_s[...]
        wide_g = g.astype(single)
        gm = wide_g + norm_back(gh, unit, spread, gain_ref[...])
        gm_ref[...] = gm
        branch = gm.astype(narrow)
        att = att_ref[...]
        grad_out = tn(att.astype(narrow), branch).astype(narrow)
        for j in range(pieces):
            at = tab_ref[inverse_at + j] * tiles + down_tiles + up_tiles
            buf_ref[at] = grad_out[j * TILE : (j + 1) * TILE]
        sums = buf_ref[small].astype(single)
        for row, value in ((0, wide_g), (5, gh * unit), (6, gh)):
            sums = jnp.where(place == row, jnp.sum(value, 0, keepdims=True), sums)
        buf_ref[small] = sums.astype(narrow)
        ga = nt(branch, wo_ref[...]).astype(narrow)
        ga_ref[...] = ga
        wide = ga.astype(single)
        delta = head_sums(wide * att)
        delta_ref[...] = delta
        dprob = head_sums(wide * tv_ref[...].astype(single))
        ods_ref[...] = (own_ref[...] * (dprob - delta)).astype(narrow)


def attend_back_kernel(tab_ref, q_ref, do_ref, kv_ref, lse_ref, delta_ref, dq_ref, dkv_ref, qm_s, dm_s):
    rows, width = q_ref.shape
    blocks, slots, _ = kv_ref.shape
    scaled = (q_ref[...].astype(single) * scale).astype(narrow)
    do = do_ref[...]
    lanes = lax.broadcasted_iota(jnp.int32, (rows, width), 1) % PAIR
    lane = lax.broadcasted_iota(jnp.int32, (1, PAIR), 1)
    nothing = jnp.zeros_like(scaled)
    qm_s[0] = jnp.where(lanes < HEAD_DIM, scaled, nothing)
    qm_s[1] = jnp.where(lanes >= HEAD_DIM, scaled, nothing)
    dm_s[0] = jnp.where(lanes < HEAD_DIM, do, nothing)
    dm_s[1] = jnp.where(lanes >= HEAD_DIM, do, nothing)

    def block(number, diagonal):
        for p in range(HEADS // 2):
            cols = slice(PAIR * p, PAIR * (p + 1))
            value_cols = slice(width + PAIR * p, width + PAIR * (p + 1))
            k = kv_ref[number, :, cols]
            v = kv_ref[number, :, value_cols]
            dk = dv = 0.0
            for half in range(2):
                h = 2 * p + half
                keep = (lane < HEAD_DIM) if half == 0 else (lane >= HEAD_DIM)
                qm = qm_s[half, :, cols]
                dm = dm_s[half, :, cols]
                s = nt(k, qm)
                prob = jnp.exp(s - lse_ref[h : h + 1, :])
                if diagonal:
                    slot = lax.broadcasted_iota(jnp.int32, s.shape, 0)
                    row = lax.broadcasted_iota(jnp.int32, s.shape, 1)
                    prob = jnp.where(3 * slot + 2 <= 3 * (row % slots) + row // slots, prob, 0.0)
                ds = (prob * (nt(v, dm) - delta_ref[h : h + 1, :])).astype(narrow)
                dk += nn(ds, qm)
                dv += nn(prob.astype(narrow), dm)
                dq = tn(ds, jnp.where(keep, k, jnp.zeros_like(k)))
                if diagonal and half == 0:
                    dq_ref[:, cols] = dq
                else:
                    dq_ref[:, cols] += dq
            dkv_ref[number, :, cols] = dk.astype(narrow)
            dkv_ref[number, :, value_cols] = dv.astype(narrow)

    block(0, True)

    def step(i, carry):
        block(tab_ref[1 + i], False)
        return carry

    def clear(i, carry):
        dkv_ref[tab_ref[1 + i]] = jnp.zeros((slots, 2 * width), narrow)
        return carry

    lax.fori_loop(0, tab_ref[0], step, 0)
    lax.fori_loop(tab_ref[0], blocks - 1, clear, 0)


def tail_kernel(
    tab_ref, x_ref, hid_ref, q_ref, tk_ref, tv_ref, ga_ref, gm_ref, own_ref, ods_ref, dq_ref, gkv_ref,
    wq_ref, wk_ref, wv_ref, ck_ref, cv_ref, gain_ref,
    gx_ref, buf_ref, *, pieces, inverse_at,
):
    rows, width = x_ref.shape
    slots = rows // TAPS
    conv_rows = TAPS * width // pieces
    conv_tiles = conv_rows // TILE
    tiles = 2 * conv_tiles + TAPS
    gk, gv = gkv_ref[:, :width], gkv_ref[:, width:]
    for number, (t_ref, grad) in enumerate(((tk_ref, gk), (tv_ref, gv))):
        for i in range(TAPS):
            conv = tn(t_ref[i * slots : (i + 1) * slots], grad).astype(narrow)
            for j in range(width // TILE):
                tile = i * (width // TILE) + j
                at = tab_ref[inverse_at + tile // conv_tiles] * tiles + number * conv_tiles + tile % conv_tiles
                buf_ref[at] = conv[j * TILE : (j + 1) * TILE]
    marks = head_rows(width)
    own_ds = tn(ods_ref[...], marks) * scale
    own_prob = tn(own_ref[...].astype(narrow), marks)
    gq = (dq_ref[...] * scale + own_ds * tk_ref[...].astype(single)).astype(narrow)
    conv_k = jnp.concatenate([nt(gk, ck_ref[i * width : (i + 1) * width]) for i in range(TAPS)], 0)
    conv_v = jnp.concatenate([nt(gv, cv_ref[i * width : (i + 1) * width]) for i in range(TAPS)], 0)
    gk = (conv_k + own_ds * q_ref[...].astype(single)).astype(narrow)
    gv = (conv_v + own_prob * ga_ref[...].astype(single)).astype(narrow)
    hidden_t = hid_ref[...].T
    grad_hidden = 0.0
    for number, (grad, w_ref) in enumerate(((gq, wq_ref), (gk, wk_ref), (gv, wv_ref))):
        grad_w = nn(hidden_t, grad).astype(narrow)
        for j in range(pieces):
            buf_ref[tab_ref[inverse_at + j] * tiles + 2 * conv_tiles + number] = grad_w[j * TILE : (j + 1) * TILE]
        grad_hidden += nt(grad, w_ref[...])
    unit, spread = standardized(x_ref[...].astype(single))
    place = lax.broadcasted_iota(jnp.int32, (TILE, width), 0)
    sums = jnp.where(place == 0, jnp.sum(grad_hidden * unit, 0, keepdims=True), 0.0)
    sums = jnp.where(place == 1, jnp.sum(grad_hidden, 0, keepdims=True), sums)
    buf_ref[buf_ref.shape[0] - 1] = sums.astype(narrow)
    gx = gm_ref[...] + norm_back(grad_hidden, unit, spread, gain_ref[...])
    gx_ref[...] = tn(token_order(rows), gx.astype(narrow)).astype(narrow)


def unpack_feed_kernel(tab_ref, buf_ref, wd_ref, wu_ref, wo_ref, *, pieces, piece_at):
    width = wd_ref.shape[1]
    down_rows = wd_ref.shape[0] // pieces
    down_tiles, up_tiles = down_rows // TILE, wu_ref.shape[1] // width
    tiles = down_tiles + up_tiles + 1

    def step(k, carry):
        piece = tab_ref[piece_at + k]
        at = k * tiles
        for t in range(down_tiles):
            wd_ref[pl.ds(pl.multiple_of(piece * down_rows + t * TILE, TILE), TILE), :] = buf_ref[at + t].astype(single)
        mine = pl.ds(pl.multiple_of(piece * TILE, TILE), TILE)
        for t in range(up_tiles):
            wu_ref[mine, t * width : (t + 1) * width] = buf_ref[at + down_tiles + t].astype(single)
        wo_ref[mine, :] = buf_ref[at + down_tiles + up_tiles].astype(single)
        return carry

    lax.fori_loop(0, pieces, step, 0, unroll=4)


def unpack_tail_kernel(tab_ref, buf_ref, ck_ref, cv_ref, wq_ref, wk_ref, wv_ref, *, pieces, piece_at):
    conv_rows = ck_ref.shape[0] // pieces
    conv_tiles = conv_rows // TILE
    tiles = 2 * conv_tiles + TAPS

    def step(k, carry):
        piece = tab_ref[piece_at + k]
        at = k * tiles
        for number, c_ref in enumerate((ck_ref, cv_ref)):
            for t in range(conv_tiles):
                rows = pl.ds(pl.multiple_of(piece * conv_rows + t * TILE, TILE), TILE)
                c_ref[rows, :] = buf_ref[at + number * conv_tiles + t].astype(single)
        mine = pl.ds(pl.multiple_of(piece * TILE, TILE), TILE)
        for number, w_ref in enumerate((wq_ref, wk_ref, wv_ref)):
            w_ref[mine, :] = buf_ref[at + 2 * conv_tiles + number].astype(single)
        return carry

    lax.fori_loop(0, pieces, step, 0, unroll=4)


def shaped(shape, kind):
    return jax.ShapeDtypeStruct(shape, kind)


def per_device(
    seq_size, batch_size,
    inputs, cotangent, ln1_gain, ln1_bias, w_query, w_key, w_value, conv_key, conv_value, w_out,
    ln2_gain, ln2_bias, w_up, up_bias, w_down, down_bias,
):
    x, g = inputs[0], cotangent[0]
    rows, width = x.shape
    slots = rows // TAPS
    ff = w_up.shape[1]
    seq_bits, batch_bits = seq_size.bit_length() - 1, batch_size.bit_length() - 1
    split_bits = min(5, seq_bits + batch_bits)
    pieces = 1 << split_bits
    piece_at, inverse_at = seq_size, seq_size + pieces
    tables = jnp.asarray(plan_tables(seq_size, batch_size, split_bits))
    table = lax.dynamic_index_in_dim(
        tables, lax.axis_index("seq") * batch_size + lax.axis_index("batch"), 0, keepdims=False
    )
    row = lambda v: v.reshape(1, -1)
    ck = conv_key.reshape(TAPS * width, width)
    cv = conv_value.reshape(TAPS * width, width)

    xp, hidden, tk, tv, kv = pl.pallas_call(
        front_kernel,
        out_shape=(
            shaped((rows, width), narrow),
            shaped((rows, width), narrow),
            shaped((rows, width), narrow),
            shaped((rows, width), narrow),
            shaped((slots, 2 * width), narrow),
        ),
        in_specs=[vmem] * 7,
        out_specs=(vmem,) * 5,
        compiler_params=params,
        name="front",
    )(x, row(ln1_gain), row(ln1_bias), w_key, w_value, ck, cv)

    all_kv = gather(kv, gather_stages(seq_size)).reshape(seq_size, slots, 2 * width)

    q, gp = pl.pallas_call(
        query_kernel,
        out_shape=(shaped((rows, width), narrow), shaped((rows, width), narrow)),
        in_specs=[vmem] * 3,
        out_specs=(vmem,) * 2,
        compiler_params=params,
        name="query",
    )(hidden, w_query, g)

    attended, lse, own_prob = pl.pallas_call(
        attend_kernel,
        out_shape=(shaped((rows, width), single), shaped((HEADS, rows), single), shaped((HEADS, rows), single)),
        in_specs=[smem] + [vmem] * 4,
        out_specs=(vmem,) * 3,
        scratch_shapes=[
            pltpu.VMEM((HEADS, rows, PAIR), single),
            pltpu.VMEM((HEADS, rows, PAIR), single),
            pltpu.VMEM((2, rows, width), narrow),
        ],
        compiler_params=params,
        name="attend",
    )(table, q, tk, tv, all_kv)

    steps = ff // width
    tiles = ff // pieces // TILE + steps + 1
    whole = lambda *shape: pl.BlockSpec(shape, lambda i: (0,) * len(shape))
    output, grad_middle, grad_attended, delta, own_ds, buffer = pl.pallas_call(
        functools.partial(feed_kernel, pieces=pieces, inverse_at=inverse_at),
        grid=(steps,),
        out_shape=(
            shaped((rows, width), narrow),
            shaped((rows, width), single),
            shaped((rows, width), narrow),
            shaped((HEADS, rows), single),
            shaped((HEADS, rows), narrow),
            shaped((pieces * tiles + 1, TILE, width), narrow),
        ),
        in_specs=[
            smem,
            whole(rows, width),
            whole(rows, width),
            whole(rows, width),
            whole(rows, width),
            whole(HEADS, rows),
            whole(width, width),
            whole(1, width),
            whole(1, width),
            pl.BlockSpec((width, width), lambda i: (0, i)),
            pl.BlockSpec((1, width), lambda i: (0, i)),
            pl.BlockSpec((width, width), lambda i: (i, 0)),
            whole(1, width),
        ],
        out_specs=(
            whole(rows, width),
            whole(rows, width),
            whole(rows, width),
            whole(HEADS, rows),
            whole(HEADS, rows),
            whole(pieces * tiles + 1, TILE, width),
        ),
        scratch_shapes=[
            pltpu.VMEM((rows, width), single),
            pltpu.VMEM((rows, width), narrow),
            pltpu.VMEM((width, rows), narrow),
            pltpu.VMEM((rows, width), single),
            pltpu.VMEM((rows, width), single),
        ],
        compiler_params=params,
        name="feed",
    )(table, xp, attended, gp, tv, own_prob, w_out, row(ln2_gain), row(ln2_bias), w_up, row(up_bias), w_down, row(down_bias))

    stages = reduce_stages(seq_size, batch_size)
    gather_back = stages[:split_bits][::-1]
    reduced = reduce_scatter(buffer, stages, split_bits)
    small_feed = reduced[-1].astype(single)
    full = gather(reduced[:-1], gather_back)
    grad_w_down, grad_w_up, grad_w_out = pl.pallas_call(
        functools.partial(unpack_feed_kernel, pieces=pieces, piece_at=piece_at),
        out_shape=(shaped((ff, width), single), shaped((width, ff), single), shaped((width, width), single)),
        in_specs=[smem, vmem],
        out_specs=(vmem,) * 3,
        compiler_params=params,
        name="unpack_feed",
    )(table, full)

    grad_q, grad_kv = pl.pallas_call(
        attend_back_kernel,
        out_shape=(shaped((rows, width), single), shaped((seq_size, slots, 2 * width), narrow)),
        in_specs=[smem] + [vmem] * 5,
        out_specs=(vmem,) * 2,
        scratch_shapes=[pltpu.VMEM((2, rows, width), narrow), pltpu.VMEM((2, rows, width), narrow)],
        compiler_params=params,
        name="attend_back",
    )(table, q, grad_attended, all_kv, lse, delta)

    for axis, pairs in gather_stages(seq_size)[::-1]:
        half = grad_kv.shape[0] // 2
        other = lax.ppermute(grad_kv[half:], axis, pairs)
        grad_kv = (grad_kv[:half].astype(single) + other.astype(single)).astype(narrow)
    grad_kv = grad_kv[0]

    tail_tiles = 2 * (TAPS * width // pieces // TILE) + TAPS
    grad_x, buffer = pl.pallas_call(
        functools.partial(tail_kernel, pieces=pieces, inverse_at=inverse_at),
        out_shape=(shaped((rows, width), narrow), shaped((pieces * tail_tiles + 1, TILE, width), narrow)),
        in_specs=[smem] + [vmem] * 17,
        out_specs=(vmem,) * 2,
        compiler_params=params,
        name="tail",
    )(
        table, xp, hidden, q, tk, tv, grad_attended, grad_middle, own_prob, own_ds, grad_q, grad_kv,
        w_query, w_key, w_value, ck, cv, row(ln1_gain),
    )
    reduced = reduce_scatter(buffer, stages, split_bits)
    small_tail = reduced[-1].astype(single)
    full = gather(reduced[:-1], gather_back)
    grad_ck, grad_cv, grad_wq, grad_wk, grad_wv = pl.pallas_call(
        functools.partial(unpack_tail_kernel, pieces=pieces, piece_at=piece_at),
        out_shape=(shaped((TAPS * width, width), single),) * 2 + (shaped((width, width), single),) * 3,
        in_specs=[smem, vmem],
        out_specs=(vmem,) * 5,
        compiler_params=params,
        name="unpack_tail",
    )(table, full)

    return (
        output[None],
        grad_x[None],
        small_tail[0],
        small_tail[1],
        grad_wq,
        grad_wk,
        grad_wv,
        grad_ck.reshape(conv_key.shape),
        grad_cv.reshape(conv_value.shape),
        grad_w_out,
        small_feed[5],
        small_feed[6],
        grad_w_up,
        small_feed[1 : 1 + steps].reshape(ff),
        grad_w_down,
        small_feed[0],
    )


def solution(mesh):
    placed = (P("batch", "seq", None),) * 2 + (P(),) * 14
    return jax.shard_map(
        functools.partial(per_device, mesh.shape["seq"], mesh.shape["batch"]),
        mesh=mesh,
        in_specs=placed,
        out_specs=placed,
        check_vma=False,
    )
```

```python
import functools

import jax
import jax.numpy as jnp
import numpy as np
from jax import lax
from jax.experimental import pallas as pl
from jax.experimental.pallas import tpu as pltpu
from jax.sharding import PartitionSpec as P

HEADS = 8
HEAD_DIM = 64
PAIR = 2 * HEAD_DIM
TAPS = 3
TILE = 16

epsilon = 1e-05
narrow = jnp.bfloat16
single = jnp.float32
scale = HEAD_DIM ** (-0.5)

vmem = pl.BlockSpec(memory_space=pltpu.VMEM)
smem = pl.BlockSpec(memory_space=pltpu.SMEM)
anywhere = pl.BlockSpec(memory_space=pl.ANY)
hbm = pl.BlockSpec(memory_space=pltpu.HBM)


def params(mib):
    return pltpu.CompilerParams(vmem_limit_bytes=mib * 2**20)


def cost(flops, moved):
    return pl.CostEstimate(flops=int(flops), bytes_accessed=int(moved), transcendentals=0)


class Loads:
    def __init__(self, sources, held, sems):
        self.held, self.waited = held, set()
        self.copies = [pltpu.make_async_copy(a, b, sems.at[i]) for i, (a, b) in enumerate(zip(sources, held))]
        for copy in self.copies:
            copy.start()

    def __getitem__(self, i):
        if i not in self.waited:
            self.copies[i].wait()
            self.waited.add(i)
        return self.held[i]


def call(
    name, body, outs, *, loads=(), table=None, operands=(), away=(), away_outs=0, in_place=0, scratch=(), mib, flops
):
    count = len(loads)
    inputs = count + (table is not None) + len(operands) + len(away)

    def kernel(*refs):
        sources, rest = refs[:count], refs[count:]
        if count == 0:
            return body(*rest)
        held, sems = rest[-count - 1 : -1], rest[-1]
        return body(Loads(sources, held, sems), *rest[: -count - 1])

    moved = sum(v.size * 2 for v in (*loads, *operands, *away, *outs))
    scratch = list(scratch)
    if count:
        scratch += [pltpu.VMEM(v.shape, v.dtype) for v in loads] + [pltpu.SemaphoreType.DMA((count,))]
    return pl.pallas_call(
        kernel,
        out_shape=tuple(outs),
        in_specs=[hbm] * count + [smem] * (table is not None) + [vmem] * len(operands) + [anywhere] * len(away),
        out_specs=(vmem,) * (len(outs) - away_outs) + (anywhere,) * away_outs,
        scratch_shapes=scratch,
        input_output_aliases={inputs - in_place + i: len(outs) - in_place + i for i in range(in_place)},
        compiler_params=params(mib),
        cost_estimate=cost(flops, moved),
        name=name,
    )(
        *[pltpu.with_memory_space_constraint(v, pltpu.HBM) for v in loads],
        *([] if table is None else [table]),
        *operands,
        *away,
    )


def tied(values, *others):
    return lax.optimization_barrier((values, others))[0]


def nn(a, b):
    return lax.dot_general(a, b, (((1,), (0,)), ((), ())), preferred_element_type=single)


def nt(a, b):
    return lax.dot_general(a, b, (((1,), (1,)), ((), ())), preferred_element_type=single)


def tn(a, b):
    return lax.dot_general(a, b, (((0,), (0,)), ((), ())), preferred_element_type=single)


def bit_masks(size):
    return [1 << b for b in range(size.bit_length() - 1)]


def seq_masks(size, core):
    masks = bit_masks(size)[1:]
    return masks if core == 0 else masks[::-1]


def seq_swap(size, stage):
    return [(i, i ^ seq_masks(size, i & 1)[stage]) for i in range(size)]


def gather_stages(seq_size):
    found = [("seq", seq_swap(seq_size, j)) for j in range(len(bit_masks(seq_size)) - 1)]
    return found + [("seq", [(i, i ^ 1) for i in range(seq_size)])]


def reduce_stages(seq_size, batch_size):
    found = [("seq", [(i, i ^ 1) for i in range(seq_size)])]
    found += [("seq", seq_swap(seq_size, j)) for j in range(len(bit_masks(seq_size)) - 1)]
    found += [("batch", [(i, i ^ m) for i in range(batch_size)]) for m in bit_masks(batch_size)]
    return found


def gather_origin(seq_size, me, block):
    count = len(bit_masks(seq_size)) - 1
    core_bit = (block >> count) & 1
    other = me ^ core_bit
    masks = seq_masks(seq_size, other & 1)
    for j in range(count):
        if (block >> j) & 1:
            other ^= masks[j]
    return other


def piece_of(seq_size, batch_size, split_bits, me_seq, me_batch, place):
    bits = [(place >> (split_bits - 1 - j)) & 1 for j in range(split_bits)]
    s = me_seq ^ bits[0]
    masks = seq_masks(seq_size, s & 1)
    z = me_batch
    for j, b in enumerate(bits[1:]):
        if j < len(masks):
            s ^= masks[j] * b
        else:
            z ^= (1 << (j - len(masks))) * b
    low_batch = z & ((1 << (split_bits - len(bit_masks(seq_size)))) - 1)
    return s + seq_size * low_batch


def gather_plan(seq_size):
    stages = gather_stages(seq_size)
    count = len(stages) - 1
    rounds = [[] for _ in range(count + 1)]
    for block in range(1, 1 << count):
        last = block.bit_length() - 1
        rounds[bin(block).count("1")].append((block, block ^ (1 << last), stages[last]))
    for found in rounds:
        blocks = [entry[0] for entry in found] or [0]
        found += [(block | (1 << count), block, stages[-1]) for block in blocks]
    return rounds


def plan_tables(seq_size, batch_size, split_bits):
    rows = []
    pieces = 1 << split_bits
    for s in range(seq_size):
        origins = [gather_origin(seq_size, s, k) for k in range(seq_size)]
        seen = [int(origin < s) for origin in origins]
        lists = []
        for first, stop in ((0, seq_size // 2), (seq_size // 2, seq_size)):
            visible = [k for k in range(first, stop) if origins[k] < s]
            lists += [len(visible)] + visible + [k for k in range(first, stop) if origins[k] > s]
        for z in range(batch_size):
            places = [piece_of(seq_size, batch_size, split_bits, s, z, k) for k in range(pieces)]
            inverse = [places.index(p) for p in range(pieces)]
            rows.append(seen + lists + places + inverse)
    return np.asarray(rows, np.int32)


def step_order(first, second, feed):
    order = ["first", "first"]
    order += [name for _ in range(max(first - 2, second)) for name in ("second", "first")]
    found, taken = [], {"first": 0, "second": 0, "feed": 0}
    limits = {"first": first, "second": second, "feed": feed}
    for name in order:
        if taken[name] == limits[name]:
            continue
        taken[name] += 1
        found.append(name)
        if name == "second" and taken["second"] >= 3 and taken["second"] % 2 == 1 and taken["feed"] < feed:
            taken["feed"] += 1
            found.append("feed")
    found += ["feed"] * (feed - taken["feed"])
    after = max(i for i, name in enumerate(found) if name == "feed") + 3 if feed else 0
    found = found[:after] + ["feed"] + found[after:]
    last = max(i for i, name in enumerate(found) if name == "second")
    return found[:last] + found[last + 1 :] + ["first", "second"]


def token_order(rows):
    slots = rows // TAPS
    r = lax.broadcasted_iota(jnp.int32, (rows, rows), 0)
    c = lax.broadcasted_iota(jnp.int32, (rows, rows), 1)
    return jnp.where(c == TAPS * (r % slots) + r // slots, 1.0, 0.0).astype(narrow)


def head_rows(width):
    r = lax.broadcasted_iota(jnp.int32, (HEADS, width), 0)
    c = lax.broadcasted_iota(jnp.int32, (HEADS, width), 1)
    return jnp.where(c // HEAD_DIM == r, 1.0, 0.0).astype(narrow)


def head_sums(values):
    marks = head_rows(values.shape[1])
    high = values.astype(narrow)
    rest = values - high.astype(single)
    middle = rest.astype(narrow)
    low = (rest - middle.astype(single)).astype(narrow)
    return nt(marks, high) + nt(marks, middle) + nt(marks, low)


def standardized(values):
    centred = values - jnp.mean(values, -1, keepdims=True)
    spread = lax.rsqrt(jnp.mean(centred * centred, -1, keepdims=True) + epsilon)
    return centred * spread, spread


def norm_back(grad, unit, spread, gain):
    inner = grad * gain
    return spread * (
        inner
        - jnp.mean(inner, -1, keepdims=True)
        - unit * jnp.mean(inner * unit, -1, keepdims=True)
    )


def front_kernel(loads, xp_ref, hid_ref, tk_ref, tv_ref, kv_ref):
    rows, width = xp_ref.shape
    slots = rows // TAPS
    order = token_order(rows)
    x = nn(order, loads[0][...])
    xp_ref[...] = x.astype(narrow)
    unit, _ = standardized(x)
    hidden = (unit * loads[1][...] + loads[2][...]).astype(narrow)
    hid_ref[...] = hidden
    for number, t_ref in enumerate((tk_ref, tv_ref)):
        t = nn(hidden, loads[3 + 2 * number][...]).astype(narrow)
        t_ref[...] = t
        c_ref = loads[4 + 2 * number]
        total = nn(t[:slots], c_ref[:width])
        for i in range(1, TAPS):
            total += nn(t[i * slots : (i + 1) * slots], c_ref[i * width : (i + 1) * width])
        kv_ref[:, number * width : (number + 1) * width] = total.astype(narrow)


def attend_block(kv_ref, number, qm_ref, m_ref, acc_ref, diagonal):
    slots, width = kv_ref.shape[1], qm_ref.shape[2]
    lane = lax.broadcasted_iota(jnp.int32, (1, PAIR), 1)
    for h in range(HEADS):
        cols = slice(PAIR * (h // 2), PAIR * (h // 2 + 1))
        keep = (lane < HEAD_DIM) if h % 2 == 0 else (lane >= HEAD_DIM)
        v = kv_ref[number, :, width + cols.start : width + cols.stop]
        v_ones = jnp.where(keep, v, jnp.ones_like(v))
        s = nt(qm_ref[h % 2, :, cols], kv_ref[number, :, cols])
        if diagonal:
            slot = lax.broadcasted_iota(jnp.int32, s.shape, 1)
            row = lax.broadcasted_iota(jnp.int32, s.shape, 0)
            s = jnp.where(3 * slot + 2 <= 3 * (row % slots) + row // slots, s, -1e30)
        before = m_ref[h]
        after = jnp.maximum(before, jnp.max(s, 1, keepdims=True))
        m_ref[h] = after
        p = jnp.exp(s - jnp.concatenate([after] * (slots // PAIR), 1))
        acc_ref[h] = acc_ref[h] * jnp.exp(before - after) + nn(p.astype(narrow), v_ones)


def split_heads(values, out_ref):
    lanes = lax.broadcasted_iota(jnp.int32, (1, values.shape[1]), 1) % PAIR
    nothing = jnp.zeros_like(values)
    out_ref[0] = jnp.where(lanes < HEAD_DIM, values, nothing)
    out_ref[1] = jnp.where(lanes >= HEAD_DIM, values, nothing)


def attend_own_kernel(loads, hid_ref, tk_ref, tv_ref, kv_ref, q_ref, gp_ref, qm_ref, own_ref, m_ref, acc_ref):
    rows, width = hid_ref.shape
    q_low = nn(hid_ref[...], loads[0][...]).astype(narrow)
    q_ref[...] = q_low
    q = q_low.astype(single)
    split_heads((q * scale).astype(narrow), qm_ref)
    own = head_sums(q * tk_ref[...].astype(single)) * scale
    own_ref[...] = own
    own_cols = own.T
    lane = lax.broadcasted_iota(jnp.int32, (1, PAIR), 1)
    for h in range(HEADS):
        keep = (lane < HEAD_DIM) if h % 2 == 0 else (lane >= HEAD_DIM)
        m_ref[h] = jnp.broadcast_to(own_cols[:, h : h + 1], (rows, PAIR))
        acc_ref[h] = jnp.where(keep, tv_ref[:, PAIR * (h // 2) : PAIR * (h // 2 + 1)].astype(single), 1.0)
    attend_block(kv_ref, 0, qm_ref, m_ref, acc_ref, True)
    gp_ref[...] = nn(token_order(rows), loads[1][...]).astype(narrow)


def attend_seen(tab_ref, blocks, kv_refs, qm_ref, m_ref, acc_ref):
    for block, kv_ref in zip(blocks, kv_refs):

        @pl.when(tab_ref[block] == 1)
        def _(kv_ref=kv_ref):
            attend_block(kv_ref, 0, qm_ref, m_ref, acc_ref, False)


def attend_more_kernel(tab_ref, qm_ref, m_in, acc_in, *rest, blocks):
    kv_refs, (m_ref, acc_ref) = rest[:-2], rest[-2:]
    m_ref[...] = m_in[...]
    acc_ref[...] = acc_in[...]
    attend_seen(tab_ref, blocks, kv_refs, qm_ref, m_ref, acc_ref)


def attend_last_kernel(tab_ref, qm_ref, own_ref, m_in, acc_in, *rest, blocks):
    kv_refs, (att_ref, lse_ref, prob_ref, m_ref, acc_ref) = rest[:-5], rest[-5:]
    m_ref[...] = m_in[...]
    acc_ref[...] = acc_in[...]
    attend_seen(tab_ref, blocks, kv_refs, qm_ref, m_ref, acc_ref)
    lane = lax.broadcasted_iota(jnp.int32, (1, PAIR), 1)
    columns = []
    for p in range(HEADS // 2):
        first, second = acc_ref[2 * p], acc_ref[2 * p + 1]
        sums = pltpu.roll(jnp.where(lane < HEAD_DIM, second, first), HEAD_DIM, 1)
        att_ref[:, PAIR * p : PAIR * (p + 1)] = jnp.where(lane < HEAD_DIM, first, second) / sums
        columns.append(m_ref[2 * p][:, :1] + jnp.log(first[:, HEAD_DIM : HEAD_DIM + 1]))
        columns.append(m_ref[2 * p + 1][:, :1] + jnp.log(second[:, :1]))
    lse = jnp.concatenate(columns, 1).T
    lse_ref[...] = lse
    prob_ref[...] = jnp.exp(own_ref[...] - lse)


def gelu_parts(u):
    bell = jnp.exp(-0.5 * (u * u))
    t = 1.0 / (1.0 + (0.3275911 * 0.5**0.5) * jnp.abs(u))
    series = t * (0.127414796 + t * (-0.142248368 + t * (0.7107068705 + t * (-0.7265760135 + t * 0.5307027145))))
    tail = series * bell
    below = jnp.where(u >= 0.0, 1.0 - tail, tail)
    return u * below, below + u * (bell * 0.3989422804014327)


def feed_kernel(loads, tab_ref, x_ref, att_ref, g_ref, wo_ref, *rest, pieces, inverse_at):
    kv_refs = rest[:-11]
    out_ref, mid_ref, gh_ref, keep_ref, send_ref, kv_all, h_s, ht_s, out_s, buf_ref, sems = rest[-11:]
    copies = [
        pltpu.make_async_copy(kv_ref, kv_all.at[pl.ds(i, 1)], sems.at[3 + i]) for i, kv_ref in enumerate(kv_refs)
    ]
    for copy in copies:
        copy.start()
    rows, width = x_ref.shape
    hidden_rows = loads.held[4].shape[0]
    steps = hidden_rows // width
    down_rows = hidden_rows // pieces
    down_tiles = down_rows // TILE
    tiles = down_tiles + steps
    middle = x_ref[...].astype(single) + nn(att_ref[...].astype(narrow), wo_ref[...])
    mid_ref[...] = middle
    unit, _ = standardized(middle)
    h = (unit * loads[0][...] + loads[1][...]).astype(narrow)
    h_s[...] = h
    ht_s[...] = h.T
    g = g_ref[...]
    wu_ref, ub_ref, wd_ref, db_ref = (loads[i] for i in range(2, 6))
    small = buf_ref.shape[0] - 1
    place = lax.broadcasted_iota(jnp.int32, (TILE, width), 0)
    here = pieces // steps
    out_s[...] = middle + db_ref[...]
    gh_ref[...] = jnp.zeros_like(middle)

    def step(i, sums):
        cols = pl.ds(pl.multiple_of(i * width, width), width)
        act, slope = gelu_parts(nn(h_s[...], wu_ref[:, cols]) + ub_ref[:, cols])
        act = act.astype(narrow)
        out_s[...] += nn(act, wd_ref[cols, :])
        gu = (nt(g_ref[...], wd_ref[cols, :]) * slope).astype(narrow)
        gh_ref[...] += nt(gu, wu_ref[:, cols])
        grad_down = tn(act, g_ref[...]).astype(narrow)
        for j in range(here):
            at = tab_ref[inverse_at + i * here + j] * tiles
            store_tiles(buf_ref, at, grad_down[j * down_rows : (j + 1) * down_rows])
        grad_up = nn(ht_s[...], gu).astype(narrow)
        for j in range(pieces):
            buf_ref[tab_ref[inverse_at + j] * tiles + down_tiles + i] = grad_up[j * TILE : (j + 1) * TILE]
        return jnp.where(place == 1 + i, jnp.sum(gu.astype(single), 0, keepdims=True), sums)

    sums = lax.fori_loop(0, steps, step, jnp.zeros((TILE, width), single))
    unit, _ = standardized(mid_ref[...])
    gh = gh_ref[...]
    for row, value in ((0, g.astype(single)), (1 + steps, gh * unit), (2 + steps, gh)):
        sums = jnp.where(place == row, jnp.sum(value, 0, keepdims=True), sums)
    buf_ref[small] = sums.astype(narrow)
    out_ref[...] = out_s[...].astype(narrow)
    split_out(buf_ref, keep_ref, send_ref, sems, 1)
    for copy in copies:
        copy.wait()


def branch_kernel(
    loads, mid_ref, gh_ref, g_ref, att_ref, tv_ref, own_ref, wo_ref, gm_ref, gw_ref, ga_ref, dm_ref, delta_ref, ods_ref
):
    unit, spread = standardized(mid_ref[...])
    gm = g_ref[...].astype(single) + norm_back(gh_ref[...], unit, spread, loads[0][...])
    gm_ref[...] = gm
    branch = gm.astype(narrow)
    att = att_ref[...]
    ga = nt(branch, wo_ref[...]).astype(narrow)
    ga_ref[...] = ga
    split_heads(ga, dm_ref)
    wide = ga.astype(single)
    delta = head_sums(wide * att)
    delta_ref[...] = delta
    dprob = head_sums(wide * tv_ref[...].astype(single))
    ods_ref[...] = (own_ref[...] * (dprob - delta)).astype(narrow)
    gw_ref[...] = tn(att.astype(narrow), branch).astype(narrow)


def reorder_kernel(out_ref, gx_ref, to_out_ref, to_gx_ref):
    order = token_order(out_ref.shape[0])
    to_out_ref[...] = tn(order, out_ref[...]).astype(narrow)
    to_gx_ref[...] = tn(order, gx_ref[...]).astype(narrow)


def back_block(kv_ref, number, pair, qm_ref, dm_ref, lse_ref, delta_ref, diagonal):
    slots, width = kv_ref.shape[1], qm_ref.shape[2]
    cols = slice(PAIR * pair, PAIR * (pair + 1))
    k = kv_ref[number, :, cols]
    v = kv_ref[number, :, width + cols.start : width + cols.stop]
    lane = lax.broadcasted_iota(jnp.int32, (1, PAIR), 1)
    scores, probs = [], []
    for half in range(2):
        h = 2 * pair + half
        prob = jnp.exp(nt(k, qm_ref[half, :, cols]) - lse_ref[h : h + 1, :])
        dprob = nt(v, dm_ref[half, :, cols])
        if diagonal:
            slot = lax.broadcasted_iota(jnp.int32, prob.shape, 0)
            row = lax.broadcasted_iota(jnp.int32, prob.shape, 1)
            prob = jnp.where(3 * slot + 2 <= 3 * (row % slots) + row // slots, prob, 0.0)
        scores.append((prob * (dprob - delta_ref[h : h + 1, :])).astype(narrow))
        probs.append(prob.astype(narrow))
    dk = nn(scores[0], qm_ref[0, :, cols]) + nn(scores[1], qm_ref[1, :, cols])
    dv = nn(probs[0], dm_ref[0, :, cols]) + nn(probs[1], dm_ref[1, :, cols])
    nothing = jnp.zeros_like(k)
    split_k = jnp.concatenate([jnp.where(lane < HEAD_DIM, k, nothing), jnp.where(lane >= HEAD_DIM, k, nothing)], 0)
    return dk, dv, tn(jnp.concatenate(scores, 0), split_k)


def attend_back_kernel(tab_ref, qm_ref, dm_ref, lse_ref, delta_ref, kv_ref, *rest, list_at, first, pair):
    dq_in, (dq_ref, out_ref) = rest[:-2], rest[-2:]
    blocks, slots, _ = out_ref.shape
    dq_ref[...] = dq_in[0][...] if dq_in else jnp.zeros(dq_ref.shape, single)

    def step(i, carry):
        number = tab_ref[list_at + 1 + i]
        dk, dv, dq = back_block(kv_ref, number, pair, qm_ref, dm_ref, lse_ref, delta_ref, False)
        dq_ref[...] += dq
        out_ref[number - first, :, :PAIR] = dk.astype(narrow)
        out_ref[number - first, :, PAIR:] = dv.astype(narrow)
        return carry

    def clear(i, carry):
        out_ref[tab_ref[list_at + 1 + i] - first] = jnp.zeros((slots, 2 * PAIR), narrow)
        return carry

    others = blocks - 1 if first == 0 else blocks
    count = tab_ref[list_at]
    lax.fori_loop(0, count, step, 0)
    lax.fori_loop(count, others, clear, 0)
    if first == 0:
        out_ref[0] = jnp.zeros((slots, 2 * PAIR), narrow)


def attend_back_own_kernel(qm_ref, dm_ref, lse_ref, delta_ref, kv_ref, *rest, pairs):
    dq_in, (dq_ref, *out_refs) = rest[:pairs], rest[pairs:]
    width = qm_ref.shape[2]
    group = width // len(out_refs)
    for pair in range(pairs):
        dk, dv, dq = back_block(kv_ref, 0, pair, qm_ref, dm_ref, lse_ref, delta_ref, True)
        dq_ref[:, PAIR * pair : PAIR * (pair + 1)] = dq_in[pair][...] + dq
        out_ref, first = out_refs[PAIR * pair // group], PAIR * pair % group
        out_ref[:, first : first + PAIR] = dk
        out_ref[:, group + first : group + first + PAIR] = dv


def sum_split_kernel(a_ref, b_ref, *out_refs, last):
    total = (a_ref[...].astype(single) + b_ref[...].astype(single)).astype(narrow)
    if len(out_refs) == 1:
        out_refs[0][...] = total
        return
    keep_ref, send_ref = out_refs
    half = (total.shape[0] - last) // 2
    keep_ref[pl.ds(0, half)] = total[:half]
    send_ref[...] = total[half:]
    if last:
        keep_ref[pl.ds(half, last)] = total[2 * half :]


def join_kernel(a_ref, b_ref, out_ref):
    half = a_ref.shape[0]
    out_ref[pl.ds(0, half)] = a_ref[...]
    out_ref[pl.ds(half, half)] = b_ref[...]


def group_split_kernel(*refs):
    shares, (keep_ref, send_ref) = refs[:-2], refs[-2:]
    pairs = len(shares) // 2
    half = keep_ref.shape[0]
    for pair in range(pairs):
        total = (shares[2 * pair][...].astype(single) + shares[2 * pair + 1][...].astype(single)).astype(narrow)
        for out_ref, part in ((keep_ref, total[:half]), (send_ref, total[half:])):
            for number in range(2):
                first = (number * pairs + pair) * PAIR
                out_ref[:, :, first : first + PAIR] = part[:, :, number * PAIR : (number + 1) * PAIR]


def store_tiles(buf_ref, first, values):
    for t in range(values.shape[0] // TILE):
        buf_ref[first + t] = values[t * TILE : (t + 1) * TILE]


def split_out(buf_ref, keep_ref, send_ref, sems, last):
    half = (buf_ref.shape[0] - last) // 2
    copies = [
        pltpu.make_async_copy(buf_ref.at[pl.ds(0, half)], keep_ref.at[pl.ds(0, half)], sems.at[0]),
        pltpu.make_async_copy(buf_ref.at[pl.ds(half, half + last)], send_ref, sems.at[1]),
    ]
    if last:
        copies.append(
            pltpu.make_async_copy(buf_ref.at[pl.ds(2 * half, last)], keep_ref.at[pl.ds(half, last)], sems.at[2])
        )
    for copy in copies:
        copy.start()
    for copy in copies:
        copy.wait()


def conv_grads(tab_ref, buf_ref, tk_ref, tv_ref, grad, tiles, pieces, inverse_at):
    width = tk_ref.shape[1]
    slots = grad.shape[0]
    group = grad.shape[1] // 2
    conv_tiles = TAPS * width // pieces // TILE
    for i in range(TAPS):
        own = slice(i * slots, (i + 1) * slots)
        both = jnp.concatenate([tn(tk_ref[own], grad[:, :group]), tn(tv_ref[own], grad[:, group:])], 1).astype(narrow)
        for j in range(width // TILE):
            tile = i * (width // TILE) + j
            at = tab_ref[inverse_at + tile // conv_tiles] * tiles + tile % conv_tiles
            buf_ref[at] = both[j * TILE : (j + 1) * TILE]


def tail_query_kernel(hid_ref, tk_ref, ods_ref, dq_ref, wq_ref, gh_ref, gw_ref):
    own_ds = tn(ods_ref[...], head_rows(tk_ref.shape[1])) * scale
    gq = (dq_ref[...] * scale + own_ds * tk_ref[...].astype(single)).astype(narrow)
    gw_ref[...] = tn(hid_ref[...], gq).astype(narrow)
    gh_ref[...] = nt(gq, wq_ref[...])


def tail_first_kernel(
    tab_ref, tk_ref, tv_ref, first_ref, second_ref, own_ref, gw_ref, gw_out_ref, ck_ref, cv_ref,
    gk_ref, gv_ref, keep_ref, send_ref, buf_ref, sems, *, pieces, inverse_at,
):
    tiles = buf_ref.shape[0] // pieces
    grad = slot_grads(first_ref, second_ref, own_ref)
    conv_grads(tab_ref, buf_ref, tk_ref, tv_ref, grad, tiles, pieces, inverse_at)
    for j in range(pieces):
        at = tab_ref[inverse_at + j] * tiles + tiles - 2
        buf_ref[at] = gw_ref[j * TILE : (j + 1) * TILE]
        buf_ref[at + 1] = gw_out_ref[j * TILE : (j + 1) * TILE]
    split_out(buf_ref, keep_ref, send_ref, sems, 0)
    conv_back(grad, ck_ref, cv_ref, 0, gk_ref, gv_ref)


def slot_grads(first_ref, second_ref, own_ref):
    return (first_ref[...].astype(single) + second_ref[...].astype(single) + own_ref[...]).astype(narrow)


def conv_back(grads, ck_ref, cv_ref, first, gk_ref, gv_ref):
    slots, width = grads.shape[0], ck_ref.shape[1]
    group = grads.shape[1] // 2
    for grad, c_ref, out_ref in ((grads[:, :group], ck_ref, gk_ref), (grads[:, group:], cv_ref, gv_ref)):
        for i in range(TAPS):
            out_ref[i * slots : (i + 1) * slots] = nt(grad, c_ref[i * width : (i + 1) * width, first : first + group])


def tail_kernel(
    tab_ref, x_ref, hid_ref, q_ref, tk_ref, tv_ref, ga_ref, gm_ref, own_ref, ods_ref, gh_ref, gk0_ref, gv0_ref,
    first_ref, second_ref, own_grad_ref, wk_ref, wv_ref, ck_ref, cv_ref, gain_ref, gx_ref, keep_ref, send_ref, buf_ref, gk_s, gv_s, sems, *, pieces, inverse_at,
):
    rows, width = x_ref.shape
    tiles = (buf_ref.shape[0] - 1) // pieces
    conv_tiles = tiles - 2
    grad = slot_grads(first_ref, second_ref, own_grad_ref)
    conv_grads(tab_ref, buf_ref, tk_ref, tv_ref, grad, tiles, pieces, inverse_at)
    marks = head_rows(width)
    own_ds = tn(ods_ref[...], marks) * scale
    own_prob = tn(own_ref[...].astype(narrow), marks)
    conv_back(grad, ck_ref, cv_ref, grad.shape[1] // 2, gk_s, gv_s)
    gk = (gk_s[...] + gk0_ref[...] + own_ds * q_ref[...].astype(single)).astype(narrow)
    gv = (gv_s[...] + gv0_ref[...] + own_prob * ga_ref[...].astype(single)).astype(narrow)
    hidden_t = hid_ref[...].T
    grad_hidden = gh_ref[...]
    for number, grad in enumerate((gk, gv)):
        grad_w = nn(hidden_t, grad).astype(narrow)
        for j in range(pieces):
            buf_ref[tab_ref[inverse_at + j] * tiles + conv_tiles + number] = grad_w[j * TILE : (j + 1) * TILE]
        grad_hidden += nt(grad, (wk_ref, wv_ref)[number][...])
    unit, spread = standardized(x_ref[...].astype(single))
    place = lax.broadcasted_iota(jnp.int32, (TILE, width), 0)
    sums = jnp.where(place == 0, jnp.sum(grad_hidden * unit, 0, keepdims=True), 0.0)
    sums = jnp.where(place == 1, jnp.sum(grad_hidden, 0, keepdims=True), sums)
    buf_ref[buf_ref.shape[0] - 1] = sums.astype(narrow)
    split_out(buf_ref, keep_ref, send_ref, sems, 1)
    gx_ref[...] = (gm_ref[...] + norm_back(grad_hidden, unit, spread, gain_ref[...])).astype(narrow)


def unpack_feed_kernel(tab_ref, own_ref, other_ref, wd_ref, wu_ref, *, pieces, piece_at):
    width = wd_ref.shape[1]
    down_rows = wd_ref.shape[0] // pieces
    down_tiles, up_tiles = down_rows // TILE, wu_ref.shape[1] // width
    tiles = down_tiles + up_tiles

    for number, buf_ref in enumerate((own_ref, other_ref)):

        def step(k, carry, number=number, buf_ref=buf_ref):
            piece = tab_ref[piece_at + number * pieces // 2 + k]
            at = k * tiles
            for t in range(down_tiles):
                rows = pl.ds(pl.multiple_of(piece * down_rows + t * TILE, TILE), TILE)
                wd_ref[rows, :] = buf_ref[at + t].astype(single)
            mine = pl.ds(pl.multiple_of(piece * TILE, TILE), TILE)
            for t in range(up_tiles):
                wu_ref[mine, t * width : (t + 1) * width] = buf_ref[at + down_tiles + t].astype(single)
            return carry

        lax.fori_loop(0, pieces // 2, step, 0, unroll=4)


def unpack_kernel(tab_ref, *rest, places, group, outs):
    bufs, rest = rest[: len(places)], rest[len(places) :]
    out_refs, (conv_s, weight_s, sems) = rest[-outs - 3 : -3], rest[-3:]
    weight_refs, conv_refs = out_refs[:-2], out_refs[-2:]
    conv_rows, columns = conv_s.shape[2], conv_s.shape[3]
    conv_tiles = conv_rows // TILE
    tiles = conv_tiles + len(weight_refs)
    copies = []
    for buf_ref, found in zip(bufs, places):
        for k, (number, piece_at) in enumerate(found):
            piece = tab_ref[piece_at]
            for t in range(conv_tiles):
                both = buf_ref[k * tiles + t].astype(single)
                conv_s[number, 0, t * TILE : (t + 1) * TILE] = both[:, :columns]
                conv_s[number, 1, t * TILE : (t + 1) * TILE] = both[:, columns:]
            for t in range(len(weight_refs)):
                weight_s[number, t] = buf_ref[k * tiles + conv_tiles + t].astype(single)
            rows = pl.ds(pl.multiple_of(piece * conv_rows, TILE), conv_rows)
            mine = pl.ds(pl.multiple_of(piece * TILE, TILE), TILE)
            cols = pl.ds(group * columns, columns)
            copies += [
                pltpu.make_async_copy(conv_s.at[number, i], ref.at[rows, cols], sems.at[number, i])
                for i, ref in enumerate(conv_refs)
            ]
            copies += [
                pltpu.make_async_copy(weight_s.at[number, i], ref.at[mine], sems.at[number, 2 + i])
                for i, ref in enumerate(weight_refs)
            ]
            for copy in copies[-outs:]:
                copy.start()
    for copy in copies:
        copy.wait()


def shaped(shape, kind):
    return jax.ShapeDtypeStruct(shape, kind)


def per_device(
    seq_size, batch_size,
    inputs, cotangent, ln1_gain, ln1_bias, w_query, w_key, w_value, conv_key, conv_value, w_out,
    ln2_gain, ln2_bias, w_up, up_bias, w_down, down_bias,
):
    x, g = inputs[0], cotangent[0]
    rows, width = x.shape
    slots = rows // TAPS
    ff = w_up.shape[1]
    seq_bits, batch_bits = seq_size.bit_length() - 1, batch_size.bit_length() - 1
    split_bits = min(5, seq_bits + batch_bits)
    pieces = 1 << split_bits
    low_list_at, high_list_at = seq_size, seq_size + seq_size // 2
    piece_at = high_list_at + 1 + seq_size // 2
    inverse_at = piece_at + pieces
    tables = jnp.asarray(plan_tables(seq_size, batch_size, split_bits))
    table = lax.dynamic_index_in_dim(
        tables, lax.axis_index("seq") * batch_size + lax.axis_index("batch"), 0, keepdims=False
    )
    x = tied(x, table)
    row = lambda v: v.reshape(1, -1)
    ck = conv_key.reshape(TAPS * width, width)
    cv = conv_value.reshape(TAPS * width, width)
    token_low, token_wide = shaped((rows, width), narrow), shaped((rows, width), single)
    head_wide, head_low = shaped((HEADS, rows), single), shaped((HEADS, rows), narrow)
    two_low = shaped((2, rows, width), narrow)

    xp, hidden, tk, tv, kv = call(
        "front",
        front_kernel,
        (token_low,) * 4 + (shaped((slots, 2 * width), narrow),),
        loads=(x, row(ln1_gain), row(ln1_bias), w_key, ck, w_value, cv),
        mib=24,
        flops=4e9,
    )

    state = shaped((HEADS, rows, PAIR), single)
    q, gp, qm, own, m, acc = call(
        "attend_own",
        attend_own_kernel,
        (token_low, token_low, two_low, head_wide, state, state),
        loads=(w_query, g),
        operands=(hidden, tk, tv, kv[None]),
        mib=16,
        flops=1e10,
    )
    blocks = {0: kv[None]}
    rounds = gather_plan(seq_size)
    calls = []
    for number, found in enumerate(rounds):
        if number > 0:
            calls.append([entry[0] for entry in rounds[number - 1]])
        held = {source: blocks[source] for _, source, _ in found if source in blocks}
        if number > 1:
            held = tied(held, m)
        for block, source, (axis, pairs) in found:
            if source in held:
                blocks[block] = lax.ppermute(held[source], axis, pairs)
        if number == 0:
            continue
        later = [entry for entry in found if entry[0] not in blocks]
        found = calls[-1]
        m, acc = call(
            f"attend_{found[0]}",
            functools.partial(attend_more_kernel, blocks=found),
            (state, state),
            table=table,
            operands=(qm, m, acc, *[blocks[k] for k in found]),
            mib=8,
            flops=1e10 * len(found),
        )
        for block, source, (axis, pairs) in later:
            blocks[block] = lax.ppermute(tied(blocks[source], m), axis, pairs)
    calls.append([entry[0] for entry in rounds[-1]])
    attended, lse, own_prob = call(
        "attend_last",
        functools.partial(attend_last_kernel, blocks=calls[-1]),
        (token_wide, head_wide, head_wide),
        table=table,
        operands=(qm, own, m, acc, *[blocks[k] for k in calls[-1]]),
        scratch=[pltpu.VMEM(state.shape, single), pltpu.VMEM(state.shape, single)],
        mib=16,
        flops=1e10 * len(calls[-1]),
    )

    steps = ff // width
    tiles = ff // pieces // TILE + steps
    half = shaped((pieces // 2 * tiles + 1, TILE, width), narrow)
    output, middle, grad_normal, keep, send, all_kv = call(
        "feed",
        functools.partial(feed_kernel, pieces=pieces, inverse_at=inverse_at),
        (token_low, token_wide, token_wide, half, half, shaped((seq_size, slots, 2 * width), narrow)),
        loads=(row(ln2_gain), row(ln2_bias), w_up, row(up_bias), w_down, row(down_bias)),
        table=table,
        operands=(xp, attended, gp, w_out),
        away=[blocks[k] for k in range(seq_size)],
        away_outs=3,
        scratch=[
            pltpu.VMEM((rows, width), narrow),
            pltpu.VMEM((width, rows), narrow),
            pltpu.VMEM((rows, width), single),
            pltpu.VMEM((pieces * tiles + 1, TILE, width), narrow),
            pltpu.SemaphoreType.DMA((3 + seq_size,)),
        ],
        mib=30,
        flops=5e10,
    )
    grad_middle, grad_w_out_here, grad_attended, dm, delta, own_ds = call(
        "branch",
        branch_kernel,
        (token_wide, shaped((width, width), narrow), token_low, two_low, head_wide, head_low),
        loads=(row(ln2_gain),),
        operands=(middle, grad_normal, gp, attended, tv, own_prob, w_out),
        mib=16,
        flops=3e10,
    )

    stages = reduce_stages(seq_size, batch_size)
    gather_back = stages[:split_bits][::-1]
    unseen = gather_stages(seq_size)[::-1]
    head_pairs = HEADS // 2

    wide_grant = 12 if seq_size <= 8 else 56
    share = shaped((seq_size // 2, slots, 2 * PAIR), narrow)

    def back(pair, high, qm, *dq):
        return call(
            f"attend_back_{pair}",
            functools.partial(
                attend_back_kernel,
                list_at=high_list_at if high else low_list_at,
                first=seq_size // 2 if high else 0,
                pair=pair,
            ),
            (shaped((rows, PAIR), single), share),
            table=table,
            operands=(qm, dm, lse, delta, all_kv, *dq),
            mib=wide_grant,
            flops=3e10,
        )

    def small_call(kernel, name, outs, *operands):
        return call(name, kernel, outs, operands=operands, mib=4, flops=sum(v.size for v in operands) * 600)

    def sum_split(a, b, last, whole=False):
        count, rest = a.shape[0], a.shape[1:]
        shapes = [count] if whole else [(count + last) // 2] * 2
        outs = tuple(shaped((n, *rest), narrow) for n in shapes)
        return small_call(functools.partial(sum_split_kernel, last=last), "sum_split", outs, a, b)

    def join(a, b):
        return small_call(join_kernel, "join", (shaped((2 * a.shape[0], *a.shape[1:]), narrow),), a, b)[0]

    class Sum:
        def __init__(self, keep, send, last):
            self.keep, self.last, self.at, self.held = keep, last, 0, None
            self.tiles = send.shape[0] - last
            self.arrived = lax.ppermute(send, *stages[0])

        def step(self, *others):
            arrived = tied(self.arrived, *others)
            self.at += 1
            if self.at > len(stages):
                self.held = join(self.held, arrived)
            elif self.at < split_bits:
                self.keep, send = sum_split(self.keep, arrived, self.last)
            else:
                (total,) = sum_split(self.keep, arrived, self.last, whole=True)
                self.keep = send = total
                if self.at == len(stages):
                    self.small = total[-1].astype(single)
                    self.held = total[:-1] if self.last else total
            if self.at >= len(stages):
                send = self.held
                self.arrived = lax.ppermute(send, *gather_back[self.at - len(stages)])
            else:
                self.arrived = lax.ppermute(send, *stages[self.at])
            return send

        def left(self):
            return len(stages) + split_bits - 1 - self.at

    class Group:
        def __init__(self):
            self.shares, self.at = [], 0

        def step(self, *others):
            self.at += 1
            if self.at == 1:
                operands = [v for kept, other in self.shares for v in (kept, tied(other, *others))]
                half = shaped((seq_size // 4, slots, width), narrow)
                self.keep, send = small_call(group_split_kernel, "group_split", (half, half), *operands)
            else:
                self.keep, send = sum_split(self.keep, tied(self.arrived, *others), 0)
            self.arrived = lax.ppermute(send, *unseen[self.at])
            return send

        def left(self):
            return len(unseen) - 1 - self.at

    feed_sum = Sum(keep, send, 1)
    first_group, second_group = Group(), Group()
    conv_tiles = TAPS * width // pieces // TILE
    first_tiles = conv_tiles + 2
    grad_q = []
    operand = tied(qm, feed_sum.step(delta))
    for pair in range(head_pairs):
        group = first_group if pair < head_pairs // 2 else second_group
        part_q, sent = back(pair, True, operand)
        arrived = lax.ppermute(sent, *unseen[0])
        waits = [part_q]
        if pair >= head_pairs // 2 and first_group.left() > 0:
            waits.append(first_group.step(*waits))
        all_q, kept = back(pair, False, tied(qm, *waits), part_q)
        grad_q.append(all_q)
        group.shares.append((kept, arrived))
        waits = [all_q]
        if pair == head_pairs - 1:
            waits.append(second_group.step(*waits))
        if feed_sum.left() > 1:
            waits.append(feed_sum.step(*waits))
        if pair >= head_pairs // 2 - 1 and first_group.left() > 0:
            waits.append(first_group.step(*waits))
        operand = tied(qm, *waits)
    own_grad = shaped((slots, width), single)
    all_q, first_own, second_own = call(
        "attend_back_own",
        functools.partial(attend_back_own_kernel, pairs=head_pairs),
        (token_wide, own_grad, own_grad),
        operands=(operand, dm, lse, delta, kv[None], *grad_q),
        mib=12,
        flops=3e10,
    )
    waits = [all_q]
    if second_group.left() > 0:
        waits.append(second_group.step(*waits))
    if feed_sum.left() > 1:
        waits.append(feed_sum.step(*waits))

    grad_hidden, grad_wq_here = call(
        "tail_query",
        tail_query_kernel,
        (token_wide, shaped((width, width), narrow)),
        operands=(tied(hidden, *waits), tk, own_ds, all_q, w_query),
        mib=16,
        flops=1e10,
    )
    while first_group.left() > 0:
        first_group.step(grad_hidden)

    half = shaped((pieces // 2 * first_tiles, TILE, width), narrow)
    grad_k, grad_v, keep0, send0 = call(
        "tail_first",
        functools.partial(tail_first_kernel, pieces=pieces, inverse_at=inverse_at),
        (token_wide, token_wide, half, half),
        table=table,
        operands=(
            tk, tv, tied(first_group.keep[0], grad_hidden), first_group.arrived[0], first_own,
            grad_wq_here, grad_w_out_here, ck, cv,
        ),
        away_outs=2,
        scratch=[pltpu.VMEM((pieces * first_tiles, TILE, width), narrow), pltpu.SemaphoreType.DMA((3,))],
        mib=20,
        flops=1.5e10,
    )
    first_sum = Sum(keep0, send0, 0)
    waits = [grad_k]
    while second_group.left() > 0:
        waits = [second_group.step(*waits)]
    if feed_sum.left() > 1:
        waits.append(feed_sum.step(*waits))

    tail_tiles = conv_tiles + 2
    half = shaped((pieces // 2 * tail_tiles + 1, TILE, width), narrow)
    grad_x, keep1, send1 = call(
        "tail",
        functools.partial(tail_kernel, pieces=pieces, inverse_at=inverse_at),
        (token_low, half, half),
        table=table,
        operands=(
            xp, hidden, q, tk, tv, grad_attended, grad_middle, own_prob, own_ds, grad_hidden, grad_k, grad_v,
            tied(second_group.keep[0], *waits), second_group.arrived[0], second_own,
            w_key, w_value, ck, cv, row(ln1_gain),
        ),
        away_outs=2,
        scratch=[
            pltpu.VMEM((pieces * tail_tiles + 1, TILE, width), narrow),
            pltpu.VMEM((rows, width), single),
            pltpu.VMEM((rows, width), single),
            pltpu.SemaphoreType.DMA((3,)),
        ],
        mib=26,
        flops=3e10,
    )
    second_sum = Sum(keep1, send1, 1)

    chains = {"first": first_sum, "feed": feed_sum, "second": second_sum}
    order = step_order(first_sum.left(), second_sum.left(), feed_sum.left())

    def unpack(name, places, group, bufs, *known):
        count = sum(len(found) for found in places)
        outs = [shaped((width, width), single)] * 2 + [shaped(ck.shape, single)] * 2
        numbered, at = [], 0
        for found in places:
            numbered.append([(at + i, piece_at + k) for i, k in enumerate(found)])
            at += len(found)
        return call(
            name,
            functools.partial(unpack_kernel, places=numbered, group=group, outs=len(outs)),
            outs,
            table=table,
            operands=bufs,
            away=known,
            away_outs=len(outs),
            in_place=len(known),
            scratch=[
                pltpu.VMEM((count, 2, conv_tiles * TILE, width // 2), single),
                pltpu.VMEM((count, len(outs) - 2, TILE, width), single),
                pltpu.SemaphoreType.DMA((count, len(outs))),
            ],
            mib=20,
            flops=1.5e10,
        )

    half_places, other_places = list(range(pieces // 2)), list(range(pieces // 2, pieces))
    waits = [grad_x]
    for number, name in enumerate(order):
        chain = chains[name]
        if chain.left() > 0:
            waits = [chain.step(*waits)]
            if chain is second_sum and chain.at == len(stages):
                small_tail, small_feed = second_sum.small, tied(feed_sum.small, *waits)
                small = (
                    small_tail[0],
                    small_tail[1],
                    small_feed[1 + steps],
                    small_feed[2 + steps],
                    small_feed[1 : 1 + steps].reshape(ff),
                    small_feed[0],
                )
                waits += small
        elif name == "feed":
            grad_w_down, grad_w_up = call(
                "unpack_feed",
                functools.partial(unpack_feed_kernel, pieces=pieces, piece_at=piece_at),
                (shaped((ff, width), single), shaped((width, ff), single)),
                table=table,
                operands=(feed_sum.held, tied(feed_sum.arrived, *waits)),
                mib=16,
                flops=2e10,
            )
            waits = [grad_w_up]
        elif name == "first":
            grad_wq, grad_w_out, *grad_convs = unpack(
                "unpack_first",
                [half_places, other_places],
                0,
                (first_sum.held, tied(first_sum.arrived, *waits)),
            )
            waits = [grad_wq]
        if number == 0:
            output, grad_x = call(
                "reorder",
                reorder_kernel,
                (token_low, token_low),
                operands=(output, tied(grad_x, *waits)),
                mib=8,
                flops=1e10,
            )
            waits = [grad_x]
    found = unpack("unpack_own", [half_places], 1, (second_sum.held,), *tied(grad_convs, *waits))
    grad_wk, grad_wv, grad_ck, grad_cv = unpack("unpack_last", [other_places], 1, (second_sum.arrived,), *found)
    return (
        output[None],
        grad_x[None],
        small[0],
        small[1],
        grad_wq,
        grad_wk,
        grad_wv,
        grad_ck.reshape(conv_key.shape),
        grad_cv.reshape(conv_value.shape),
        grad_w_out,
        small[2],
        small[3],
        grad_w_up,
        small[4],
        grad_w_down,
        small[5],
    )


def solution(mesh):
    placed = (P("batch", "seq", None),) * 2 + (P(),) * 14
    return jax.shard_map(
        functools.partial(per_device, mesh.shape["seq"], mesh.shape["batch"]),
        mesh=mesh,
        in_specs=placed,
        out_specs=placed,
        check_vma=False,
    )
```

```python
import functools

import jax
import jax.numpy as jnp
import numpy as np
from jax import lax
from jax.experimental import pallas as pl
from jax.experimental.pallas import tpu as pltpu
from jax.sharding import PartitionSpec as P

HEADS = 8
HEAD_DIM = 64
PAIR = 2 * HEAD_DIM
TAPS = 3
TILE = 16
COLUMNS = 512
GROUPS = (2, 2)

epsilon = 1e-05
narrow = jnp.bfloat16
single = jnp.float32
scale = HEAD_DIM ** (-0.5)

vmem = pl.BlockSpec(memory_space=pltpu.VMEM)
smem = pl.BlockSpec(memory_space=pltpu.SMEM)
anywhere = pl.BlockSpec(memory_space=pl.ANY)
hbm = pl.BlockSpec(memory_space=pltpu.HBM)


def params(mib):
    return pltpu.CompilerParams(vmem_limit_bytes=mib * 2**20)


def cost(flops, moved):
    return pl.CostEstimate(flops=int(flops), bytes_accessed=int(moved), transcendentals=0)


class Loads:
    def __init__(self, sources, held, sems):
        self.held, self.waited = held, set()
        self.copies = [pltpu.make_async_copy(a, b, sems.at[i]) for i, (a, b) in enumerate(zip(sources, held))]
        for copy in self.copies:
            copy.start()

    def __getitem__(self, i):
        if i not in self.waited:
            self.copies[i].wait()
            self.waited.add(i)
        return self.held[i]


def call(
    name, body, outs, *, loads=(), table=None, operands=(), away=(), away_outs=0, in_place=0, scratch=(), mib, flops
):
    count = len(loads)
    inputs = count + (table is not None) + len(operands) + len(away)

    def kernel(*refs):
        sources, rest = refs[:count], refs[count:]
        if count == 0:
            return body(*rest)
        held, sems = rest[-count - 1 : -1], rest[-1]
        return body(Loads(sources, held, sems), *rest[: -count - 1])

    moved = sum(v.size * 2 for v in (*loads, *operands, *away, *outs))
    scratch = list(scratch)
    if count:
        scratch += [pltpu.VMEM(v.shape, v.dtype) for v in loads] + [pltpu.SemaphoreType.DMA((count,))]
    return pl.pallas_call(
        kernel,
        out_shape=tuple(outs),
        in_specs=[hbm] * count + [smem] * (table is not None) + [vmem] * len(operands) + [anywhere] * len(away),
        out_specs=(vmem,) * (len(outs) - away_outs) + (anywhere,) * away_outs,
        scratch_shapes=scratch,
        input_output_aliases={inputs - in_place + i: len(outs) - in_place + i for i in range(in_place)},
        compiler_params=params(mib),
        cost_estimate=cost(flops, moved),
        name=name,
    )(
        *[pltpu.with_memory_space_constraint(v, pltpu.HBM) for v in loads],
        *([] if table is None else [table]),
        *operands,
        *away,
    )


def tied(values, *others):
    return lax.optimization_barrier((values, others))[0]


def nn(a, b):
    return lax.dot_general(a, b, (((1,), (0,)), ((), ())), preferred_element_type=single)


def nt(a, b):
    return lax.dot_general(a, b, (((1,), (1,)), ((), ())), preferred_element_type=single)


def tn(a, b):
    return lax.dot_general(a, b, (((0,), (0,)), ((), ())), preferred_element_type=single)


def bit_masks(size):
    return [1 << b for b in range(size.bit_length() - 1)]


def seq_masks(size, core):
    masks = bit_masks(size)[1:]
    return masks if core == 0 else masks[::-1]


def seq_swap(size, stage):
    return [(i, i ^ seq_masks(size, i & 1)[stage]) for i in range(size)]


def gather_stages(seq_size):
    found = [("seq", seq_swap(seq_size, j)) for j in range(len(bit_masks(seq_size)) - 1)]
    return found + [("seq", [(i, i ^ 1) for i in range(seq_size)])]


def reduce_stages(seq_size, batch_size, split_bits):
    found = [(2, "seq", [[(i, i ^ 1) for i in range(seq_size)]])]
    found += [(2, "seq", [seq_swap(seq_size, j)]) for j in range(len(bit_masks(seq_size)) - 1)]
    split = split_bits - len(found)
    for j, mask in enumerate(bit_masks(batch_size)):
        found.append((2 if j < split else 1, "batch", [[(i, i ^ mask) for i in range(batch_size)]]))
    return found


def gather_origin(seq_size, me, block):
    count = len(bit_masks(seq_size)) - 1
    core_bit = (block >> count) & 1
    other = me ^ core_bit
    masks = seq_masks(seq_size, other & 1)
    for j in range(count):
        if (block >> j) & 1:
            other ^= masks[j]
    return other


def piece_of(seq_size, batch_size, split_bits, me_seq, me_batch, place):
    bits = [(place >> (split_bits - 1 - j)) & 1 for j in range(split_bits)]
    s = me_seq ^ bits[0]
    masks = seq_masks(seq_size, s & 1)
    z = me_batch
    for j, b in enumerate(bits[1:]):
        if j < len(masks):
            s ^= masks[j] * b
        else:
            z ^= (1 << (j - len(masks))) * b
    low_batch = z & ((1 << (split_bits - len(bit_masks(seq_size)))) - 1)
    return s + seq_size * low_batch


def gather_plan(seq_size):
    stages = gather_stages(seq_size)
    count = len(stages) - 1
    rounds = [[] for _ in range(count + 1)]
    for block in range(1, 1 << count):
        last = block.bit_length() - 1
        rounds[bin(block).count("1")].append((block, block ^ (1 << last), stages[last]))
    for found in rounds:
        blocks = [entry[0] for entry in found] or [0]
        found += [(block | (1 << count), block, stages[-1]) for block in blocks]
    return rounds


def plan_tables(seq_size, batch_size, split_bits):
    rows = []
    pieces = 1 << split_bits
    for s in range(seq_size):
        origins = [gather_origin(seq_size, s, k) for k in range(seq_size)]
        seen = [int(origin < s) for origin in origins]
        visible = [k for k in range(seq_size) if origins[k] < s]
        lists = [len(visible)] + visible + [k for k in range(seq_size) if origins[k] > s]
        for z in range(batch_size):
            places = [piece_of(seq_size, batch_size, split_bits, s, z, k) for k in range(pieces)]
            inverse = [places.index(p) for p in range(pieces)]
            rows.append(seen + lists + places + inverse)
    return np.asarray(rows, np.int32)


def token_order(rows):
    slots = rows // TAPS
    r = lax.broadcasted_iota(jnp.int32, (rows, rows), 0)
    c = lax.broadcasted_iota(jnp.int32, (rows, rows), 1)
    return jnp.where(c == TAPS * (r % slots) + r // slots, 1.0, 0.0).astype(narrow)


def head_rows(width):
    r = lax.broadcasted_iota(jnp.int32, (HEADS, width), 0)
    c = lax.broadcasted_iota(jnp.int32, (HEADS, width), 1)
    return jnp.where(c // HEAD_DIM == r, 1.0, 0.0).astype(narrow)


def head_sums(values):
    marks = head_rows(values.shape[1])
    high = values.astype(narrow)
    rest = values - high.astype(single)
    middle = rest.astype(narrow)
    low = (rest - middle.astype(single)).astype(narrow)
    return nt(marks, high) + nt(marks, middle) + nt(marks, low)


def standardized(values):
    centred = values - jnp.mean(values, -1, keepdims=True)
    spread = lax.rsqrt(jnp.mean(centred * centred, -1, keepdims=True) + epsilon)
    return centred * spread, spread


def norm_back(grad, unit, spread, gain):
    inner = grad * gain
    return spread * (
        inner
        - jnp.mean(inner, -1, keepdims=True)
        - unit * jnp.mean(inner * unit, -1, keepdims=True)
    )


def front_kernel(loads, xp_ref, hid_ref, tk_ref, tv_ref, kv_ref):
    rows, width = xp_ref.shape
    slots = rows // TAPS
    order = token_order(rows)
    x = nn(order, loads[0][...])
    xp_ref[...] = x.astype(narrow)
    unit, _ = standardized(x)
    hidden = (unit * loads[1][...] + loads[2][...]).astype(narrow)
    hid_ref[...] = hidden
    for number, t_ref in enumerate((tk_ref, tv_ref)):
        t = nn(hidden, loads[3 + 2 * number][...]).astype(narrow)
        t_ref[...] = t
        c_ref = loads[4 + 2 * number]
        total = nn(t[:slots], c_ref[:width])
        for i in range(1, TAPS):
            total += nn(t[i * slots : (i + 1) * slots], c_ref[i * width : (i + 1) * width])
        kv_ref[:, number * width : (number + 1) * width] = total.astype(narrow)


def attend_block(kv_ref, number, qm_ref, m_ref, acc_ref, diagonal):
    slots, width = kv_ref.shape[1], qm_ref.shape[2]
    lane = lax.broadcasted_iota(jnp.int32, (1, PAIR), 1)

    def heads(i, carry):
        for n in range(4):
            h = 4 * i + n
            first = pl.multiple_of((h // 2) * PAIR, PAIR)
            cols, value_cols = pl.ds(first, PAIR), pl.ds(width + first, PAIR)
            keep = (lane < HEAD_DIM) if n % 2 == 0 else (lane >= HEAD_DIM)
            v = kv_ref[number, :, value_cols]
            v_ones = jnp.where(keep, v, jnp.ones_like(v))
            s = nt(qm_ref[n % 2, :, cols], kv_ref[number, :, cols])
            if diagonal:
                slot = lax.broadcasted_iota(jnp.int32, s.shape, 1)
                row = lax.broadcasted_iota(jnp.int32, s.shape, 0)
                s = jnp.where(3 * slot + 2 <= 3 * (row % slots) + row // slots, s, -1e30)
            before = m_ref[h]
            after = jnp.maximum(before, jnp.max(s, 1, keepdims=True))
            m_ref[h] = after
            p = jnp.exp(s - jnp.concatenate([after] * (slots // PAIR), 1))
            acc_ref[h] = acc_ref[h] * jnp.exp(before - after) + nn(p.astype(narrow), v_ones)
        return carry

    lax.fori_loop(0, HEADS // 4, heads, 0)


def split_heads(values, out_ref):
    lanes = lax.broadcasted_iota(jnp.int32, (1, values.shape[1]), 1) % PAIR
    nothing = jnp.zeros_like(values)
    out_ref[0] = jnp.where(lanes < HEAD_DIM, values, nothing)
    out_ref[1] = jnp.where(lanes >= HEAD_DIM, values, nothing)


def attend_own_kernel(loads, hid_ref, tk_ref, tv_ref, kv_ref, q_ref, gp_ref, qm_ref, own_ref, m_ref, acc_ref):
    rows, width = hid_ref.shape
    q_low = nn(hid_ref[...], loads[0][...]).astype(narrow)
    q_ref[...] = q_low
    q = q_low.astype(single)
    split_heads((q * scale).astype(narrow), qm_ref)
    own = head_sums(q * tk_ref[...].astype(single)) * scale
    own_ref[...] = own
    own_cols = own.T
    lane = lax.broadcasted_iota(jnp.int32, (1, PAIR), 1)
    for h in range(HEADS):
        keep = (lane < HEAD_DIM) if h % 2 == 0 else (lane >= HEAD_DIM)
        m_ref[h] = jnp.broadcast_to(own_cols[:, h : h + 1], (rows, PAIR))
        acc_ref[h] = jnp.where(keep, tv_ref[:, PAIR * (h // 2) : PAIR * (h // 2 + 1)].astype(single), 1.0)
    attend_block(kv_ref, 0, qm_ref, m_ref, acc_ref, True)
    gp_ref[...] = nn(token_order(rows), loads[1][...]).astype(narrow)


def attend_seen(tab_ref, blocks, kv_refs, qm_ref, m_ref, acc_ref):
    for block, kv_ref in zip(blocks, kv_refs):

        @pl.when(tab_ref[block] == 1)
        def _(kv_ref=kv_ref):
            attend_block(kv_ref, 0, qm_ref, m_ref, acc_ref, False)


def attend_more_kernel(tab_ref, qm_ref, m_in, acc_in, *rest, blocks):
    kv_refs, (m_ref, acc_ref) = rest[:-2], rest[-2:]
    m_ref[...] = m_in[...]
    acc_ref[...] = acc_in[...]
    attend_seen(tab_ref, blocks, kv_refs, qm_ref, m_ref, acc_ref)


def attend_last_kernel(tab_ref, qm_ref, own_ref, m_in, acc_in, *rest, blocks):
    kv_refs, (att_ref, lse_ref, prob_ref, m_ref, acc_ref) = rest[:-5], rest[-5:]
    m_ref[...] = m_in[...]
    acc_ref[...] = acc_in[...]
    attend_seen(tab_ref, blocks, kv_refs, qm_ref, m_ref, acc_ref)
    lane = lax.broadcasted_iota(jnp.int32, (1, PAIR), 1)
    columns = []
    for p in range(HEADS // 2):
        first, second = acc_ref[2 * p], acc_ref[2 * p + 1]
        sums = pltpu.roll(jnp.where(lane < HEAD_DIM, second, first), HEAD_DIM, 1)
        att_ref[:, PAIR * p : PAIR * (p + 1)] = jnp.where(lane < HEAD_DIM, first, second) / sums
        columns.append(m_ref[2 * p][:, :1] + jnp.log(first[:, HEAD_DIM : HEAD_DIM + 1]))
        columns.append(m_ref[2 * p + 1][:, :1] + jnp.log(second[:, :1]))
    lse = jnp.concatenate(columns, 1).T
    lse_ref[...] = lse
    prob_ref[...] = jnp.exp(own_ref[...] - lse)


def gelu_parts(u):
    bell = jnp.exp(-0.5 * (u * u))
    t = 1.0 / (1.0 + (0.3275911 * 0.5**0.5) * jnp.abs(u))
    series = t * (0.127414796 + t * (-0.142248368 + t * (0.7107068705 + t * (-0.7265760135 + t * 0.5307027145))))
    tail = series * bell
    below = jnp.where(u >= 0.0, 1.0 - tail, tail)
    return u * below, below + u * (bell * 0.3989422804014327)


def feed_kernel(loads, tab_ref, x_ref, att_ref, g_ref, wo_ref, *rest, pieces, inverse_at):
    kv_refs = rest[:-11]
    out_ref, mid_ref, gh_ref, keep_ref, send_ref, kv_all, h_s, ht_s, out_s, buf_ref, sems = rest[-11:]
    copies = [
        pltpu.make_async_copy(kv_ref, kv_all.at[pl.ds(i, 1)], sems.at[3 + i]) for i, kv_ref in enumerate(kv_refs)
    ]
    for copy in copies:
        copy.start()
    rows, width = x_ref.shape
    hidden_rows = loads.held[4].shape[0]
    steps = hidden_rows // width
    down_rows = hidden_rows // pieces
    down_tiles = down_rows // TILE
    tiles = down_tiles + steps
    middle = x_ref[...].astype(single) + nn(att_ref[...].astype(narrow), wo_ref[...])
    mid_ref[...] = middle
    unit, _ = standardized(middle)
    h = (unit * loads[0][...] + loads[1][...]).astype(narrow)
    h_s[...] = h
    ht_s[...] = h.T
    g = g_ref[...]
    wu_ref, ub_ref, wd_ref, db_ref = (loads[i] for i in range(2, 6))
    small = buf_ref.shape[0] - 1
    place = lax.broadcasted_iota(jnp.int32, (TILE, width), 0)
    here = pieces // steps
    out_s[...] = middle + db_ref[...]
    gh_ref[...] = jnp.zeros_like(middle)

    def step(i, sums):
        cols = pl.ds(pl.multiple_of(i * width, width), width)
        act, slope = gelu_parts(nn(h_s[...], wu_ref[:, cols]) + ub_ref[:, cols])
        act = act.astype(narrow)
        out_s[...] += nn(act, wd_ref[cols, :])
        gu = (nt(g_ref[...], wd_ref[cols, :]) * slope).astype(narrow)
        gh_ref[...] += nt(gu, wu_ref[:, cols])
        grad_down = tn(act, g_ref[...]).astype(narrow)
        for j in range(here):
            at = tab_ref[inverse_at + i * here + j] * tiles
            store_tiles(buf_ref, at, grad_down[j * down_rows : (j + 1) * down_rows])
        grad_up = nn(ht_s[...], gu).astype(narrow)
        for j in range(pieces):
            buf_ref[tab_ref[inverse_at + j] * tiles + down_tiles + i] = grad_up[j * TILE : (j + 1) * TILE]
        return jnp.where(place == 1 + i, jnp.sum(gu.astype(single), 0, keepdims=True), sums)

    sums = lax.fori_loop(0, steps, step, jnp.zeros((TILE, width), single))
    unit, _ = standardized(mid_ref[...])
    gh = gh_ref[...]
    for row, value in ((0, g.astype(single)), (1 + steps, gh * unit), (2 + steps, gh)):
        sums = jnp.where(place == row, jnp.sum(value, 0, keepdims=True), sums)
    buf_ref[small] = sums.astype(narrow)
    out_ref[...] = out_s[...].astype(narrow)
    split_out(buf_ref, keep_ref, send_ref, sems, 1)
    for copy in copies:
        copy.wait()


def branch_kernel(
    loads, mid_ref, gh_ref, g_ref, att_ref, tv_ref, own_ref, wo_ref, gm_ref, gw_ref, ga_ref, dm_ref, delta_ref, ods_ref
):
    unit, spread = standardized(mid_ref[...])
    gm = g_ref[...].astype(single) + norm_back(gh_ref[...], unit, spread, loads[0][...])
    gm_ref[...] = gm
    branch = gm.astype(narrow)
    att = att_ref[...]
    ga = nt(branch, wo_ref[...]).astype(narrow)
    ga_ref[...] = ga
    split_heads(ga, dm_ref)
    wide = ga.astype(single)
    delta = head_sums(wide * att)
    delta_ref[...] = delta
    dprob = head_sums(wide * tv_ref[...].astype(single))
    ods_ref[...] = (own_ref[...] * (dprob - delta)).astype(narrow)
    gw_ref[...] = tn(att.astype(narrow), branch).astype(narrow)


def reorder_kernel(out_ref, gx_ref, to_out_ref, to_gx_ref):
    order = token_order(out_ref.shape[0])
    to_out_ref[...] = tn(order, out_ref[...]).astype(narrow)
    to_gx_ref[...] = tn(order, gx_ref[...]).astype(narrow)


def back_block(kv_ref, number, pair, qm_ref, dm_ref, lse_ref, delta_ref, diagonal):
    slots, width = kv_ref.shape[1], qm_ref.shape[2]
    cols = slice(PAIR * pair, PAIR * (pair + 1))
    k = kv_ref[number, :, cols]
    v = kv_ref[number, :, width + cols.start : width + cols.stop]
    lane = lax.broadcasted_iota(jnp.int32, (1, PAIR), 1)
    scores, probs = [], []
    for half in range(2):
        h = 2 * pair + half
        prob = jnp.exp(nt(k, qm_ref[half, :, cols]) - lse_ref[h : h + 1, :])
        dprob = nt(v, dm_ref[half, :, cols])
        if diagonal:
            slot = lax.broadcasted_iota(jnp.int32, prob.shape, 0)
            row = lax.broadcasted_iota(jnp.int32, prob.shape, 1)
            prob = jnp.where(3 * slot + 2 <= 3 * (row % slots) + row // slots, prob, 0.0)
        scores.append((prob * (dprob - delta_ref[h : h + 1, :])).astype(narrow))
        probs.append(prob.astype(narrow))
    dk = nn(scores[0], qm_ref[0, :, cols]) + nn(scores[1], qm_ref[1, :, cols])
    dv = nn(probs[0], dm_ref[0, :, cols]) + nn(probs[1], dm_ref[1, :, cols])
    nothing = jnp.zeros_like(k)
    split_k = jnp.concatenate([jnp.where(lane < HEAD_DIM, k, nothing), jnp.where(lane >= HEAD_DIM, k, nothing)], 0)
    return dk, dv, tn(jnp.concatenate(scores, 0), split_k)


def attend_back_kernel(
    tab_ref, qm_ref, dm_ref, lse_ref, delta_ref, kv_ref, dq_ref, keep_ref, send_ref, *, list_at, pair
):
    half, slots, _ = keep_ref.shape

    def store(number, dk, dv):
        @pl.when(number < half)
        def _():
            keep_ref[number, :, :PAIR] = dk
            keep_ref[number, :, PAIR:] = dv

        @pl.when(number >= half)
        def _():
            send_ref[number - half, :, :PAIR] = dk
            send_ref[number - half, :, PAIR:] = dv

    def step(i, carry):
        number = tab_ref[list_at + 1 + i]
        dk, dv, dq = back_block(kv_ref, number, pair, qm_ref, dm_ref, lse_ref, delta_ref, False)
        dq_ref[...] += dq
        store(number, dk.astype(narrow), dv.astype(narrow))
        return carry

    def clear(i, carry):
        nothing = jnp.zeros((slots, PAIR), narrow)
        store(tab_ref[list_at + 1 + i], nothing, nothing)
        return carry

    dq_ref[...] = jnp.zeros(dq_ref.shape, single)
    keep_ref[0] = jnp.zeros((slots, 2 * PAIR), narrow)
    lax.fori_loop(0, tab_ref[list_at], step, 0)
    lax.fori_loop(tab_ref[list_at], 2 * half - 1, clear, 0)


def attend_back_own_kernel(qm_ref, dm_ref, lse_ref, delta_ref, kv_ref, *rest, first):
    dq_in, (dq_ref, out_ref) = rest[:-2], rest[-2:]
    group = out_ref.shape[1] // 2
    for i, ref in enumerate(dq_in):
        dk, dv, dq = back_block(kv_ref, 0, first + i, qm_ref, dm_ref, lse_ref, delta_ref, True)
        cols = slice(PAIR * i, PAIR * (i + 1))
        dq_ref[:, cols] = ref[...] + dq
        out_ref[:, cols] = dk
        out_ref[:, group + PAIR * i : group + PAIR * (i + 1)] = dv


def sum_split_kernel(*refs, count, last):
    total = refs[0][...].astype(single)
    for ref in refs[1:count]:
        total += ref[...].astype(single)
    total = total.astype(narrow)
    outs = refs[count:]
    size = (total.shape[0] - last) // len(outs)
    for i, out_ref in enumerate(outs):
        if i == len(outs) - 1:
            out_ref[...] = total[i * size :]
        else:
            out_ref[pl.ds(0, size)] = total[i * size : (i + 1) * size]
            if last:
                out_ref[pl.ds(size, last)] = total[len(outs) * size :]


def join_kernel(*refs):
    parts, out_ref = refs[:-1], refs[-1]
    size = parts[0].shape[0]
    for i, ref in enumerate(parts):
        out_ref[pl.ds(i * size, size)] = ref[...]


def group_split_kernel(*refs):
    totals, (keep_ref, send_ref) = refs[:-2], refs[-2:]
    pairs = len(totals)
    half = keep_ref.shape[0]
    for pair, ref in enumerate(totals):
        for number in range(2):
            cols = slice(number * PAIR, (number + 1) * PAIR)
            first = (number * pairs + pair) * PAIR
            keep_ref[:, :, first : first + PAIR] = ref[pl.ds(0, half), :, cols]
            send_ref[:, :, first : first + PAIR] = ref[pl.ds(half, half), :, cols]


def store_tiles(buf_ref, first, values):
    for t in range(values.shape[0] // TILE):
        buf_ref[first + t] = values[t * TILE : (t + 1) * TILE]


def split_out(buf_ref, keep_ref, send_ref, sems, last):
    half = (buf_ref.shape[0] - last) // 2
    copies = [
        pltpu.make_async_copy(buf_ref.at[pl.ds(0, half)], keep_ref.at[pl.ds(0, half)], sems.at[0]),
        pltpu.make_async_copy(buf_ref.at[pl.ds(half, half + last)], send_ref, sems.at[1]),
    ]
    if last:
        copies.append(
            pltpu.make_async_copy(buf_ref.at[pl.ds(2 * half, last)], keep_ref.at[pl.ds(half, last)], sems.at[2])
        )
    for copy in copies:
        copy.start()
    for copy in copies:
        copy.wait()


def conv_grads(tab_ref, buf_ref, tk_ref, tv_ref, grad, tiles, pieces, inverse_at):
    width = tk_ref.shape[1]
    slots = grad.shape[0]
    group = grad.shape[1] // 2
    conv_tiles = TAPS * width // pieces // TILE
    for i in range(TAPS):
        own = slice(i * slots, (i + 1) * slots)
        both = jnp.concatenate([tn(tk_ref[own], grad[:, :group]), tn(tv_ref[own], grad[:, group:])], 1).astype(narrow)
        for j in range(width // TILE):
            tile = i * (width // TILE) + j
            at = tab_ref[inverse_at + tile // conv_tiles] * tiles + tile % conv_tiles
            for c in range(2 * group // COLUMNS):
                buf_ref[at + c * conv_tiles] = both[j * TILE : (j + 1) * TILE, c * COLUMNS : (c + 1) * COLUMNS]


def weight_grads(tab_ref, buf_ref, grad, first, tiles, pieces, inverse_at):
    for j in range(pieces):
        at = tab_ref[inverse_at + j] * tiles + first
        for c in range(grad.shape[1] // COLUMNS):
            buf_ref[at + c] = grad[j * TILE : (j + 1) * TILE, c * COLUMNS : (c + 1) * COLUMNS]


def tail_query_kernel(hid_ref, tk_ref, ods_ref, wq_ref, *rest):
    dq_refs, (gh_ref, gw_ref) = rest[:-2], rest[-2:]
    own_ds = tn(ods_ref[...], head_rows(tk_ref.shape[1])) * scale
    dq = jnp.concatenate([ref[...] for ref in dq_refs], 1)
    gq = (dq * scale + own_ds * tk_ref[...].astype(single)).astype(narrow)
    gw_ref[...] = tn(hid_ref[...], gq).astype(narrow)
    gh_ref[...] = nt(gq, wq_ref[...])


def tail_first_kernel(
    tab_ref, tk_ref, tv_ref, first_ref, second_ref, own_ref, gw_out_ref, ck_ref, cv_ref,
    gk_ref, gv_ref, keep_ref, send_ref, buf_ref, sems, *, pieces, inverse_at,
):
    tiles = buf_ref.shape[0] // pieces
    grad = slot_grads(first_ref, second_ref, own_ref)
    conv_grads(tab_ref, buf_ref, tk_ref, tv_ref, grad, tiles, pieces, inverse_at)
    blocks = gw_out_ref.shape[1] // COLUMNS
    weight_grads(tab_ref, buf_ref, gw_out_ref, tiles - blocks, tiles, pieces, inverse_at)
    split_out(buf_ref, keep_ref, send_ref, sems, 0)
    conv_back(grad, ck_ref, cv_ref, 0, gk_ref, gv_ref)


def slot_grads(*refs):
    return sum(ref[...].astype(single) for ref in refs).astype(narrow)


def conv_back(grads, ck_ref, cv_ref, first, gk_ref, gv_ref):
    slots, width = grads.shape[0], ck_ref.shape[1]
    group = grads.shape[1] // 2
    for grad, c_ref, out_ref in ((grads[:, :group], ck_ref, gk_ref), (grads[:, group:], cv_ref, gv_ref)):
        for i in range(TAPS):
            out_ref[i * slots : (i + 1) * slots] = nt(grad, c_ref[i * width : (i + 1) * width, first : first + group])


def tail_kernel(
    tab_ref, x_ref, hid_ref, q_ref, tk_ref, tv_ref, ga_ref, gm_ref, own_ref, ods_ref, gh_ref, gk0_ref, gv0_ref,
    first_ref, second_ref, own_grad_ref, gwq_ref, wk_ref, wv_ref, ck_ref, cv_ref, gain_ref, gx_ref, keep_ref, send_ref, buf_ref, gk_s, gv_s, sems, *, pieces, inverse_at,
):
    rows, width = x_ref.shape
    tiles = (buf_ref.shape[0] - 1) // pieces
    blocks = width // COLUMNS
    grad = slot_grads(first_ref, second_ref, own_grad_ref)
    conv_grads(tab_ref, buf_ref, tk_ref, tv_ref, grad, tiles, pieces, inverse_at)
    marks = head_rows(width)
    own_ds = tn(ods_ref[...], marks) * scale
    own_prob = tn(own_ref[...].astype(narrow), marks)
    conv_back(grad, ck_ref, cv_ref, width - grad.shape[1] // 2, gk_s, gv_s)
    gk = (gk_s[...] + gk0_ref[...] + own_ds * q_ref[...].astype(single)).astype(narrow)
    gv = (gv_s[...] + gv0_ref[...] + own_prob * ga_ref[...].astype(single)).astype(narrow)
    weight_grads(tab_ref, buf_ref, gwq_ref, tiles - 3 * blocks, tiles, pieces, inverse_at)
    hidden_t = hid_ref[...].T
    grad_hidden = gh_ref[...]
    for number, grad in enumerate((gk, gv)):
        grad_w = nn(hidden_t, grad).astype(narrow)
        weight_grads(tab_ref, buf_ref, grad_w, tiles - (2 - number) * blocks, tiles, pieces, inverse_at)
        grad_hidden += nt(grad, (wk_ref, wv_ref)[number][...])
    unit, spread = standardized(x_ref[...].astype(single))
    place = lax.broadcasted_iota(jnp.int32, (TILE, COLUMNS), 0)
    sums = jnp.zeros((TILE, COLUMNS), single)
    for first, value in ((0, grad_hidden * unit), (blocks, grad_hidden)):
        total = jnp.sum(value, 0, keepdims=True)
        for c in range(blocks):
            sums = jnp.where(place == first + c, total[:, c * COLUMNS : (c + 1) * COLUMNS], sums)
    buf_ref[buf_ref.shape[0] - 1] = sums.astype(narrow)
    split_out(buf_ref, keep_ref, send_ref, sems, 1)
    gx_ref[...] = (gm_ref[...] + norm_back(grad_hidden, unit, spread, gain_ref[...])).astype(narrow)


def unpack_feed_kernel(tab_ref, own_ref, other_ref, wd_ref, wu_ref, *, pieces, piece_at):
    width = wd_ref.shape[1]
    down_rows = wd_ref.shape[0] // pieces
    down_tiles, up_tiles = down_rows // TILE, wu_ref.shape[1] // width
    tiles = down_tiles + up_tiles

    for number, buf_ref in enumerate((own_ref, other_ref)):

        def step(k, carry, number=number, buf_ref=buf_ref):
            piece = tab_ref[piece_at + number * pieces // 2 + k]
            at = k * tiles
            for t in range(down_tiles):
                rows = pl.ds(pl.multiple_of(piece * down_rows + t * TILE, TILE), TILE)
                wd_ref[rows, :] = buf_ref[at + t].astype(single)
            mine = pl.ds(pl.multiple_of(piece * TILE, TILE), TILE)
            for t in range(up_tiles):
                wu_ref[mine, t * width : (t + 1) * width] = buf_ref[at + down_tiles + t].astype(single)
            return carry

        lax.fori_loop(0, pieces // 2, step, 0, unroll=4)


def unpack_kernel(tab_ref, *rest, places, first_column, outs):
    bufs, rest = rest[: len(places)], rest[len(places) :]
    out_refs, (conv_s, weight_s, sems) = rest[-outs - 3 : -3], rest[-3:]
    weight_refs, conv_refs = out_refs[:-2], out_refs[-2:]
    conv_rows, columns = conv_s.shape[2], conv_s.shape[3]
    conv_tiles = conv_rows // TILE
    blocks = weight_s.shape[3] // COLUMNS
    weights_at = conv_tiles * (2 * columns // COLUMNS)
    tiles = weights_at + blocks * len(weight_refs)
    copies = []
    for buf_ref, found in zip(bufs, places):
        for k, (number, piece_at) in enumerate(found):
            piece = tab_ref[piece_at]
            for t in range(conv_tiles):
                for unit in range(2 * columns // PAIR):
                    which, first = unit * PAIR // columns, unit * PAIR % columns
                    block, lanes = unit * PAIR // COLUMNS, unit * PAIR % COLUMNS
                    conv_s[number, which, t * TILE : (t + 1) * TILE, first : first + PAIR] = buf_ref[
                        k * tiles + block * conv_tiles + t, :, lanes : lanes + PAIR
                    ].astype(single)
            for t in range(len(weight_refs)):
                for c in range(blocks):
                    weight_s[number, t, :, c * COLUMNS : (c + 1) * COLUMNS] = buf_ref[
                        k * tiles + weights_at + t * blocks + c
                    ].astype(single)
            rows = pl.ds(pl.multiple_of(piece * conv_rows, TILE), conv_rows)
            mine = pl.ds(pl.multiple_of(piece * TILE, TILE), TILE)
            cols = pl.ds(first_column, columns)
            copies += [
                pltpu.make_async_copy(conv_s.at[number, i], ref.at[rows, cols], sems.at[number, i])
                for i, ref in enumerate(conv_refs)
            ]
            copies += [
                pltpu.make_async_copy(weight_s.at[number, i], ref.at[mine], sems.at[number, 2 + i])
                for i, ref in enumerate(weight_refs)
            ]
            for copy in copies[-outs:]:
                copy.start()
    for copy in copies:
        copy.wait()


def shaped(shape, kind):
    return jax.ShapeDtypeStruct(shape, kind)


def per_device(
    seq_size, batch_size,
    inputs, cotangent, ln1_gain, ln1_bias, w_query, w_key, w_value, conv_key, conv_value, w_out,
    ln2_gain, ln2_bias, w_up, up_bias, w_down, down_bias,
):
    x, g = inputs[0], cotangent[0]
    rows, width = x.shape
    slots = rows // TAPS
    ff = w_up.shape[1]
    seq_bits, batch_bits = seq_size.bit_length() - 1, batch_size.bit_length() - 1
    split_bits = min(5, seq_bits + batch_bits)
    pieces = 1 << split_bits
    list_at = seq_size
    piece_at = list_at + seq_size
    inverse_at = piece_at + pieces
    tables = jnp.asarray(plan_tables(seq_size, batch_size, split_bits))
    table = lax.dynamic_index_in_dim(
        tables, lax.axis_index("seq") * batch_size + lax.axis_index("batch"), 0, keepdims=False
    )
    x = tied(x, table)
    row = lambda v: v.reshape(1, -1)
    ck = conv_key.reshape(TAPS * width, width)
    cv = conv_value.reshape(TAPS * width, width)
    token_low, token_wide = shaped((rows, width), narrow), shaped((rows, width), single)
    head_wide, head_low = shaped((HEADS, rows), single), shaped((HEADS, rows), narrow)
    two_low = shaped((2, rows, width), narrow)

    xp, hidden, tk, tv, kv = call(
        "front",
        front_kernel,
        (token_low,) * 4 + (shaped((slots, 2 * width), narrow),),
        loads=(x, row(ln1_gain), row(ln1_bias), w_key, ck, w_value, cv),
        mib=24,
        flops=4e9,
    )

    state = shaped((HEADS, rows, PAIR), single)
    q, gp, qm, own, m, acc = call(
        "attend_own",
        attend_own_kernel,
        (token_low, token_low, two_low, head_wide, state, state),
        loads=(w_query, g),
        operands=(hidden, tk, tv, kv[None]),
        mib=16,
        flops=1e10,
    )
    blocks = {0: kv[None]}
    rounds = gather_plan(seq_size)
    calls = []
    for number, found in enumerate(rounds):
        if number > 0:
            calls.append([entry[0] for entry in rounds[number - 1]])
        held = {source: blocks[source] for _, source, _ in found if source in blocks}
        if number > 1:
            held = tied(held, m)
        for block, source, (axis, pairs) in found:
            if source in held:
                blocks[block] = lax.ppermute(held[source], axis, pairs)
        if number == 0:
            continue
        later = [entry for entry in found if entry[0] not in blocks]
        found = calls[-1]
        m, acc = call(
            f"attend_{found[0]}",
            functools.partial(attend_more_kernel, blocks=found),
            (state, state),
            table=table,
            operands=(qm, m, acc, *[blocks[k] for k in found]),
            mib=8,
            flops=1e10 * len(found),
        )
        for block, source, (axis, pairs) in later:
            blocks[block] = lax.ppermute(tied(blocks[source], m), axis, pairs)
    calls.append([entry[0] for entry in rounds[-1]])
    attended, lse, own_prob = call(
        "attend_last",
        functools.partial(attend_last_kernel, blocks=calls[-1]),
        (token_wide, head_wide, head_wide),
        table=table,
        operands=(qm, own, m, acc, *[blocks[k] for k in calls[-1]]),
        scratch=[pltpu.VMEM(state.shape, single), pltpu.VMEM(state.shape, single)],
        mib=16,
        flops=1e10 * len(calls[-1]),
    )

    steps = ff // width
    tiles = ff // pieces // TILE + steps
    half = shaped((pieces // 2 * tiles + 1, TILE, width), narrow)
    output, middle, grad_normal, keep, send, all_kv = call(
        "feed",
        functools.partial(feed_kernel, pieces=pieces, inverse_at=inverse_at),
        (token_low, token_wide, token_wide, half, half, shaped((seq_size, slots, 2 * width), narrow)),
        loads=(row(ln2_gain), row(ln2_bias), w_up, row(up_bias), w_down, row(down_bias)),
        table=table,
        operands=(xp, attended, gp, w_out),
        away=[blocks[k] for k in range(seq_size)],
        away_outs=3,
        scratch=[
            pltpu.VMEM((rows, width), narrow),
            pltpu.VMEM((width, rows), narrow),
            pltpu.VMEM((rows, width), single),
            pltpu.VMEM((pieces * tiles + 1, TILE, width), narrow),
            pltpu.SemaphoreType.DMA((3 + seq_size,)),
        ],
        mib=30,
        flops=5e10,
    )
    grad_middle, grad_w_out_here, grad_attended, dm, delta, own_ds = call(
        "branch",
        branch_kernel,
        (token_wide, shaped((width, width), narrow), token_low, two_low, head_wide, head_low),
        loads=(row(ln2_gain),),
        operands=(middle, grad_normal, gp, attended, tv, own_prob, w_out),
        mib=16,
        flops=3e10,
    )

    stages = reduce_stages(seq_size, batch_size, split_bits)
    gather_back = [stage for stage in stages if stage[0] > 1][::-1]
    unseen = gather_stages(seq_size)[::-1]
    head_pairs = HEADS // 2

    wide_grant = 12 if seq_size <= 8 else 56
    share = shaped((seq_size // 2, slots, 2 * PAIR), narrow)

    def back(pair, qm):
        return call(
            f"attend_back_{pair}",
            functools.partial(attend_back_kernel, list_at=list_at, pair=pair),
            (shaped((rows, PAIR), single), share, share),
            table=table,
            operands=(qm, dm, lse, delta, all_kv),
            mib=wide_grant,
            flops=3e10,
        )

    def small_call(kernel, name, outs, *operands):
        return call(name, kernel, outs, operands=operands, mib=4, flops=sum(v.size for v in operands) * 600)

    def sum_split(buffers, last, cut):
        count, rest = buffers[0].shape[0], buffers[0].shape[1:]
        outs = (shaped(((count - last) // cut + last, *rest), narrow),) * cut
        kernel = functools.partial(sum_split_kernel, count=len(buffers), last=last)
        return small_call(kernel, "sum_split", outs, *buffers)

    def join(*parts):
        out = shaped((len(parts) * parts[0].shape[0], *parts[0].shape[1:]), narrow)
        return small_call(join_kernel, "join", (out,), *parts)[0]

    def exchange(stage, parts):
        return [lax.ppermute(part, stage[1], pairs) for part, pairs in zip(parts, stage[2])]

    class Sum:
        def __init__(self, keep, send, last):
            self.keep, self.last, self.at = keep, last, 0
            self.arrived = exchange(stages[0], [send])

        def step(self, *others):
            arrived = tied(self.arrived, *others)
            self.at += 1
            if self.at < len(stages):
                cut = stages[self.at][0]
                parts = sum_split((self.keep, *arrived), self.last, cut)
                self.keep, sent = parts[0], parts[1:] if cut > 1 else parts
                self.arrived = exchange(stages[self.at], sent)
                return sent[0]
            if self.at == len(stages):
                (total,) = sum_split((self.keep, *arrived), self.last, 1)
                self.small = total[-1].astype(single)
                self.held = total[:-1] if self.last else total
            else:
                self.held = join(self.held, *arrived)
            stage = gather_back[self.at - len(stages)]
            self.arrived = exchange(stage, [self.held] * len(stage[2]))
            return self.held

        def left(self):
            return len(stages) + len(gather_back) - 1 - self.at

    class Group:
        def __init__(self):
            self.shares, self.at = [], 0

        def step(self, *others):
            self.at += 1
            if self.at == 1:
                operands = tied(self.shares, *others)
                half = shaped((seq_size // 4, slots, len(self.shares) * 2 * PAIR), narrow)
                self.keep, send = small_call(group_split_kernel, "group_split", (half, half), *operands)
            else:
                self.keep, send = sum_split((self.keep, tied(self.arrived, *others)), 0, 2)
            self.arrived = lax.ppermute(send, *unseen[self.at])
            return send

        def left(self):
            return len(unseen) - 1 - self.at

    conv_tiles = TAPS * width // pieces // TILE
    blocks_wide = width // COLUMNS
    first_tiles, tail_tiles = (
        conv_tiles * (group * 2 * PAIR // COLUMNS) + count * blocks_wide for group, count in zip(GROUPS, (1, 3))
    )

    sums = {"feed": Sum(keep, send, 1)}
    first_group, second_group = Group(), Group()
    waits = [sums["feed"].step(delta)]
    state_back = {"grads": []}

    def advance(name, kept=0):
        if name in sums and sums[name].left() > kept:
            waits.append(sums[name].step(*waits))

    def advance_group(group):
        if group.left() > 0:
            waits.append(group.step(*waits))

    def first_convs():
        half = shaped((pieces // 2 * first_tiles, TILE, COLUMNS), narrow)
        while first_group.left() > 0:
            advance_group(first_group)
        grad_k, grad_v, keep0, send0 = call(
            "tail_first",
            functools.partial(tail_first_kernel, pieces=pieces, inverse_at=inverse_at),
            (token_wide, token_wide, half, half),
            table=table,
            operands=(
                tk, tv, tied(first_group.keep[0], *waits), first_group.arrived[0], first_own, grad_w_out_here, ck, cv,
            ),
            away_outs=2,
            scratch=[pltpu.VMEM((pieces * first_tiles, TILE, COLUMNS), narrow), pltpu.SemaphoreType.DMA((3,))],
            mib=20,
            flops=1.5e10,
        )
        sums["first"] = Sum(keep0, send0, 0)
        waits.append(grad_k)
        return grad_k, grad_v

    def add_share(group, kept, arrived):
        (total,) = sum_split(tied((kept, arrived), *waits), 0, 1)
        waits.append(total)
        group.shares.append(total)

    partial_q, pending = [], None
    for pair in range(head_pairs):
        in_first = pair < GROUPS[0]
        grads, kept, sent = back(pair, tied(qm, *waits))
        waits = [grads]
        partial_q.append(grads)
        if pair < head_pairs - 1:
            advance("feed", 1)
        if pending is not None:
            add_share(*pending)
        pending = (first_group if in_first else second_group, kept, lax.ppermute(sent, *unseen[0]))
        if pair >= GROUPS[0]:
            advance_group(first_group)
    def own_block(first, count):
        return call(
            f"attend_back_own_{first}",
            functools.partial(attend_back_own_kernel, first=first),
            (shaped((rows, count * PAIR), single), shaped((slots, count * 2 * PAIR), single)),
            operands=(tied(qm, *waits), dm, lse, delta, kv[None], *partial_q[first : first + count]),
            mib=12,
            flops=1e10,
        )

    later_q, second_own = own_block(GROUPS[0], GROUPS[1])
    waits = [later_q]
    add_share(*pending)
    advance_group(second_group)
    advance("feed", 1)
    early_q, first_own = own_block(0, GROUPS[0])
    waits = [early_q]
    grad_k, grad_v = first_convs()
    grad_hidden, grad_wq_here = call(
        "tail_query",
        tail_query_kernel,
        (token_wide, shaped((width, width), narrow)),
        operands=(tied(hidden, *waits), tk, own_ds, w_query, early_q, later_q),
        mib=16,
        flops=5e9,
    )
    waits = [grad_hidden]
    while second_group.left() > 0:
        advance_group(second_group)
    advance("feed", 1)
    half = shaped((pieces // 2 * tail_tiles + 1, TILE, COLUMNS), narrow)
    grad_x, keep1, send1 = call(
        "tail",
        functools.partial(tail_kernel, pieces=pieces, inverse_at=inverse_at),
        (token_low, half, half),
        table=table,
        operands=(
            xp, hidden, q, tk, tv, grad_attended, grad_middle, own_prob, own_ds, grad_hidden, grad_k, grad_v,
            tied(second_group.keep[0], *waits), second_group.arrived[0], second_own, grad_wq_here,
            w_key, w_value, ck, cv, row(ln1_gain),
        ),
        away_outs=2,
        scratch=[
            pltpu.VMEM((pieces * tail_tiles + 1, TILE, COLUMNS), narrow),
            pltpu.VMEM((rows, width), single),
            pltpu.VMEM((rows, width), single),
            pltpu.SemaphoreType.DMA((3,)),
        ],
        mib=26,
        flops=3e10,
    )
    sums["second"] = Sum(keep1, send1, 1)
    waits = [grad_x]

    def unpack(name, places, heads, weights, bufs, *known):
        count = sum(len(found) for found in places)
        outs = [shaped((width, width), single)] * weights + [shaped(ck.shape, single)] * 2
        numbered, at = [], 0
        for found in places:
            numbered.append([(at + i, piece_at + k) for i, k in enumerate(found)])
            at += len(found)
        return call(
            name,
            functools.partial(unpack_kernel, places=numbered, first_column=heads[0] * PAIR, outs=len(outs)),
            outs,
            table=table,
            operands=bufs,
            away=known,
            away_outs=len(outs),
            in_place=len(known),
            scratch=[
                pltpu.VMEM((count, 2, conv_tiles * TILE, heads[1] * PAIR), single),
                pltpu.VMEM((count, len(outs) - 2, TILE, width), single),
                pltpu.SemaphoreType.DMA((count, len(outs))),
            ],
            mib=20,
            flops=1.5e10,
        )

    half_places, other_places = list(range(pieces // 2)), list(range(pieces // 2, pieces))
    def finish_feed(*others):
        grads = call(
            "unpack_feed",
            functools.partial(unpack_feed_kernel, pieces=pieces, piece_at=piece_at),
            (shaped((ff, width), single), shaped((width, ff), single)),
            table=table,
            operands=(sums["feed"].held, tied(sums["feed"].arrived[0], *others)),
            mib=16,
            flops=2e10,
        )
        small = sums["feed"].small
        small = (small[1 + steps], small[2 + steps], small[1 : 1 + steps].reshape(ff), small[0])
        return (*grads, *small)

    places = (GROUPS[0], GROUPS[1])
    for action in "0R1F00101F01F0101F01U1u1":
        if action in "01F":
            advance({"0": "first", "1": "second", "F": "feed"}[action])
            waits = waits[-1:]
        elif action == "R":
            output, grad_x = call(
                "reorder",
                reorder_kernel,
                (token_low, token_low),
                operands=(output, tied(grad_x, *waits)),
                mib=8,
                flops=1e10,
            )
            waits.append(grad_x)
        elif action == "U":
            while sums["feed"].left() > 0:
                advance("feed")
            grad_w_down, grad_w_up, *small_feed = finish_feed(*waits)
            waits.append(grad_w_up)
        elif action == "u":
            while sums["first"].left() > 0:
                advance("first")
            while sums["second"].left() > 1:
                advance("second")
            small_tail = sums["second"].small[: 2 * blocks_wide].reshape(2, width)
            waits.append(small_tail)
            grad_w_out, *convs = unpack(
                "unpack_first",
                [half_places, other_places],
                (0, GROUPS[0]),
                1,
                (sums["first"].held, tied(sums["first"].arrived[0], *waits)),
            )
            waits.append(grad_w_out)
    last = sums["second"]
    found = unpack("unpack_own", [half_places], places, 3, (last.held,), *tied(convs, *waits))
    grad_wq, grad_wk, grad_wv, grad_ck, grad_cv = unpack(
        "unpack_last", [other_places], places, 3, (last.arrived[0],), *found
    )
    return (
        output[None],
        grad_x[None],
        small_tail[0],
        small_tail[1],
        grad_wq,
        grad_wk,
        grad_wv,
        grad_ck.reshape(conv_key.shape),
        grad_cv.reshape(conv_value.shape),
        grad_w_out,
        small_feed[0],
        small_feed[1],
        grad_w_up,
        small_feed[2],
        grad_w_down,
        small_feed[3],
    )


def solution(mesh):
    placed = (P("batch", "seq", None),) * 2 + (P(),) * 14
    return jax.shard_map(
        functools.partial(per_device, mesh.shape["seq"], mesh.shape["batch"]),
        mesh=mesh,
        in_specs=placed,
        out_specs=placed,
        check_vma=False,
    )
```

```python
import functools

import jax
import jax.numpy as jnp
import numpy as np
from jax import lax
from jax.experimental import pallas as pl
from jax.experimental.pallas import tpu as pltpu
from jax.sharding import PartitionSpec as P

HEADS = 8
HEAD_DIM = 64
PAIR = 2 * HEAD_DIM
TAPS = 3
TILE = 16
COLUMNS = 512
GROUPS = (2, 2)

epsilon = 1e-05
narrow = jnp.bfloat16
single = jnp.float32
scale = HEAD_DIM ** (-0.5)

vmem = pl.BlockSpec(memory_space=pltpu.VMEM)
smem = pl.BlockSpec(memory_space=pltpu.SMEM)
anywhere = pl.BlockSpec(memory_space=pl.ANY)
hbm = pl.BlockSpec(memory_space=pltpu.HBM)


def params(mib):
    return pltpu.CompilerParams(vmem_limit_bytes=mib * 2**20)


def cost(flops, moved):
    return pl.CostEstimate(flops=int(flops), bytes_accessed=int(moved), transcendentals=0)


class Loads:
    def __init__(self, sources, held, sems):
        self.held, self.waited = held, set()
        self.copies = [pltpu.make_async_copy(a, b, sems.at[i]) for i, (a, b) in enumerate(zip(sources, held))]
        for copy in self.copies:
            copy.start()

    def __getitem__(self, i):
        if i not in self.waited:
            self.copies[i].wait()
            self.waited.add(i)
        return self.held[i]


def call(
    name, body, outs, *, loads=(), table=None, operands=(), away=(), away_outs=0, in_place=0, scratch=(), mib, flops
):
    count = len(loads)
    inputs = count + (table is not None) + len(operands) + len(away)

    def kernel(*refs):
        sources, rest = refs[:count], refs[count:]
        if count == 0:
            return body(*rest)
        held, sems = rest[-count - 1 : -1], rest[-1]
        return body(Loads(sources, held, sems), *rest[: -count - 1])

    moved = sum(v.size * 2 for v in (*loads, *operands, *away, *outs))
    scratch = list(scratch)
    if count:
        scratch += [pltpu.VMEM(v.shape, v.dtype) for v in loads] + [pltpu.SemaphoreType.DMA((count,))]
    return pl.pallas_call(
        kernel,
        out_shape=tuple(outs),
        in_specs=[hbm] * count + [smem] * (table is not None) + [vmem] * len(operands) + [anywhere] * len(away),
        out_specs=(vmem,) * (len(outs) - away_outs) + (anywhere,) * away_outs,
        scratch_shapes=scratch,
        input_output_aliases={inputs - in_place + i: len(outs) - in_place + i for i in range(in_place)},
        compiler_params=params(mib),
        cost_estimate=cost(flops, moved),
        name=name,
    )(
        *[pltpu.with_memory_space_constraint(v, pltpu.HBM) for v in loads],
        *([] if table is None else [table]),
        *operands,
        *away,
    )


def tied(values, *others):
    return lax.optimization_barrier((values, others))[0]


def nn(a, b):
    return lax.dot_general(a, b, (((1,), (0,)), ((), ())), preferred_element_type=single)


def nt(a, b):
    return lax.dot_general(a, b, (((1,), (1,)), ((), ())), preferred_element_type=single)


def tn(a, b):
    return lax.dot_general(a, b, (((0,), (0,)), ((), ())), preferred_element_type=single)


def bit_masks(size):
    return [1 << b for b in range(size.bit_length() - 1)]


def seq_masks(size, core):
    masks = bit_masks(size)[1:]
    return masks if core == 0 else masks[::-1]


def seq_swap(size, stage):
    return [(i, i ^ seq_masks(size, i & 1)[stage]) for i in range(size)]


def gather_stages(seq_size):
    found = [("seq", seq_swap(seq_size, j)) for j in range(len(bit_masks(seq_size)) - 1)]
    return found + [("seq", [(i, i ^ 1) for i in range(seq_size)])]


def reduce_stages(seq_size, batch_size, split_bits):
    found = [(2, "seq", [[(i, i ^ 1) for i in range(seq_size)]])]
    found += [(2, "seq", [seq_swap(seq_size, j)]) for j in range(len(bit_masks(seq_size)) - 1)]
    split = split_bits - len(found)
    for j, mask in enumerate(bit_masks(batch_size)):
        found.append((2 if j < split else 1, "batch", [[(i, i ^ mask) for i in range(batch_size)]]))
    return found


def gather_origin(seq_size, me, block):
    count = len(bit_masks(seq_size)) - 1
    core_bit = (block >> count) & 1
    other = me ^ core_bit
    masks = seq_masks(seq_size, other & 1)
    for j in range(count):
        if (block >> j) & 1:
            other ^= masks[j]
    return other


def piece_of(seq_size, batch_size, split_bits, me_seq, me_batch, place):
    bits = [(place >> (split_bits - 1 - j)) & 1 for j in range(split_bits)]
    s = me_seq ^ bits[0]
    masks = seq_masks(seq_size, s & 1)
    z = me_batch
    for j, b in enumerate(bits[1:]):
        if j < len(masks):
            s ^= masks[j] * b
        else:
            z ^= (1 << (j - len(masks))) * b
    low_batch = z & ((1 << (split_bits - len(bit_masks(seq_size)))) - 1)
    return s + seq_size * low_batch


def gather_plan(seq_size):
    stages = gather_stages(seq_size)
    count = len(stages) - 1
    rounds = [[] for _ in range(count + 1)]
    for block in range(1, 1 << count):
        last = block.bit_length() - 1
        rounds[bin(block).count("1")].append((block, block ^ (1 << last), stages[last]))
    for found in rounds:
        blocks = [entry[0] for entry in found] or [0]
        found += [(block | (1 << count), block, stages[-1]) for block in blocks]
    return rounds


def plan_tables(seq_size, batch_size, split_bits):
    rows = []
    pieces = 1 << split_bits
    for s in range(seq_size):
        origins = [gather_origin(seq_size, s, k) for k in range(seq_size)]
        seen = [int(origin < s) for origin in origins]
        visible = [k for k in range(seq_size) if origins[k] < s]
        lists = [len(visible)] + visible + [k for k in range(seq_size) if origins[k] > s]
        for z in range(batch_size):
            places = [piece_of(seq_size, batch_size, split_bits, s, z, k) for k in range(pieces)]
            inverse = [places.index(p) for p in range(pieces)]
            rows.append(seen + lists + places + inverse)
    return np.asarray(rows, np.int32)


def token_order(rows):
    slots = rows // TAPS
    r = lax.broadcasted_iota(jnp.int32, (rows, rows), 0)
    c = lax.broadcasted_iota(jnp.int32, (rows, rows), 1)
    return jnp.where(c == TAPS * (r % slots) + r // slots, 1.0, 0.0).astype(narrow)


def head_rows(width):
    r = lax.broadcasted_iota(jnp.int32, (HEADS, width), 0)
    c = lax.broadcasted_iota(jnp.int32, (HEADS, width), 1)
    return jnp.where(c // HEAD_DIM == r, 1.0, 0.0).astype(narrow)


def head_sums(values):
    marks = head_rows(values.shape[1])
    high = values.astype(narrow)
    rest = values - high.astype(single)
    middle = rest.astype(narrow)
    low = (rest - middle.astype(single)).astype(narrow)
    return nt(marks, high) + nt(marks, middle) + nt(marks, low)


def standardized(values):
    centred = values - jnp.mean(values, -1, keepdims=True)
    spread = lax.rsqrt(jnp.mean(centred * centred, -1, keepdims=True) + epsilon)
    return centred * spread, spread


def norm_back(grad, unit, spread, gain):
    inner = grad * gain
    return spread * (
        inner
        - jnp.mean(inner, -1, keepdims=True)
        - unit * jnp.mean(inner * unit, -1, keepdims=True)
    )


def front_kernel(loads, xp_ref, hid_ref, tk_ref, tv_ref, kv_ref):
    rows, width = xp_ref.shape
    slots = rows // TAPS
    order = token_order(rows)
    x = nn(order, loads[0][...])
    xp_ref[...] = x.astype(narrow)
    unit, _ = standardized(x)
    hidden = (unit * loads[1][...] + loads[2][...]).astype(narrow)
    hid_ref[...] = hidden
    for number, t_ref in enumerate((tk_ref, tv_ref)):
        t = nn(hidden, loads[3 + 2 * number][...]).astype(narrow)
        t_ref[...] = t
        c_ref = loads[4 + 2 * number]
        total = nn(t[:slots], c_ref[:width])
        for i in range(1, TAPS):
            total += nn(t[i * slots : (i + 1) * slots], c_ref[i * width : (i + 1) * width])
        kv_ref[:, number * width : (number + 1) * width] = total.astype(narrow)


def attend_block(kv_ref, number, qm_ref, m_ref, acc_ref, diagonal):
    slots, width = kv_ref.shape[1], qm_ref.shape[2]
    lane = lax.broadcasted_iota(jnp.int32, (1, PAIR), 1)

    def heads(i, carry):
        for n in range(4):
            h = 4 * i + n
            first = pl.multiple_of((h // 2) * PAIR, PAIR)
            cols, value_cols = pl.ds(first, PAIR), pl.ds(width + first, PAIR)
            keep = (lane < HEAD_DIM) if n % 2 == 0 else (lane >= HEAD_DIM)
            v = kv_ref[number, :, value_cols]
            v_ones = jnp.where(keep, v, jnp.ones_like(v))
            s = nt(qm_ref[n % 2, :, cols], kv_ref[number, :, cols])
            if diagonal:
                slot = lax.broadcasted_iota(jnp.int32, s.shape, 1)
                row = lax.broadcasted_iota(jnp.int32, s.shape, 0)
                s = jnp.where(3 * slot + 2 <= 3 * (row % slots) + row // slots, s, -1e30)
            before = m_ref[h]
            after = jnp.maximum(before, jnp.max(s, 1, keepdims=True))
            m_ref[h] = after
            p = jnp.exp(s - jnp.concatenate([after] * (slots // PAIR), 1))
            acc_ref[h] = acc_ref[h] * jnp.exp(before - after) + nn(p.astype(narrow), v_ones)
        return carry

    lax.fori_loop(0, HEADS // 4, heads, 0)


def split_heads(values, out_ref):
    lanes = lax.broadcasted_iota(jnp.int32, (1, values.shape[1]), 1) % PAIR
    nothing = jnp.zeros_like(values)
    out_ref[0] = jnp.where(lanes < HEAD_DIM, values, nothing)
    out_ref[1] = jnp.where(lanes >= HEAD_DIM, values, nothing)


def attend_own_kernel(loads, hid_ref, tk_ref, tv_ref, kv_ref, q_ref, gp_ref, qm_ref, own_ref, m_ref, acc_ref):
    rows, width = hid_ref.shape
    q_low = nn(hid_ref[...], loads[0][...]).astype(narrow)
    q_ref[...] = q_low
    q = q_low.astype(single)
    split_heads((q * scale).astype(narrow), qm_ref)
    own = head_sums(q * tk_ref[...].astype(single)) * scale
    own_ref[...] = own
    own_cols = own.T
    lane = lax.broadcasted_iota(jnp.int32, (1, PAIR), 1)
    for h in range(HEADS):
        keep = (lane < HEAD_DIM) if h % 2 == 0 else (lane >= HEAD_DIM)
        m_ref[h] = jnp.broadcast_to(own_cols[:, h : h + 1], (rows, PAIR))
        acc_ref[h] = jnp.where(keep, tv_ref[:, PAIR * (h // 2) : PAIR * (h // 2 + 1)].astype(single), 1.0)
    attend_block(kv_ref, 0, qm_ref, m_ref, acc_ref, True)
    gp_ref[...] = nn(token_order(rows), loads[1][...]).astype(narrow)


def attend_seen(tab_ref, blocks, kv_refs, qm_ref, m_ref, acc_ref):
    for block, kv_ref in zip(blocks, kv_refs):

        @pl.when(tab_ref[block] == 1)
        def _(kv_ref=kv_ref):
            attend_block(kv_ref, 0, qm_ref, m_ref, acc_ref, False)


def attend_more_kernel(tab_ref, qm_ref, m_in, acc_in, *rest, blocks):
    kv_refs, (m_ref, acc_ref) = rest[:-2], rest[-2:]
    m_ref[...] = m_in[...]
    acc_ref[...] = acc_in[...]
    attend_seen(tab_ref, blocks, kv_refs, qm_ref, m_ref, acc_ref)


def attend_last_kernel(tab_ref, qm_ref, own_ref, m_in, acc_in, *rest, blocks):
    kv_refs, (att_ref, lse_ref, prob_ref, m_ref, acc_ref) = rest[:-5], rest[-5:]
    m_ref[...] = m_in[...]
    acc_ref[...] = acc_in[...]
    attend_seen(tab_ref, blocks, kv_refs, qm_ref, m_ref, acc_ref)
    lane = lax.broadcasted_iota(jnp.int32, (1, PAIR), 1)
    columns = []
    for p in range(HEADS // 2):
        first, second = acc_ref[2 * p], acc_ref[2 * p + 1]
        sums = pltpu.roll(jnp.where(lane < HEAD_DIM, second, first), HEAD_DIM, 1)
        att_ref[:, PAIR * p : PAIR * (p + 1)] = jnp.where(lane < HEAD_DIM, first, second) / sums
        columns.append(m_ref[2 * p][:, :1] + jnp.log(first[:, HEAD_DIM : HEAD_DIM + 1]))
        columns.append(m_ref[2 * p + 1][:, :1] + jnp.log(second[:, :1]))
    lse = jnp.concatenate(columns, 1).T
    lse_ref[...] = lse
    prob_ref[...] = jnp.exp(own_ref[...] - lse)


def gelu_parts(u):
    bell = jnp.exp(-0.5 * (u * u))
    t = 1.0 / (1.0 + (0.3275911 * 0.5**0.5) * jnp.abs(u))
    series = t * (0.127414796 + t * (-0.142248368 + t * (0.7107068705 + t * (-0.7265760135 + t * 0.5307027145))))
    tail = series * bell
    below = jnp.where(u >= 0.0, 1.0 - tail, tail)
    return u * below, below + u * (bell * 0.3989422804014327)


def feed_kernel(loads, tab_ref, x_ref, att_ref, g_ref, wo_ref, *rest, pieces, inverse_at):
    kv_refs = rest[:-11]
    out_ref, mid_ref, gh_ref, keep_ref, send_ref, kv_all, h_s, ht_s, out_s, buf_ref, sems = rest[-11:]
    copies = [
        pltpu.make_async_copy(kv_ref, kv_all.at[pl.ds(i, 1)], sems.at[3 + i]) for i, kv_ref in enumerate(kv_refs)
    ]
    for copy in copies:
        copy.start()
    rows, width = x_ref.shape
    hidden_rows = loads.held[4].shape[0]
    steps = hidden_rows // width
    down_rows = hidden_rows // pieces
    down_tiles = down_rows // TILE
    tiles = down_tiles + steps
    middle = x_ref[...].astype(single) + nn(att_ref[...].astype(narrow), wo_ref[...])
    mid_ref[...] = middle
    unit, _ = standardized(middle)
    h = (unit * loads[0][...] + loads[1][...]).astype(narrow)
    h_s[...] = h
    ht_s[...] = h.T
    g = g_ref[...]
    wu_ref, ub_ref, wd_ref, db_ref = (loads[i] for i in range(2, 6))
    small = buf_ref.shape[0] - 1
    place = lax.broadcasted_iota(jnp.int32, (TILE, width), 0)
    here = pieces // steps
    out_s[...] = middle + db_ref[...]
    gh_ref[...] = jnp.zeros_like(middle)

    def step(i, sums):
        cols = pl.ds(pl.multiple_of(i * width, width), width)
        act, slope = gelu_parts(nn(h_s[...], wu_ref[:, cols]) + ub_ref[:, cols])
        act = act.astype(narrow)
        out_s[...] += nn(act, wd_ref[cols, :])
        gu = (nt(g_ref[...], wd_ref[cols, :]) * slope).astype(narrow)
        gh_ref[...] += nt(gu, wu_ref[:, cols])
        grad_down = tn(act, g_ref[...]).astype(narrow)
        for j in range(here):
            at = tab_ref[inverse_at + i * here + j] * tiles
            store_tiles(buf_ref, at, grad_down[j * down_rows : (j + 1) * down_rows])
        grad_up = nn(ht_s[...], gu).astype(narrow)
        for j in range(pieces):
            buf_ref[tab_ref[inverse_at + j] * tiles + down_tiles + i] = grad_up[j * TILE : (j + 1) * TILE]
        return jnp.where(place == 1 + i, jnp.sum(gu.astype(single), 0, keepdims=True), sums)

    sums = lax.fori_loop(0, steps, step, jnp.zeros((TILE, width), single))
    unit, _ = standardized(mid_ref[...])
    gh = gh_ref[...]
    for row, value in ((0, g.astype(single)), (1 + steps, gh * unit), (2 + steps, gh)):
        sums = jnp.where(place == row, jnp.sum(value, 0, keepdims=True), sums)
    buf_ref[small] = sums.astype(narrow)
    out_ref[...] = out_s[...].astype(narrow)
    split_out(buf_ref, keep_ref, send_ref, sems, 1)
    for copy in copies:
        copy.wait()


def branch_kernel(
    loads, mid_ref, gh_ref, g_ref, att_ref, tv_ref, own_ref, wo_ref, gm_ref, gw_ref, ga_ref, dm_ref, delta_ref, ods_ref
):
    unit, spread = standardized(mid_ref[...])
    gm = g_ref[...].astype(single) + norm_back(gh_ref[...], unit, spread, loads[0][...])
    gm_ref[...] = gm
    branch = gm.astype(narrow)
    att = att_ref[...]
    ga = nt(branch, wo_ref[...]).astype(narrow)
    ga_ref[...] = ga
    split_heads(ga, dm_ref)
    wide = ga.astype(single)
    delta = head_sums(wide * att)
    delta_ref[...] = delta
    dprob = head_sums(wide * tv_ref[...].astype(single))
    ods_ref[...] = (own_ref[...] * (dprob - delta)).astype(narrow)
    gw_ref[...] = tn(att.astype(narrow), branch).astype(narrow)


def reorder_kernel(out_ref, gx_ref, to_out_ref, to_gx_ref):
    order = token_order(out_ref.shape[0])
    to_out_ref[...] = tn(order, out_ref[...]).astype(narrow)
    to_gx_ref[...] = tn(order, gx_ref[...]).astype(narrow)


def back_block(kv_ref, number, pair, qm_ref, dm_ref, lse_ref, delta_ref, diagonal):
    slots, width = kv_ref.shape[1], qm_ref.shape[2]
    cols = slice(PAIR * pair, PAIR * (pair + 1))
    k = kv_ref[number, :, cols]
    v = kv_ref[number, :, width + cols.start : width + cols.stop]
    lane = lax.broadcasted_iota(jnp.int32, (1, PAIR), 1)
    scores, probs = [], []
    for half in range(2):
        h = 2 * pair + half
        prob = jnp.exp(nt(k, qm_ref[half, :, cols]) - lse_ref[h : h + 1, :])
        dprob = nt(v, dm_ref[half, :, cols])
        if diagonal:
            slot = lax.broadcasted_iota(jnp.int32, prob.shape, 0)
            row = lax.broadcasted_iota(jnp.int32, prob.shape, 1)
            prob = jnp.where(3 * slot + 2 <= 3 * (row % slots) + row // slots, prob, 0.0)
        scores.append((prob * (dprob - delta_ref[h : h + 1, :])).astype(narrow))
        probs.append(prob.astype(narrow))
    dk = nn(scores[0], qm_ref[0, :, cols]) + nn(scores[1], qm_ref[1, :, cols])
    dv = nn(probs[0], dm_ref[0, :, cols]) + nn(probs[1], dm_ref[1, :, cols])
    nothing = jnp.zeros_like(k)
    split_k = jnp.concatenate([jnp.where(lane < HEAD_DIM, k, nothing), jnp.where(lane >= HEAD_DIM, k, nothing)], 0)
    return dk, dv, tn(jnp.concatenate(scores, 0), split_k)


def attend_back_kernel(
    tab_ref, qm_ref, dm_ref, lse_ref, delta_ref, kv_ref, dq_ref, keep_ref, send_ref, *, list_at, pair
):
    half, slots, _ = keep_ref.shape

    def store(number, dk, dv):
        @pl.when(number < half)
        def _():
            keep_ref[number, :, :PAIR] = dk
            keep_ref[number, :, PAIR:] = dv

        @pl.when(number >= half)
        def _():
            send_ref[number - half, :, :PAIR] = dk
            send_ref[number - half, :, PAIR:] = dv

    def step(i, carry):
        number = tab_ref[list_at + 1 + i]
        dk, dv, dq = back_block(kv_ref, number, pair, qm_ref, dm_ref, lse_ref, delta_ref, False)
        dq_ref[...] += dq
        store(number, dk.astype(narrow), dv.astype(narrow))
        return carry

    def clear(i, carry):
        nothing = jnp.zeros((slots, PAIR), narrow)
        store(tab_ref[list_at + 1 + i], nothing, nothing)
        return carry

    dq_ref[...] = jnp.zeros(dq_ref.shape, single)
    keep_ref[0] = jnp.zeros((slots, 2 * PAIR), narrow)
    lax.fori_loop(0, tab_ref[list_at], step, 0)
    lax.fori_loop(tab_ref[list_at], 2 * half - 1, clear, 0)


def attend_back_own_kernel(qm_ref, dm_ref, lse_ref, delta_ref, kv_ref, *rest, first):
    dq_in, (dq_ref, out_ref) = rest[:-2], rest[-2:]
    group = out_ref.shape[1] // 2
    for i, ref in enumerate(dq_in):
        dk, dv, dq = back_block(kv_ref, 0, first + i, qm_ref, dm_ref, lse_ref, delta_ref, True)
        cols = slice(PAIR * i, PAIR * (i + 1))
        dq_ref[:, cols] = ref[...] + dq
        out_ref[:, cols] = dk
        out_ref[:, group + PAIR * i : group + PAIR * (i + 1)] = dv


def sum_split_kernel(*refs, count, last):
    total = refs[0][...].astype(single)
    for ref in refs[1:count]:
        total += ref[...].astype(single)
    total = total.astype(narrow)
    outs = refs[count:]
    size = (total.shape[0] - last) // len(outs)
    for i, out_ref in enumerate(outs):
        if i == len(outs) - 1:
            out_ref[...] = total[i * size :]
        else:
            out_ref[pl.ds(0, size)] = total[i * size : (i + 1) * size]
            if last:
                out_ref[pl.ds(size, last)] = total[len(outs) * size :]


def sum_last_kernel(*refs, count, last):
    total = refs[0][...].astype(single)
    for ref in refs[1:count]:
        total += ref[...].astype(single)
    size = total.shape[0] - last
    refs[count][...] = total[:size].astype(narrow)
    refs[count + 1][...] = total[size:]


def join_kernel(*refs):
    parts, out_ref = refs[:-1], refs[-1]
    size = parts[0].shape[0]
    for i, ref in enumerate(parts):
        out_ref[pl.ds(i * size, size)] = ref[...]


def group_split_kernel(*refs):
    totals, (keep_ref, send_ref) = refs[:-2], refs[-2:]
    pairs = len(totals)
    half = keep_ref.shape[0]
    for pair, ref in enumerate(totals):
        for number in range(2):
            cols = slice(number * PAIR, (number + 1) * PAIR)
            first = (number * pairs + pair) * PAIR
            keep_ref[:, :, first : first + PAIR] = ref[pl.ds(0, half), :, cols]
            send_ref[:, :, first : first + PAIR] = ref[pl.ds(half, half), :, cols]


def store_tiles(buf_ref, first, values):
    for t in range(values.shape[0] // TILE):
        buf_ref[first + t] = values[t * TILE : (t + 1) * TILE]


def start_split(buf_ref, keep_ref, send_ref, sems, last):
    half = (buf_ref.shape[0] - last) // 2
    copies = [
        pltpu.make_async_copy(buf_ref.at[pl.ds(0, half)], keep_ref.at[pl.ds(0, half)], sems.at[0]),
        pltpu.make_async_copy(buf_ref.at[pl.ds(half, half + last)], send_ref, sems.at[1]),
    ]
    if last:
        copies.append(
            pltpu.make_async_copy(buf_ref.at[pl.ds(2 * half, last)], keep_ref.at[pl.ds(half, last)], sems.at[2])
        )
    for copy in copies:
        copy.start()
    return copies


def split_out(buf_ref, keep_ref, send_ref, sems, last):
    for copy in start_split(buf_ref, keep_ref, send_ref, sems, last):
        copy.wait()


def conv_grads(tab_ref, buf_ref, tk_ref, tv_ref, grad, tiles, pieces, inverse_at):
    width = tk_ref.shape[1]
    slots = grad.shape[0]
    group = grad.shape[1] // 2
    conv_tiles = TAPS * width // pieces // TILE
    for i in range(TAPS):
        own = slice(i * slots, (i + 1) * slots)
        both = jnp.concatenate([tn(tk_ref[own], grad[:, :group]), tn(tv_ref[own], grad[:, group:])], 1).astype(narrow)
        for j in range(width // TILE):
            tile = i * (width // TILE) + j
            at = tab_ref[inverse_at + tile // conv_tiles] * tiles + tile % conv_tiles
            for c in range(2 * group // COLUMNS):
                buf_ref[at + c * conv_tiles] = both[j * TILE : (j + 1) * TILE, c * COLUMNS : (c + 1) * COLUMNS]


def weight_grads(tab_ref, buf_ref, grad, first, tiles, pieces, inverse_at):
    for j in range(pieces):
        at = tab_ref[inverse_at + j] * tiles + first
        for c in range(grad.shape[1] // COLUMNS):
            buf_ref[at + c] = grad[j * TILE : (j + 1) * TILE, c * COLUMNS : (c + 1) * COLUMNS]


def middle_kernel(
    tab_ref, qm_ref, dm_ref, lse_ref, delta_ref, kv_ref, tk_ref, tv_ref, first_ref, second_ref, gw_out_ref, ck_ref, cv_ref,
    *rest, pieces, inverse_at,
):
    dq_refs, (gk_ref, gv_ref, dq_ref, keep_ref, send_ref, buf_ref, own_s, sems) = rest[:-8], rest[-8:]
    attend_back_own_kernel(qm_ref, dm_ref, lse_ref, delta_ref, kv_ref, *dq_refs, dq_ref, own_s, first=0)
    tiles = buf_ref.shape[0] // pieces
    blocks = gw_out_ref.shape[1] // COLUMNS
    grad = slot_grads(first_ref, second_ref, own_s)
    conv_grads(tab_ref, buf_ref, tk_ref, tv_ref, grad, tiles, pieces, inverse_at)
    weight_grads(tab_ref, buf_ref, gw_out_ref, tiles - blocks, tiles, pieces, inverse_at)
    copies = start_split(buf_ref, keep_ref, send_ref, sems, 0)
    conv_back(grad, ck_ref, cv_ref, 0, gk_ref, gv_ref)
    for copy in copies:
        copy.wait()


def tail_query_kernel(hid_ref, tk_ref, ods_ref, wq_ref, early_ref, later_ref, gh_ref, gw_ref):
    own_ds = tn(ods_ref[...], head_rows(tk_ref.shape[1])) * scale
    dq = jnp.concatenate([early_ref[...], later_ref[...]], 1)
    gq = (dq * scale + own_ds * tk_ref[...].astype(single)).astype(narrow)
    gw_ref[...] = tn(hid_ref[...], gq).astype(narrow)
    gh_ref[...] = nt(gq, wq_ref[...])


def slot_grads(*refs):
    return sum(ref[...].astype(single) for ref in refs).astype(narrow)


def conv_back(grads, ck_ref, cv_ref, first, gk_ref, gv_ref):
    slots, width = grads.shape[0], ck_ref.shape[1]
    group = grads.shape[1] // 2
    for grad, c_ref, out_ref in ((grads[:, :group], ck_ref, gk_ref), (grads[:, group:], cv_ref, gv_ref)):
        for i in range(TAPS):
            out_ref[i * slots : (i + 1) * slots] = nt(grad, c_ref[i * width : (i + 1) * width, first : first + group])


def tail_kernel(
    tab_ref, x_ref, hid_ref, q_ref, tk_ref, tv_ref, ga_ref, gm_ref, own_ref, ods_ref, gh_ref, gk0_ref, gv0_ref,
    first_ref, second_ref, own_grad_ref, gwq_ref, wk_ref, wv_ref, ck_ref, cv_ref, gain_ref, gx_ref, keep_ref, send_ref, buf_ref, gk_s, gv_s, sems, *, pieces, inverse_at,
):
    rows, width = x_ref.shape
    tiles = (buf_ref.shape[0] - 1) // pieces
    blocks = width // COLUMNS
    grad = slot_grads(first_ref, second_ref, own_grad_ref)
    conv_grads(tab_ref, buf_ref, tk_ref, tv_ref, grad, tiles, pieces, inverse_at)
    marks = head_rows(width)
    own_ds = tn(ods_ref[...], marks) * scale
    own_prob = tn(own_ref[...].astype(narrow), marks)
    conv_back(grad, ck_ref, cv_ref, width - grad.shape[1] // 2, gk_s, gv_s)
    gk = (gk_s[...] + gk0_ref[...] + own_ds * q_ref[...].astype(single)).astype(narrow)
    gv = (gv_s[...] + gv0_ref[...] + own_prob * ga_ref[...].astype(single)).astype(narrow)
    weight_grads(tab_ref, buf_ref, gwq_ref, tiles - 3 * blocks, tiles, pieces, inverse_at)
    hidden_t = hid_ref[...].T
    grad_hidden = gh_ref[...]
    for number, grad in enumerate((gk, gv)):
        grad_w = nn(hidden_t, grad).astype(narrow)
        weight_grads(tab_ref, buf_ref, grad_w, tiles - (2 - number) * blocks, tiles, pieces, inverse_at)
        grad_hidden += nt(grad, (wk_ref, wv_ref)[number][...])
    unit, spread = standardized(x_ref[...].astype(single))
    place = lax.broadcasted_iota(jnp.int32, (TILE, COLUMNS), 0)
    sums = jnp.zeros((TILE, COLUMNS), single)
    for first, value in ((0, grad_hidden * unit), (blocks, grad_hidden)):
        total = jnp.sum(value, 0, keepdims=True)
        for c in range(blocks):
            sums = jnp.where(place == first + c, total[:, c * COLUMNS : (c + 1) * COLUMNS], sums)
    buf_ref[buf_ref.shape[0] - 1] = sums.astype(narrow)
    split_out(buf_ref, keep_ref, send_ref, sems, 1)
    gx_ref[...] = (gm_ref[...] + norm_back(grad_hidden, unit, spread, gain_ref[...])).astype(narrow)


def unpack_feed_kernel(
    tab_ref, own_ref, other_ref, small_ref, wd_ref, wu_ref, gain_ref, bias_ref, up_ref, down_ref, *, pieces, piece_at
):
    width = wd_ref.shape[1]
    down_rows = wd_ref.shape[0] // pieces
    down_tiles, up_tiles = down_rows // TILE, wu_ref.shape[1] // width
    tiles = down_tiles + up_tiles
    down_ref[...] = small_ref[0, 0:1, :]
    for t in range(up_tiles):
        up_ref[:, t * width : (t + 1) * width] = small_ref[0, 1 + t : 2 + t, :]
    gain_ref[...] = small_ref[0, 1 + up_tiles : 2 + up_tiles, :]
    bias_ref[...] = small_ref[0, 2 + up_tiles : 3 + up_tiles, :]

    for number, buf_ref in enumerate((own_ref, other_ref)):

        def step(k, carry, number=number, buf_ref=buf_ref):
            piece = tab_ref[piece_at + number * pieces // 2 + k]
            at = k * tiles
            for t in range(down_tiles):
                rows = pl.ds(pl.multiple_of(piece * down_rows + t * TILE, TILE), TILE)
                wd_ref[rows, :] = buf_ref[at + t].astype(single)
            mine = pl.ds(pl.multiple_of(piece * TILE, TILE), TILE)
            for t in range(up_tiles):
                wu_ref[mine, t * width : (t + 1) * width] = buf_ref[at + down_tiles + t].astype(single)
            return carry

        lax.fori_loop(0, pieces // 2, step, 0, unroll=4)


def unpack_kernel(tab_ref, *rest, parts, half, piece_at, first_column, outs, small):
    bufs, rest = rest[: len(parts)], rest[len(parts) :]
    if small:
        small_ref, small_outs, rest = rest[0], rest[-5 - outs : -3 - outs], rest[1:]
        for i, ref in enumerate(small_outs):
            ref[...] = small_ref[0, i : i + 1, :]
    out_refs, (conv_s, weight_s, sems) = rest[-outs - 3 : -3], rest[-3:]
    weight_refs, conv_refs = out_refs[:-2], out_refs[-2:]
    conv_rows, columns = conv_s.shape[2], conv_s.shape[3]
    conv_tiles = conv_rows // TILE
    blocks = weight_s.shape[3] // COLUMNS
    weights_at = conv_tiles * (2 * columns // COLUMNS)
    tiles = weights_at + blocks * len(weight_refs)

    def copies(number, place):
        piece = tab_ref[piece_at + place]
        rows = pl.ds(pl.multiple_of(piece * conv_rows, TILE), conv_rows)
        mine = pl.ds(pl.multiple_of(piece * TILE, TILE), TILE)
        cols = pl.ds(first_column, columns)
        return [
            pltpu.make_async_copy(conv_s.at[number, i], ref.at[rows, cols], sems.at[number, i])
            for i, ref in enumerate(conv_refs)
        ] + [
            pltpu.make_async_copy(weight_s.at[number, i], ref.at[mine], sems.at[number, 2 + i])
            for i, ref in enumerate(weight_refs)
        ]

    for order, (buf_ref, part) in enumerate(zip(bufs, parts)):

        def step(k, carry, order=order, buf_ref=buf_ref, part=part):
            number = order * half + k
            for t in range(conv_tiles):
                for unit in range(2 * columns // PAIR):
                    which, first = unit * PAIR // columns, unit * PAIR % columns
                    block, lanes = unit * PAIR // COLUMNS, unit * PAIR % COLUMNS
                    conv_s[number, which, t * TILE : (t + 1) * TILE, first : first + PAIR] = buf_ref[
                        k * tiles + block * conv_tiles + t, :, lanes : lanes + PAIR
                    ].astype(single)
            for t in range(len(weight_refs)):
                for c in range(blocks):
                    weight_s[number, t, :, c * COLUMNS : (c + 1) * COLUMNS] = buf_ref[
                        k * tiles + weights_at + t * blocks + c
                    ].astype(single)
            for copy in copies(number, part * half + k):
                copy.start()
            return carry

        lax.fori_loop(0, half, step, 0)

    for order, part in enumerate(parts):

        def finish(k, carry, order=order, part=part):
            for copy in copies(order * half + k, part * half + k):
                copy.wait()
            return carry

        lax.fori_loop(0, half, finish, 0)


def shaped(shape, kind):
    return jax.ShapeDtypeStruct(shape, kind)


def per_device(
    seq_size, batch_size,
    inputs, cotangent, ln1_gain, ln1_bias, w_query, w_key, w_value, conv_key, conv_value, w_out,
    ln2_gain, ln2_bias, w_up, up_bias, w_down, down_bias,
):
    x, g = inputs[0], cotangent[0]
    rows, width = x.shape
    slots = rows // TAPS
    ff = w_up.shape[1]
    seq_bits, batch_bits = seq_size.bit_length() - 1, batch_size.bit_length() - 1
    split_bits = min(5, seq_bits + batch_bits)
    pieces = 1 << split_bits
    list_at = seq_size
    piece_at = list_at + seq_size
    inverse_at = piece_at + pieces
    tables = jnp.asarray(plan_tables(seq_size, batch_size, split_bits))
    table = lax.dynamic_index_in_dim(
        tables, lax.axis_index("seq") * batch_size + lax.axis_index("batch"), 0, keepdims=False
    )
    x = tied(x, table)
    row = lambda v: v.reshape(1, -1)
    ck = conv_key.reshape(TAPS * width, width)
    cv = conv_value.reshape(TAPS * width, width)
    token_low, token_wide = shaped((rows, width), narrow), shaped((rows, width), single)
    head_wide, head_low = shaped((HEADS, rows), single), shaped((HEADS, rows), narrow)
    two_low = shaped((2, rows, width), narrow)

    xp, hidden, tk, tv, kv = call(
        "front",
        front_kernel,
        (token_low,) * 4 + (shaped((slots, 2 * width), narrow),),
        loads=(x, row(ln1_gain), row(ln1_bias), w_key, ck, w_value, cv),
        mib=24,
        flops=4e9,
    )

    state = shaped((HEADS, rows, PAIR), single)
    q, gp, qm, own, m, acc = call(
        "attend_own",
        attend_own_kernel,
        (token_low, token_low, two_low, head_wide, state, state),
        loads=(w_query, g),
        operands=(hidden, tk, tv, kv[None]),
        mib=16,
        flops=1e10,
    )
    blocks = {0: kv[None]}
    rounds = gather_plan(seq_size)
    calls = []
    for number, found in enumerate(rounds):
        if number > 0:
            calls.append([entry[0] for entry in rounds[number - 1]])
        held = {source: blocks[source] for _, source, _ in found if source in blocks}
        if number > 1:
            held = tied(held, m)
        for block, source, (axis, pairs) in found:
            if source in held:
                blocks[block] = lax.ppermute(held[source], axis, pairs)
        if number == 0:
            continue
        later = [entry for entry in found if entry[0] not in blocks]
        found = calls[-1]
        m, acc = call(
            f"attend_{found[0]}",
            functools.partial(attend_more_kernel, blocks=found),
            (state, state),
            table=table,
            operands=(qm, m, acc, *[blocks[k] for k in found]),
            mib=8,
            flops=1e10 * len(found),
        )
        for block, source, (axis, pairs) in later:
            blocks[block] = lax.ppermute(tied(blocks[source], m), axis, pairs)
    calls.append([entry[0] for entry in rounds[-1]])
    attended, lse, own_prob = call(
        "attend_last",
        functools.partial(attend_last_kernel, blocks=calls[-1]),
        (token_wide, head_wide, head_wide),
        table=table,
        operands=(qm, own, m, acc, *[blocks[k] for k in calls[-1]]),
        scratch=[pltpu.VMEM(state.shape, single), pltpu.VMEM(state.shape, single)],
        mib=16,
        flops=1e10 * len(calls[-1]),
    )

    steps = ff // width
    tiles = ff // pieces // TILE + steps
    half = shaped((pieces // 2 * tiles + 1, TILE, width), narrow)
    output, middle, grad_normal, keep, send, all_kv = call(
        "feed",
        functools.partial(feed_kernel, pieces=pieces, inverse_at=inverse_at),
        (token_low, token_wide, token_wide, half, half, shaped((seq_size, slots, 2 * width), narrow)),
        loads=(row(ln2_gain), row(ln2_bias), w_up, row(up_bias), w_down, row(down_bias)),
        table=table,
        operands=(xp, attended, gp, w_out),
        away=[blocks[k] for k in range(seq_size)],
        away_outs=3,
        scratch=[
            pltpu.VMEM((rows, width), narrow),
            pltpu.VMEM((width, rows), narrow),
            pltpu.VMEM((rows, width), single),
            pltpu.VMEM((pieces * tiles + 1, TILE, width), narrow),
            pltpu.SemaphoreType.DMA((3 + seq_size,)),
        ],
        mib=30,
        flops=5e10,
    )
    grad_middle, grad_w_out_here, grad_attended, dm, delta, own_ds = call(
        "branch",
        branch_kernel,
        (token_wide, shaped((width, width), narrow), token_low, two_low, head_wide, head_low),
        loads=(row(ln2_gain),),
        operands=(middle, grad_normal, gp, attended, tv, own_prob, w_out),
        mib=16,
        flops=1e11,
    )

    stages = reduce_stages(seq_size, batch_size, split_bits)
    gather_back = [stage for stage in stages if stage[0] > 1][::-1]
    unseen = gather_stages(seq_size)[::-1]
    head_pairs = HEADS // 2

    wide_grant = 12 if seq_size <= 8 else 56
    share = shaped((seq_size // 2, slots, 2 * PAIR), narrow)

    def back(pair, qm):
        return call(
            f"attend_back_{pair}",
            functools.partial(attend_back_kernel, list_at=list_at, pair=pair),
            (shaped((rows, PAIR), single), share, share),
            table=table,
            operands=(qm, dm, lse, delta, all_kv),
            mib=wide_grant,
            flops=1e11,
        )

    def small_call(kernel, name, outs, *operands):
        return call(name, kernel, outs, operands=operands, mib=4, flops=sum(v.size for v in operands) * 600)

    def sum_split(buffers, last, cut):
        count, rest = buffers[0].shape[0], buffers[0].shape[1:]
        outs = (shaped(((count - last) // cut + last, *rest), narrow),) * cut
        kernel = functools.partial(sum_split_kernel, count=len(buffers), last=last)
        return small_call(kernel, "sum_split", outs, *buffers)

    def join(*parts):
        out = shaped((len(parts) * parts[0].shape[0], *parts[0].shape[1:]), narrow)
        return small_call(join_kernel, "join", (out,), *parts)[0]

    def exchange(stage, parts):
        return [lax.ppermute(part, stage[1], pairs) for part, pairs in zip(parts, stage[2])]

    class Sum:
        def __init__(self, keep, send, last):
            self.keep, self.last, self.at = keep, last, 0
            self.arrived = exchange(stages[0], [send])

        def step(self, *others):
            arrived = tied(self.arrived, *others)
            self.at += 1
            if self.at < len(stages):
                cut = stages[self.at][0]
                parts = sum_split((self.keep, *arrived), self.last, cut)
                self.keep, sent = parts[0], parts[1:] if cut > 1 else parts
                self.arrived = exchange(stages[self.at], sent)
                return sent[0]
            if self.at == len(stages):
                buffers = (self.keep, *arrived)
                if self.last:
                    count, rest = buffers[0].shape[0], buffers[0].shape[1:]
                    outs = (shaped((count - self.last, *rest), narrow), shaped((self.last, *rest), single))
                    kernel = functools.partial(sum_last_kernel, count=len(buffers), last=self.last)
                    self.held, self.small = small_call(kernel, "sum_last", outs, *buffers)
                else:
                    (self.held,) = sum_split(buffers, 0, 1)
            else:
                self.held = join(self.held, *arrived)
            stage = gather_back[self.at - len(stages)]
            self.arrived = exchange(stage, [self.held] * len(stage[2]))
            return self.held

        def left(self):
            return len(stages) + len(gather_back) - 1 - self.at

    class Group:
        def __init__(self):
            self.shares, self.at = [], 0

        def step(self, *others):
            self.at += 1
            if self.at == 1:
                operands = tied(self.shares, *others)
                half = shaped((seq_size // 4, slots, len(self.shares) * 2 * PAIR), narrow)
                self.keep, send = small_call(group_split_kernel, "group_split", (half, half), *operands)
            else:
                self.keep, send = sum_split((self.keep, tied(self.arrived, *others)), 0, 2)
            self.arrived = lax.ppermute(send, *unseen[self.at])
            return send

        def left(self):
            return len(unseen) - 1 - self.at

    conv_tiles = TAPS * width // pieces // TILE
    blocks_wide = width // COLUMNS
    first_tiles, tail_tiles = (
        conv_tiles * (group * 2 * PAIR // COLUMNS) + count * blocks_wide for group, count in zip(GROUPS, (1, 3))
    )

    sums = {"feed": Sum(keep, send, 1)}
    first_group, second_group = Group(), Group()
    waits = [sums["feed"].step(delta)]
    state_back = {"grads": []}

    def advance(name, kept=0):
        if name in sums and sums[name].left() > kept:
            waits.append(sums[name].step(*waits))

    def advance_group(group):
        if group.left() > 0:
            waits.append(group.step(*waits))

    def add_share(group, kept, arrived):
        (total,) = sum_split(tied((kept, arrived), *waits), 0, 1)
        waits.append(total)
        group.shares.append(total)

    partial_q, pending = [], None
    for pair in range(head_pairs):
        in_first = pair < GROUPS[0]
        grads, kept, sent = back(pair, tied(qm, *waits))
        waits = [grads]
        partial_q.append(grads)
        if pair < head_pairs - 1:
            advance("feed", 1)
        if pending is not None:
            add_share(*pending)
        pending = (first_group if in_first else second_group, kept, lax.ppermute(sent, *unseen[0]))
        if pair >= GROUPS[0]:
            advance_group(first_group)
    def own_block(first, count):
        return call(
            f"attend_back_own_{first}",
            functools.partial(attend_back_own_kernel, first=first),
            (shaped((rows, count * PAIR), single), shaped((slots, count * 2 * PAIR), single)),
            operands=(tied(qm, *waits), dm, lse, delta, kv[None], *partial_q[first : first + count]),
            mib=12,
            flops=1e11,
        )

    later_q, second_own = own_block(GROUPS[0], GROUPS[1])
    waits = [later_q]
    add_share(*pending)
    advance_group(second_group)
    advance("feed", 1)
    while first_group.left() > 0:
        advance_group(first_group)
    half = shaped((pieces // 2 * first_tiles, TILE, COLUMNS), narrow)
    grad_k, grad_v, early_q, keep0, send0 = call(
        "middle",
        functools.partial(middle_kernel, pieces=pieces, inverse_at=inverse_at),
        (token_wide, token_wide, shaped((rows, GROUPS[0] * PAIR), single), half, half),
        table=table,
        operands=(
            tied(qm, *waits), dm, lse, delta, kv[None], tk, tv, first_group.keep[0], first_group.arrived[0],
            grad_w_out_here, ck, cv, *partial_q[: GROUPS[0]],
        ),
        away_outs=2,
        scratch=[
            pltpu.VMEM((pieces * first_tiles, TILE, COLUMNS), narrow),
            pltpu.VMEM((slots, GROUPS[0] * 2 * PAIR), single),
            pltpu.SemaphoreType.DMA((3,)),
        ],
        mib=24,
        flops=1e11,
    )
    sums["first"] = Sum(keep0, send0, 0)
    waits = [grad_k]
    advance("feed", 1)
    advance_group(second_group)
    grad_hidden, grad_wq_here = call(
        "tail_query",
        tail_query_kernel,
        (token_wide, shaped((width, width), narrow)),
        operands=(tied(hidden, *waits), tk, own_ds, w_query, early_q, later_q),
        mib=16,
        flops=1e11,
    )
    waits = [grad_hidden]
    while second_group.left() > 0:
        advance_group(second_group)
    advance("first")
    half = shaped((pieces // 2 * tail_tiles + 1, TILE, COLUMNS), narrow)
    grad_x, keep1, send1 = call(
        "tail",
        functools.partial(tail_kernel, pieces=pieces, inverse_at=inverse_at),
        (token_low, half, half),
        table=table,
        operands=(
            xp, hidden, q, tk, tv, grad_attended, grad_middle, own_prob, own_ds, grad_hidden, grad_k, grad_v,
            tied(second_group.keep[0], *waits), second_group.arrived[0], second_own, grad_wq_here,
            w_key, w_value, ck, cv, row(ln1_gain),
        ),
        away_outs=2,
        scratch=[
            pltpu.VMEM((pieces * tail_tiles + 1, TILE, COLUMNS), narrow),
            pltpu.VMEM((rows, width), single),
            pltpu.VMEM((rows, width), single),
            pltpu.SemaphoreType.DMA((3,)),
        ],
        mib=26,
        flops=1e11,
    )
    sums["second"] = Sum(keep1, send1, 1)
    waits = [grad_x]

    def unpack(name, parts, heads, weights, bufs, *known, small=()):
        count = len(parts) * pieces // 2
        outs = [shaped((width, width), single)] * weights + [shaped(ck.shape, single)] * 2
        first = [shaped((1, width), single)] * (2 * len(small))
        return call(
            name,
            functools.partial(
                unpack_kernel,
                parts=parts,
                half=pieces // 2,
                piece_at=piece_at,
                first_column=heads[0] * PAIR,
                outs=len(outs),
                small=len(small),
            ),
            first + outs,
            table=table,
            operands=(*bufs, *small),
            away=known,
            away_outs=len(outs),
            in_place=len(known),
            scratch=[
                pltpu.VMEM((count, 2, conv_tiles * TILE, heads[1] * PAIR), single),
                pltpu.VMEM((count, weights, TILE, width), single),
                pltpu.SemaphoreType.DMA((count, len(outs))),
            ],
            mib=20,
            flops=1e11,
        )

    def finish_feed(*others):
        vector = shaped((1, width), single)
        return call(
            "unpack_feed",
            functools.partial(unpack_feed_kernel, pieces=pieces, piece_at=piece_at),
            (shaped((ff, width), single), shaped((width, ff), single), vector, vector, shaped((1, ff), single), vector),
            table=table,
            operands=(sums["feed"].held, tied(sums["feed"].arrived[0], *others), sums["feed"].small),
            mib=16,
            flops=2e10,
        )

    places = (GROUPS[0], GROUPS[1])
    for action in "F0R010010101F0111F01Uu1":
        if action in "01F":
            advance({"0": "first", "1": "second", "F": "feed"}[action])
            waits = waits[-1:]
        elif action == "R":
            output, grad_x = call(
                "reorder",
                reorder_kernel,
                (token_low, token_low),
                operands=(output, tied(grad_x, *waits)),
                mib=8,
                flops=1e11,
            )
            waits.append(grad_x)
        elif action == "U":
            while sums["feed"].left() > 0:
                advance("feed")
            grad_w_down, grad_w_up, *small_feed = finish_feed(*waits)
            waits.append(grad_w_up)
        elif action == "u":
            while sums["first"].left() > 0:
                advance("first")
            while sums["second"].left() > 1:
                advance("second")
            grad_w_out, *convs = unpack(
                "unpack_first",
                (0, 1),
                (0, GROUPS[0]),
                1,
                (sums["first"].held, tied(sums["first"].arrived[0], *waits)),
            )
            waits.append(grad_w_out)
    last = sums["second"]
    small_first, small_second, *found = unpack(
        "unpack_own", (0,), places, 3, (last.held,), *tied(convs, *waits), small=(last.small,)
    )
    grad_wq, grad_wk, grad_wv, grad_ck, grad_cv = unpack(
        "unpack_last", (1,), places, 3, (last.arrived[0],), *found
    )
    return (
        output[None],
        grad_x[None],
        small_first[0],
        small_second[0],
        grad_wq,
        grad_wk,
        grad_wv,
        grad_ck.reshape(conv_key.shape),
        grad_cv.reshape(conv_value.shape),
        grad_w_out,
        small_feed[0][0],
        small_feed[1][0],
        grad_w_up,
        small_feed[2][0],
        grad_w_down,
        small_feed[3][0],
    )


def solution(mesh):
    placed = (P("batch", "seq", None),) * 2 + (P(),) * 14
    return jax.shard_map(
        functools.partial(per_device, mesh.shape["seq"], mesh.shape["batch"]),
        mesh=mesh,
        in_specs=placed,
        out_specs=placed,
        check_vma=False,
    )
```

```python
import functools

import jax
import jax.numpy as jnp
import numpy as np
from jax import lax
from jax.experimental import pallas as pl
from jax.experimental.pallas import tpu as pltpu
from jax.sharding import PartitionSpec as P

HEADS = 8
HEAD_DIM = 64
PAIR = 2 * HEAD_DIM
TAPS = 3
TILE = 16
COLUMNS = 512
GROUPS = (2, 2)

epsilon = 1e-05
narrow = jnp.bfloat16
single = jnp.float32
scale = HEAD_DIM ** (-0.5)

vmem = pl.BlockSpec(memory_space=pltpu.VMEM)
smem = pl.BlockSpec(memory_space=pltpu.SMEM)
anywhere = pl.BlockSpec(memory_space=pl.ANY)
hbm = pl.BlockSpec(memory_space=pltpu.HBM)


def params(mib):
    return pltpu.CompilerParams(vmem_limit_bytes=mib * 2**20)


def cost(flops, moved):
    return pl.CostEstimate(flops=int(flops), bytes_accessed=int(moved), transcendentals=0)


class Loads:
    def __init__(self, sources, held, sems):
        self.held, self.waited = held, set()
        self.copies = [pltpu.make_async_copy(a, b, sems.at[i]) for i, (a, b) in enumerate(zip(sources, held))]
        for copy in self.copies:
            copy.start()

    def __getitem__(self, i):
        if i not in self.waited:
            self.copies[i].wait()
            self.waited.add(i)
        return self.held[i]


def call(
    name, body, outs, *, loads=(), table=None, operands=(), away=(), away_outs=0, in_place=0, scratch=(), mib, flops
):
    count = len(loads)
    inputs = count + (table is not None) + len(operands) + len(away)

    def kernel(*refs):
        sources, rest = refs[:count], refs[count:]
        if count == 0:
            return body(*rest)
        held, sems = rest[-count - 1 : -1], rest[-1]
        return body(Loads(sources, held, sems), *rest[: -count - 1])

    moved = sum(v.size * 2 for v in (*loads, *operands, *away, *outs))
    scratch = list(scratch)
    if count:
        scratch += [pltpu.VMEM(v.shape, v.dtype) for v in loads] + [pltpu.SemaphoreType.DMA((count,))]
    return pl.pallas_call(
        kernel,
        out_shape=tuple(outs),
        in_specs=[hbm] * count + [smem] * (table is not None) + [vmem] * len(operands) + [anywhere] * len(away),
        out_specs=(vmem,) * (len(outs) - away_outs) + (anywhere,) * away_outs,
        scratch_shapes=scratch,
        input_output_aliases={inputs - in_place + i: len(outs) - in_place + i for i in range(in_place)},
        compiler_params=params(mib),
        cost_estimate=cost(flops, moved),
        name=name,
    )(
        *[pltpu.with_memory_space_constraint(v, pltpu.HBM) for v in loads],
        *([] if table is None else [table]),
        *operands,
        *away,
    )


def tied(values, *others):
    return lax.optimization_barrier((values, others))[0]


def nn(a, b):
    return lax.dot_general(a, b, (((1,), (0,)), ((), ())), preferred_element_type=single)


def nt(a, b):
    return lax.dot_general(a, b, (((1,), (1,)), ((), ())), preferred_element_type=single)


def tn(a, b):
    return lax.dot_general(a, b, (((0,), (0,)), ((), ())), preferred_element_type=single)


def bit_masks(size):
    return [1 << b for b in range(size.bit_length() - 1)]


def seq_masks(size, core):
    masks = bit_masks(size)[1:]
    return masks if core == 0 else masks[::-1]


def seq_swap(size, stage):
    return [(i, i ^ seq_masks(size, i & 1)[stage]) for i in range(size)]


def gather_stages(seq_size):
    found = [("seq", seq_swap(seq_size, j)) for j in range(len(bit_masks(seq_size)) - 1)]
    return found + [("seq", [(i, i ^ 1) for i in range(seq_size)])]


def reduce_stages(seq_size, batch_size, split_bits):
    found = [(2, "seq", [[(i, i ^ 1) for i in range(seq_size)]])]
    found += [(2, "seq", [seq_swap(seq_size, j)]) for j in range(len(bit_masks(seq_size)) - 1)]
    split = split_bits - len(found)
    for j, mask in enumerate(bit_masks(batch_size)):
        found.append((2 if j < split else 1, "batch", [[(i, i ^ mask) for i in range(batch_size)]]))
    return found


def gather_origin(seq_size, me, block):
    count = len(bit_masks(seq_size)) - 1
    core_bit = (block >> count) & 1
    other = me ^ core_bit
    masks = seq_masks(seq_size, other & 1)
    for j in range(count):
        if (block >> j) & 1:
            other ^= masks[j]
    return other


def piece_of(seq_size, batch_size, split_bits, me_seq, me_batch, place):
    bits = [(place >> (split_bits - 1 - j)) & 1 for j in range(split_bits)]
    s = me_seq ^ bits[0]
    masks = seq_masks(seq_size, s & 1)
    z = me_batch
    for j, b in enumerate(bits[1:]):
        if j < len(masks):
            s ^= masks[j] * b
        else:
            z ^= (1 << (j - len(masks))) * b
    low_batch = z & ((1 << (split_bits - len(bit_masks(seq_size)))) - 1)
    return s + seq_size * low_batch


def gather_plan(seq_size):
    stages = gather_stages(seq_size)
    count = len(stages) - 1
    rounds = [[] for _ in range(count + 1)]
    for block in range(1, 1 << count):
        last = block.bit_length() - 1
        rounds[bin(block).count("1")].append((block, block ^ (1 << last), stages[last]))
    for found in rounds:
        blocks = [entry[0] for entry in found] or [0]
        found += [(block | (1 << count), block, stages[-1]) for block in blocks]
    return rounds


def plan_tables(seq_size, batch_size, split_bits):
    rows = []
    pieces = 1 << split_bits
    for s in range(seq_size):
        origins = [gather_origin(seq_size, s, k) for k in range(seq_size)]
        seen = [int(origin < s) for origin in origins]
        visible = [k for k in range(seq_size) if origins[k] < s]
        lists = [len(visible)] + visible + [k for k in range(seq_size) if origins[k] > s]
        for z in range(batch_size):
            places = [piece_of(seq_size, batch_size, split_bits, s, z, k) for k in range(pieces)]
            inverse = [places.index(p) for p in range(pieces)]
            rows.append(seen + lists + places + inverse)
    return np.asarray(rows, np.int32)


def token_order(rows):
    slots = rows // TAPS
    r = lax.broadcasted_iota(jnp.int32, (rows, rows), 0)
    c = lax.broadcasted_iota(jnp.int32, (rows, rows), 1)
    return jnp.where(c == TAPS * (r % slots) + r // slots, 1.0, 0.0).astype(narrow)


def head_rows(width):
    r = lax.broadcasted_iota(jnp.int32, (HEADS, width), 0)
    c = lax.broadcasted_iota(jnp.int32, (HEADS, width), 1)
    return jnp.where(c // HEAD_DIM == r, 1.0, 0.0).astype(narrow)


def head_sums(values):
    marks = head_rows(values.shape[1])
    high = values.astype(narrow)
    rest = values - high.astype(single)
    middle = rest.astype(narrow)
    low = (rest - middle.astype(single)).astype(narrow)
    return nt(marks, high) + nt(marks, middle) + nt(marks, low)


def standardized(values):
    centred = values - jnp.mean(values, -1, keepdims=True)
    spread = lax.rsqrt(jnp.mean(centred * centred, -1, keepdims=True) + epsilon)
    return centred * spread, spread


def norm_back(grad, unit, spread, gain):
    inner = grad * gain
    return spread * (
        inner
        - jnp.mean(inner, -1, keepdims=True)
        - unit * jnp.mean(inner * unit, -1, keepdims=True)
    )


def front_kernel(loads, xp_ref, hid_ref, tk_ref, tv_ref, kv_ref):
    rows, width = xp_ref.shape
    slots = rows // TAPS
    order = token_order(rows)
    x = nn(order, loads[0][...])
    xp_ref[...] = x.astype(narrow)
    unit, _ = standardized(x)
    hidden = (unit * loads[1][...] + loads[2][...]).astype(narrow)
    hid_ref[...] = hidden
    for number, t_ref in enumerate((tk_ref, tv_ref)):
        t = nn(hidden, loads[3 + 2 * number][...]).astype(narrow)
        t_ref[...] = t
        c_ref = loads[4 + 2 * number]
        total = nn(t[:slots], c_ref[:width])
        for i in range(1, TAPS):
            total += nn(t[i * slots : (i + 1) * slots], c_ref[i * width : (i + 1) * width])
        kv_ref[:, number * width : (number + 1) * width] = total.astype(narrow)


def attend_block(kv_ref, number, qm_ref, m_ref, acc_ref, diagonal):
    slots, width = kv_ref.shape[1], qm_ref.shape[2]
    lane = lax.broadcasted_iota(jnp.int32, (1, PAIR), 1)
    for h in range(HEADS):
        cols = slice(PAIR * (h // 2), PAIR * (h // 2 + 1))
        keep = (lane < HEAD_DIM) if h % 2 == 0 else (lane >= HEAD_DIM)
        v = kv_ref[number, :, width + cols.start : width + cols.stop]
        v_ones = jnp.where(keep, v, jnp.ones_like(v))
        s = nt(qm_ref[h % 2, :, cols], kv_ref[number, :, cols])
        if diagonal:
            slot = lax.broadcasted_iota(jnp.int32, s.shape, 1)
            row = lax.broadcasted_iota(jnp.int32, s.shape, 0)
            s = jnp.where(3 * slot + 2 <= 3 * (row % slots) + row // slots, s, -1e30)
        before = m_ref[h]
        after = jnp.maximum(before, jnp.max(s, 1, keepdims=True))
        m_ref[h] = after
        p = jnp.exp(s - jnp.concatenate([after] * (slots // PAIR), 1))
        acc_ref[h] = acc_ref[h] * jnp.exp(before - after) + nn(p.astype(narrow), v_ones)


def split_heads(values, out_ref):
    lanes = lax.broadcasted_iota(jnp.int32, (1, values.shape[1]), 1) % PAIR
    nothing = jnp.zeros_like(values)
    out_ref[0] = jnp.where(lanes < HEAD_DIM, values, nothing)
    out_ref[1] = jnp.where(lanes >= HEAD_DIM, values, nothing)


def attend_own_kernel(loads, hid_ref, tk_ref, tv_ref, kv_ref, q_ref, gp_ref, qm_ref, own_ref, m_ref, acc_ref):
    rows, width = hid_ref.shape
    q_low = nn(hid_ref[...], loads[0][...]).astype(narrow)
    q_ref[...] = q_low
    q = q_low.astype(single)
    split_heads((q * scale).astype(narrow), qm_ref)
    own = head_sums(q * tk_ref[...].astype(single)) * scale
    own_ref[...] = own
    own_cols = own.T
    lane = lax.broadcasted_iota(jnp.int32, (1, PAIR), 1)
    for h in range(HEADS):
        keep = (lane < HEAD_DIM) if h % 2 == 0 else (lane >= HEAD_DIM)
        m_ref[h] = jnp.broadcast_to(own_cols[:, h : h + 1], (rows, PAIR))
        acc_ref[h] = jnp.where(keep, tv_ref[:, PAIR * (h // 2) : PAIR * (h // 2 + 1)].astype(single), 1.0)
    attend_block(kv_ref, 0, qm_ref, m_ref, acc_ref, True)
    gp_ref[...] = nn(token_order(rows), loads[1][...]).astype(narrow)


def attend_seen(tab_ref, blocks, kv_refs, qm_ref, m_ref, acc_ref):
    for block, kv_ref in zip(blocks, kv_refs):

        @pl.when(tab_ref[block] == 1)
        def _(kv_ref=kv_ref):
            attend_block(kv_ref, 0, qm_ref, m_ref, acc_ref, False)


def attend_more_kernel(tab_ref, qm_ref, m_in, acc_in, *rest, blocks):
    kv_refs, (m_ref, acc_ref) = rest[:-2], rest[-2:]
    m_ref[...] = m_in[...]
    acc_ref[...] = acc_in[...]
    attend_seen(tab_ref, blocks, kv_refs, qm_ref, m_ref, acc_ref)


def attend_last_kernel(tab_ref, qm_ref, own_ref, m_in, acc_in, *rest, blocks):
    kv_refs, (att_ref, lse_ref, prob_ref, m_ref, acc_ref) = rest[:-5], rest[-5:]
    m_ref[...] = m_in[...]
    acc_ref[...] = acc_in[...]
    attend_seen(tab_ref, blocks, kv_refs, qm_ref, m_ref, acc_ref)
    lane = lax.broadcasted_iota(jnp.int32, (1, PAIR), 1)
    columns = []
    for p in range(HEADS // 2):
        first, second = acc_ref[2 * p], acc_ref[2 * p + 1]
        sums = pltpu.roll(jnp.where(lane < HEAD_DIM, second, first), HEAD_DIM, 1)
        att_ref[:, PAIR * p : PAIR * (p + 1)] = jnp.where(lane < HEAD_DIM, first, second) / sums
        columns.append(m_ref[2 * p][:, :1] + jnp.log(first[:, HEAD_DIM : HEAD_DIM + 1]))
        columns.append(m_ref[2 * p + 1][:, :1] + jnp.log(second[:, :1]))
    lse = jnp.concatenate(columns, 1).T
    lse_ref[...] = lse
    prob_ref[...] = jnp.exp(own_ref[...] - lse)


def gelu_parts(u):
    bell = jnp.exp(-0.5 * (u * u))
    t = 1.0 / (1.0 + (0.3275911 * 0.5**0.5) * jnp.abs(u))
    series = t * (0.127414796 + t * (-0.142248368 + t * (0.7107068705 + t * (-0.7265760135 + t * 0.5307027145))))
    tail = series * bell
    below = jnp.where(u >= 0.0, 1.0 - tail, tail)
    return u * below, below + u * (bell * 0.3989422804014327)


def feed_kernel(loads, tab_ref, x_ref, att_ref, g_ref, wo_ref, *rest, pieces, inverse_at):
    kv_refs = rest[:-11]
    out_ref, mid_ref, gh_ref, keep_ref, send_ref, kv_all, h_s, ht_s, out_s, buf_ref, sems = rest[-11:]
    copies = [
        pltpu.make_async_copy(kv_ref, kv_all.at[pl.ds(i, 1)], sems.at[3 + i]) for i, kv_ref in enumerate(kv_refs)
    ]
    for copy in copies:
        copy.start()
    rows, width = x_ref.shape
    hidden_rows = loads.held[4].shape[0]
    steps = hidden_rows // width
    down_rows = hidden_rows // pieces
    down_tiles = down_rows // TILE
    tiles = down_tiles + steps
    middle = x_ref[...].astype(single) + nn(att_ref[...].astype(narrow), wo_ref[...])
    mid_ref[...] = middle
    unit, _ = standardized(middle)
    h = (unit * loads[0][...] + loads[1][...]).astype(narrow)
    h_s[...] = h
    ht_s[...] = h.T
    g = g_ref[...]
    wu_ref, ub_ref, wd_ref, db_ref = (loads[i] for i in range(2, 6))
    small = buf_ref.shape[0] - 1
    place = lax.broadcasted_iota(jnp.int32, (TILE, width), 0)
    here = pieces // steps
    out_s[...] = middle + db_ref[...]
    gh_ref[...] = jnp.zeros_like(middle)

    def step(i, sums):
        cols = pl.ds(pl.multiple_of(i * width, width), width)
        act, slope = gelu_parts(nn(h_s[...], wu_ref[:, cols]) + ub_ref[:, cols])
        act = act.astype(narrow)
        out_s[...] += nn(act, wd_ref[cols, :])
        gu = (nt(g_ref[...], wd_ref[cols, :]) * slope).astype(narrow)
        gh_ref[...] += nt(gu, wu_ref[:, cols])
        grad_down = tn(act, g_ref[...]).astype(narrow)
        for j in range(here):
            at = tab_ref[inverse_at + i * here + j] * tiles
            store_tiles(buf_ref, at, grad_down[j * down_rows : (j + 1) * down_rows])
        grad_up = nn(ht_s[...], gu).astype(narrow)
        for j in range(pieces):
            buf_ref[tab_ref[inverse_at + j] * tiles + down_tiles + i] = grad_up[j * TILE : (j + 1) * TILE]
        return jnp.where(place == 1 + i, jnp.sum(gu.astype(single), 0, keepdims=True), sums)

    sums = lax.fori_loop(0, steps, step, jnp.zeros((TILE, width), single))
    unit, _ = standardized(mid_ref[...])
    gh = gh_ref[...]
    for row, value in ((0, g.astype(single)), (1 + steps, gh * unit), (2 + steps, gh)):
        sums = jnp.where(place == row, jnp.sum(value, 0, keepdims=True), sums)
    buf_ref[small] = sums.astype(narrow)
    out_ref[...] = out_s[...].astype(narrow)
    split_out(buf_ref, keep_ref, send_ref, sems, 1)
    for copy in copies:
        copy.wait()


def branch_kernel(
    loads, mid_ref, gh_ref, g_ref, att_ref, tv_ref, own_ref, wo_ref, gm_ref, gw_ref, ga_ref, dm_ref, delta_ref, ods_ref
):
    unit, spread = standardized(mid_ref[...])
    gm = g_ref[...].astype(single) + norm_back(gh_ref[...], unit, spread, loads[0][...])
    gm_ref[...] = gm
    branch = gm.astype(narrow)
    att = att_ref[...]
    ga = nt(branch, wo_ref[...]).astype(narrow)
    ga_ref[...] = ga
    split_heads(ga, dm_ref)
    wide = ga.astype(single)
    delta = head_sums(wide * att)
    delta_ref[...] = delta
    dprob = head_sums(wide * tv_ref[...].astype(single))
    ods_ref[...] = (own_ref[...] * (dprob - delta)).astype(narrow)
    gw_ref[...] = tn(att.astype(narrow), branch).astype(narrow)


def reorder_kernel(out_ref, gx_ref, to_out_ref, to_gx_ref):
    order = token_order(out_ref.shape[0])
    to_out_ref[...] = tn(order, out_ref[...]).astype(narrow)
    to_gx_ref[...] = tn(order, gx_ref[...]).astype(narrow)


def back_block(kv_ref, number, pair, qm_ref, dm_ref, lse_ref, delta_ref, diagonal):
    slots, width = kv_ref.shape[1], qm_ref.shape[2]
    cols = slice(PAIR * pair, PAIR * (pair + 1))
    k = kv_ref[number, :, cols]
    v = kv_ref[number, :, width + cols.start : width + cols.stop]
    lane = lax.broadcasted_iota(jnp.int32, (1, PAIR), 1)
    scores, probs = [], []
    for half in range(2):
        h = 2 * pair + half
        prob = jnp.exp(nt(k, qm_ref[half, :, cols]) - lse_ref[h : h + 1, :])
        dprob = nt(v, dm_ref[half, :, cols])
        if diagonal:
            slot = lax.broadcasted_iota(jnp.int32, prob.shape, 0)
            row = lax.broadcasted_iota(jnp.int32, prob.shape, 1)
            prob = jnp.where(3 * slot + 2 <= 3 * (row % slots) + row // slots, prob, 0.0)
        scores.append((prob * (dprob - delta_ref[h : h + 1, :])).astype(narrow))
        probs.append(prob.astype(narrow))
    dk = nn(scores[0], qm_ref[0, :, cols]) + nn(scores[1], qm_ref[1, :, cols])
    dv = nn(probs[0], dm_ref[0, :, cols]) + nn(probs[1], dm_ref[1, :, cols])
    nothing = jnp.zeros_like(k)
    split_k = jnp.concatenate([jnp.where(lane < HEAD_DIM, k, nothing), jnp.where(lane >= HEAD_DIM, k, nothing)], 0)
    return dk, dv, tn(jnp.concatenate(scores, 0), split_k)


def attend_back_kernel(
    tab_ref, qm_ref, dm_ref, lse_ref, delta_ref, kv_ref, dq_ref, keep_ref, send_ref, *, list_at, pair
):
    half, slots, _ = keep_ref.shape

    def store(number, dk, dv):
        @pl.when(number < half)
        def _():
            keep_ref[number, :, :PAIR] = dk
            keep_ref[number, :, PAIR:] = dv

        @pl.when(number >= half)
        def _():
            send_ref[number - half, :, :PAIR] = dk
            send_ref[number - half, :, PAIR:] = dv

    def step(i, carry):
        number = tab_ref[list_at + 1 + i]
        dk, dv, dq = back_block(kv_ref, number, pair, qm_ref, dm_ref, lse_ref, delta_ref, False)
        dq_ref[...] += dq
        store(number, dk.astype(narrow), dv.astype(narrow))
        return carry

    def clear(i, carry):
        nothing = jnp.zeros((slots, PAIR), narrow)
        store(tab_ref[list_at + 1 + i], nothing, nothing)
        return carry

    dq_ref[...] = jnp.zeros(dq_ref.shape, single)
    keep_ref[0] = jnp.zeros((slots, 2 * PAIR), narrow)
    lax.fori_loop(0, tab_ref[list_at], step, 0)
    lax.fori_loop(tab_ref[list_at], 2 * half - 1, clear, 0)


def attend_back_own_kernel(qm_ref, dm_ref, lse_ref, delta_ref, kv_ref, *rest, first):
    dq_in, (dq_ref, out_ref) = rest[:-2], rest[-2:]
    group = out_ref.shape[1] // 2
    for i, ref in enumerate(dq_in):
        dk, dv, dq = back_block(kv_ref, 0, first + i, qm_ref, dm_ref, lse_ref, delta_ref, True)
        cols = slice(PAIR * i, PAIR * (i + 1))
        dq_ref[:, cols] = ref[...] + dq
        out_ref[:, cols] = dk
        out_ref[:, group + PAIR * i : group + PAIR * (i + 1)] = dv


def sum_split_kernel(*refs, count, last):
    total = refs[0][...].astype(single)
    for ref in refs[1:count]:
        total += ref[...].astype(single)
    total = total.astype(narrow)
    outs = refs[count:]
    size = (total.shape[0] - last) // len(outs)
    for i, out_ref in enumerate(outs):
        if i == len(outs) - 1:
            out_ref[...] = total[i * size :]
        else:
            out_ref[pl.ds(0, size)] = total[i * size : (i + 1) * size]
            if last:
                out_ref[pl.ds(size, last)] = total[len(outs) * size :]


def sum_last_kernel(*refs, count, last):
    total = refs[0][...].astype(single)
    for ref in refs[1:count]:
        total += ref[...].astype(single)
    size = total.shape[0] - last
    refs[count][...] = total[:size].astype(narrow)
    refs[count + 1][...] = total[size:]


def join_kernel(*refs):
    parts, out_ref = refs[:-1], refs[-1]
    size = parts[0].shape[0]
    for i, ref in enumerate(parts):
        out_ref[pl.ds(i * size, size)] = ref[...]


def group_split_kernel(*refs):
    totals, (keep_ref, send_ref) = refs[:-2], refs[-2:]
    pairs = len(totals)
    half = keep_ref.shape[0]
    for pair, ref in enumerate(totals):
        for number in range(2):
            cols = slice(number * PAIR, (number + 1) * PAIR)
            first = (number * pairs + pair) * PAIR
            keep_ref[:, :, first : first + PAIR] = ref[pl.ds(0, half), :, cols]
            send_ref[:, :, first : first + PAIR] = ref[pl.ds(half, half), :, cols]


def store_tiles(buf_ref, first, values):
    for t in range(values.shape[0] // TILE):
        buf_ref[first + t] = values[t * TILE : (t + 1) * TILE]


def start_split(buf_ref, keep_ref, send_ref, sems, last):
    half = (buf_ref.shape[0] - last) // 2
    copies = [
        pltpu.make_async_copy(buf_ref.at[pl.ds(0, half)], keep_ref.at[pl.ds(0, half)], sems.at[0]),
        pltpu.make_async_copy(buf_ref.at[pl.ds(half, half + last)], send_ref, sems.at[1]),
    ]
    if last:
        copies.append(
            pltpu.make_async_copy(buf_ref.at[pl.ds(2 * half, last)], keep_ref.at[pl.ds(half, last)], sems.at[2])
        )
    for copy in copies:
        copy.start()
    return copies


def split_out(buf_ref, keep_ref, send_ref, sems, last):
    for copy in start_split(buf_ref, keep_ref, send_ref, sems, last):
        copy.wait()


def conv_grads(tab_ref, buf_ref, tk_ref, tv_ref, grad, tiles, pieces, inverse_at):
    width = tk_ref.shape[1]
    slots = grad.shape[0]
    group = grad.shape[1] // 2
    conv_tiles = TAPS * width // pieces // TILE
    for i in range(TAPS):
        own = slice(i * slots, (i + 1) * slots)
        both = jnp.concatenate([tn(tk_ref[own], grad[:, :group]), tn(tv_ref[own], grad[:, group:])], 1).astype(narrow)
        for j in range(width // TILE):
            tile = i * (width // TILE) + j
            at = tab_ref[inverse_at + tile // conv_tiles] * tiles + tile % conv_tiles
            for c in range(2 * group // COLUMNS):
                buf_ref[at + c * conv_tiles] = both[j * TILE : (j + 1) * TILE, c * COLUMNS : (c + 1) * COLUMNS]


def weight_grads(tab_ref, buf_ref, grad, first, tiles, pieces, inverse_at):
    for j in range(pieces):
        at = tab_ref[inverse_at + j] * tiles + first
        for c in range(grad.shape[1] // COLUMNS):
            buf_ref[at + c] = grad[j * TILE : (j + 1) * TILE, c * COLUMNS : (c + 1) * COLUMNS]


def middle_kernel(
    tab_ref, qm_ref, dm_ref, lse_ref, delta_ref, kv_ref, tk_ref, tv_ref, first_ref, second_ref, gw_out_ref, ck_ref, cv_ref,
    *rest, pieces, inverse_at,
):
    dq_refs, (gk_ref, gv_ref, dq_ref, keep_ref, send_ref, buf_ref, own_s, sems) = rest[:-8], rest[-8:]
    attend_back_own_kernel(qm_ref, dm_ref, lse_ref, delta_ref, kv_ref, *dq_refs, dq_ref, own_s, first=0)
    tiles = buf_ref.shape[0] // pieces
    blocks = gw_out_ref.shape[1] // COLUMNS
    grad = slot_grads(first_ref, second_ref, own_s)
    conv_grads(tab_ref, buf_ref, tk_ref, tv_ref, grad, tiles, pieces, inverse_at)
    weight_grads(tab_ref, buf_ref, gw_out_ref, tiles - blocks, tiles, pieces, inverse_at)
    copies = start_split(buf_ref, keep_ref, send_ref, sems, 0)
    conv_back(grad, ck_ref, cv_ref, 0, gk_ref, gv_ref)
    for copy in copies:
        copy.wait()


def tail_query_kernel(hid_ref, tk_ref, ods_ref, wq_ref, early_ref, later_ref, gh_ref, gw_ref):
    own_ds = tn(ods_ref[...], head_rows(tk_ref.shape[1])) * scale
    dq = jnp.concatenate([early_ref[...], later_ref[...]], 1)
    gq = (dq * scale + own_ds * tk_ref[...].astype(single)).astype(narrow)
    gw_ref[...] = tn(hid_ref[...], gq).astype(narrow)
    gh_ref[...] = nt(gq, wq_ref[...])


def slot_grads(*refs):
    return sum(ref[...].astype(single) for ref in refs).astype(narrow)


def conv_back(grads, ck_ref, cv_ref, first, gk_ref, gv_ref):
    slots, width = grads.shape[0], ck_ref.shape[1]
    group = grads.shape[1] // 2
    for grad, c_ref, out_ref in ((grads[:, :group], ck_ref, gk_ref), (grads[:, group:], cv_ref, gv_ref)):
        for i in range(TAPS):
            out_ref[i * slots : (i + 1) * slots] = nt(grad, c_ref[i * width : (i + 1) * width, first : first + group])


def tail_kernel(
    tab_ref, x_ref, hid_ref, q_ref, tk_ref, tv_ref, ga_ref, gm_ref, own_ref, ods_ref, gh_ref, gk0_ref, gv0_ref,
    first_ref, second_ref, own_grad_ref, gwq_ref, wk_ref, wv_ref, ck_ref, cv_ref, gain_ref, gx_ref, keep_ref, send_ref, buf_ref, gk_s, gv_s, sems, *, pieces, inverse_at,
):
    rows, width = x_ref.shape
    tiles = (buf_ref.shape[0] - 1) // pieces
    blocks = width // COLUMNS
    grad = slot_grads(first_ref, second_ref, own_grad_ref)
    conv_grads(tab_ref, buf_ref, tk_ref, tv_ref, grad, tiles, pieces, inverse_at)
    marks = head_rows(width)
    own_ds = tn(ods_ref[...], marks) * scale
    own_prob = tn(own_ref[...].astype(narrow), marks)
    conv_back(grad, ck_ref, cv_ref, width - grad.shape[1] // 2, gk_s, gv_s)
    gk = (gk_s[...] + gk0_ref[...] + own_ds * q_ref[...].astype(single)).astype(narrow)
    gv = (gv_s[...] + gv0_ref[...] + own_prob * ga_ref[...].astype(single)).astype(narrow)
    weight_grads(tab_ref, buf_ref, gwq_ref, tiles - 3 * blocks, tiles, pieces, inverse_at)
    hidden_t = hid_ref[...].T
    grad_hidden = gh_ref[...]
    for number, grad in enumerate((gk, gv)):
        grad_w = nn(hidden_t, grad).astype(narrow)
        weight_grads(tab_ref, buf_ref, grad_w, tiles - (2 - number) * blocks, tiles, pieces, inverse_at)
        grad_hidden += nt(grad, (wk_ref, wv_ref)[number][...])
    unit, spread = standardized(x_ref[...].astype(single))
    place = lax.broadcasted_iota(jnp.int32, (TILE, COLUMNS), 0)
    sums = jnp.zeros((TILE, COLUMNS), single)
    for first, value in ((0, grad_hidden * unit), (blocks, grad_hidden)):
        total = jnp.sum(value, 0, keepdims=True)
        for c in range(blocks):
            sums = jnp.where(place == first + c, total[:, c * COLUMNS : (c + 1) * COLUMNS], sums)
    buf_ref[buf_ref.shape[0] - 1] = sums.astype(narrow)
    split_out(buf_ref, keep_ref, send_ref, sems, 1)
    gx_ref[...] = (gm_ref[...] + norm_back(grad_hidden, unit, spread, gain_ref[...])).astype(narrow)


def unpack_feed_kernel(
    tab_ref, own_ref, other_ref, small_ref, wd_ref, wu_ref, gain_ref, bias_ref, up_ref, down_ref, *, pieces, piece_at
):
    width = wd_ref.shape[1]
    down_rows = wd_ref.shape[0] // pieces
    down_tiles, up_tiles = down_rows // TILE, wu_ref.shape[1] // width
    tiles = down_tiles + up_tiles
    down_ref[...] = small_ref[0, 0:1, :]
    for t in range(up_tiles):
        up_ref[:, t * width : (t + 1) * width] = small_ref[0, 1 + t : 2 + t, :]
    gain_ref[...] = small_ref[0, 1 + up_tiles : 2 + up_tiles, :]
    bias_ref[...] = small_ref[0, 2 + up_tiles : 3 + up_tiles, :]

    for number, buf_ref in enumerate((own_ref, other_ref)):

        def step(k, carry, number=number, buf_ref=buf_ref):
            piece = tab_ref[piece_at + number * pieces // 2 + k]
            at = k * tiles
            for t in range(down_tiles):
                rows = pl.ds(pl.multiple_of(piece * down_rows + t * TILE, TILE), TILE)
                wd_ref[rows, :] = buf_ref[at + t].astype(single)
            mine = pl.ds(pl.multiple_of(piece * TILE, TILE), TILE)
            for t in range(up_tiles):
                wu_ref[mine, t * width : (t + 1) * width] = buf_ref[at + down_tiles + t].astype(single)
            return carry

        lax.fori_loop(0, pieces // 2, step, 0, unroll=4)


def unpack_kernel(tab_ref, *rest, parts, half, piece_at, first_column, outs, small):
    bufs, rest = rest[: len(parts)], rest[len(parts) :]
    if small:
        small_ref, small_outs, rest = rest[0], rest[-5 - outs : -3 - outs], rest[1:]
        for i, ref in enumerate(small_outs):
            ref[...] = small_ref[0, i : i + 1, :]
    out_refs, (conv_s, weight_s, sems) = rest[-outs - 3 : -3], rest[-3:]
    weight_refs, conv_refs = out_refs[:-2], out_refs[-2:]
    conv_rows, columns = conv_s.shape[2], conv_s.shape[3]
    conv_tiles = conv_rows // TILE
    blocks = weight_s.shape[3] // COLUMNS
    weights_at = conv_tiles * (2 * columns // COLUMNS)
    tiles = weights_at + blocks * len(weight_refs)

    def copies(number, place):
        piece = tab_ref[piece_at + place]
        rows = pl.ds(pl.multiple_of(piece * conv_rows, TILE), conv_rows)
        mine = pl.ds(pl.multiple_of(piece * TILE, TILE), TILE)
        cols = pl.ds(first_column, columns)
        return [
            pltpu.make_async_copy(conv_s.at[number, i], ref.at[rows, cols], sems.at[number, i])
            for i, ref in enumerate(conv_refs)
        ] + [
            pltpu.make_async_copy(weight_s.at[number, i], ref.at[mine], sems.at[number, 2 + i])
            for i, ref in enumerate(weight_refs)
        ]

    for order, (buf_ref, part) in enumerate(zip(bufs, parts)):

        def step(k, carry, order=order, buf_ref=buf_ref, part=part):
            number = order * half + k
            for t in range(conv_tiles):
                for unit in range(2 * columns // PAIR):
                    which, first = unit * PAIR // columns, unit * PAIR % columns
                    block, lanes = unit * PAIR // COLUMNS, unit * PAIR % COLUMNS
                    conv_s[number, which, t * TILE : (t + 1) * TILE, first : first + PAIR] = buf_ref[
                        k * tiles + block * conv_tiles + t, :, lanes : lanes + PAIR
                    ].astype(single)
            for t in range(len(weight_refs)):
                for c in range(blocks):
                    weight_s[number, t, :, c * COLUMNS : (c + 1) * COLUMNS] = buf_ref[
                        k * tiles + weights_at + t * blocks + c
                    ].astype(single)
            for copy in copies(number, part * half + k):
                copy.start()
            return carry

        lax.fori_loop(0, half, step, 0)

    for order, part in enumerate(parts):

        def finish(k, carry, order=order, part=part):
            for copy in copies(order * half + k, part * half + k):
                copy.wait()
            return carry

        lax.fori_loop(0, half, finish, 0)


def shaped(shape, kind):
    return jax.ShapeDtypeStruct(shape, kind)


def per_device(
    seq_size, batch_size,
    inputs, cotangent, ln1_gain, ln1_bias, w_query, w_key, w_value, conv_key, conv_value, w_out,
    ln2_gain, ln2_bias, w_up, up_bias, w_down, down_bias,
):
    x, g = inputs[0], cotangent[0]
    rows, width = x.shape
    slots = rows // TAPS
    ff = w_up.shape[1]
    seq_bits, batch_bits = seq_size.bit_length() - 1, batch_size.bit_length() - 1
    split_bits = min(5, seq_bits + batch_bits)
    pieces = 1 << split_bits
    list_at = seq_size
    piece_at = list_at + seq_size
    inverse_at = piece_at + pieces
    tables = jnp.asarray(plan_tables(seq_size, batch_size, split_bits))
    table = lax.dynamic_index_in_dim(
        tables, lax.axis_index("seq") * batch_size + lax.axis_index("batch"), 0, keepdims=False
    )
    x = tied(x, table)
    row = lambda v: v.reshape(1, -1)
    ck = conv_key.reshape(TAPS * width, width)
    cv = conv_value.reshape(TAPS * width, width)
    token_low, token_wide = shaped((rows, width), narrow), shaped((rows, width), single)
    head_wide, head_low = shaped((HEADS, rows), single), shaped((HEADS, rows), narrow)
    two_low = shaped((2, rows, width), narrow)

    xp, hidden, tk, tv, kv = call(
        "front",
        front_kernel,
        (token_low,) * 4 + (shaped((slots, 2 * width), narrow),),
        loads=(x, row(ln1_gain), row(ln1_bias), w_key, ck, w_value, cv),
        mib=24,
        flops=4e9,
    )

    state = shaped((HEADS, rows, PAIR), single)
    q, gp, qm, own, m, acc = call(
        "attend_own",
        attend_own_kernel,
        (token_low, token_low, two_low, head_wide, state, state),
        loads=(w_query, g),
        operands=(hidden, tk, tv, kv[None]),
        mib=16,
        flops=1e10,
    )
    blocks = {0: kv[None]}
    rounds = gather_plan(seq_size)
    calls = []
    for number, found in enumerate(rounds):
        if number > 0:
            calls.append([entry[0] for entry in rounds[number - 1]])
        held = {source: blocks[source] for _, source, _ in found if source in blocks}
        if number > 1:
            held = tied(held, m)
        for block, source, (axis, pairs) in found:
            if source in held:
                blocks[block] = lax.ppermute(held[source], axis, pairs)
        if number == 0:
            continue
        later = [entry for entry in found if entry[0] not in blocks]
        halves = [[k for k in calls[-1] if k < seq_size // 2], [k for k in calls[-1] if k >= seq_size // 2]]
        for found in halves:
            if not found:
                continue
            m, acc = call(
                f"attend_{found[0]}",
                functools.partial(attend_more_kernel, blocks=found),
                (state, state),
                table=table,
                operands=(qm, m, acc, *[blocks[k] for k in found]),
                mib=8,
                flops=1e11,
            )
            if later:
                for block, source, (axis, pairs) in later:
                    blocks[block] = lax.ppermute(tied(blocks[source], m), axis, pairs)
                later = []
    calls.append([entry[0] for entry in rounds[-1]])
    attended, lse, own_prob = call(
        "attend_last",
        functools.partial(attend_last_kernel, blocks=calls[-1]),
        (token_wide, head_wide, head_wide),
        table=table,
        operands=(qm, own, m, acc, *[blocks[k] for k in calls[-1]]),
        scratch=[pltpu.VMEM(state.shape, single), pltpu.VMEM(state.shape, single)],
        mib=16,
        flops=1e10 * len(calls[-1]),
    )

    steps = ff // width
    tiles = ff // pieces // TILE + steps
    half = shaped((pieces // 2 * tiles + 1, TILE, width), narrow)
    output, middle, grad_normal, keep, send, all_kv = call(
        "feed",
        functools.partial(feed_kernel, pieces=pieces, inverse_at=inverse_at),
        (token_low, token_wide, token_wide, half, half, shaped((seq_size, slots, 2 * width), narrow)),
        loads=(row(ln2_gain), row(ln2_bias), w_up, row(up_bias), w_down, row(down_bias)),
        table=table,
        operands=(xp, attended, gp, w_out),
        away=[blocks[k] for k in range(seq_size)],
        away_outs=3,
        scratch=[
            pltpu.VMEM((rows, width), narrow),
            pltpu.VMEM((width, rows), narrow),
            pltpu.VMEM((rows, width), single),
            pltpu.VMEM((pieces * tiles + 1, TILE, width), narrow),
            pltpu.SemaphoreType.DMA((3 + seq_size,)),
        ],
        mib=30,
        flops=5e10,
    )
    grad_middle, grad_w_out_here, grad_attended, dm, delta, own_ds = call(
        "branch",
        branch_kernel,
        (token_wide, shaped((width, width), narrow), token_low, two_low, head_wide, head_low),
        loads=(row(ln2_gain),),
        operands=(middle, grad_normal, gp, attended, tv, own_prob, w_out),
        mib=16,
        flops=1e11,
    )

    stages = reduce_stages(seq_size, batch_size, split_bits)
    gather_back = [stage for stage in stages if stage[0] > 1][::-1]
    unseen = gather_stages(seq_size)[::-1]
    head_pairs = HEADS // 2

    wide_grant = 12 if seq_size <= 8 else 56
    share = shaped((seq_size // 2, slots, 2 * PAIR), narrow)

    def back(pair, qm):
        return call(
            f"attend_back_{pair}",
            functools.partial(attend_back_kernel, list_at=list_at, pair=pair),
            (shaped((rows, PAIR), single), share, share),
            table=table,
            operands=(qm, dm, lse, delta, all_kv),
            mib=wide_grant,
            flops=1e11,
        )

    def small_call(kernel, name, outs, *operands):
        return call(name, kernel, outs, operands=operands, mib=4, flops=sum(v.size for v in operands) * 600)

    def sum_split(buffers, last, cut):
        count, rest = buffers[0].shape[0], buffers[0].shape[1:]
        outs = (shaped(((count - last) // cut + last, *rest), narrow),) * cut
        kernel = functools.partial(sum_split_kernel, count=len(buffers), last=last)
        return small_call(kernel, "sum_split", outs, *buffers)

    def join(*parts):
        out = shaped((len(parts) * parts[0].shape[0], *parts[0].shape[1:]), narrow)
        return small_call(join_kernel, "join", (out,), *parts)[0]

    def exchange(stage, parts):
        return [lax.ppermute(part, stage[1], pairs) for part, pairs in zip(parts, stage[2])]

    class Sum:
        def __init__(self, keep, send, last):
            self.keep, self.last, self.at = keep, last, 0
            self.arrived = exchange(stages[0], [send])

        def step(self, *others):
            arrived = tied(self.arrived, *others)
            self.at += 1
            if self.at < len(stages):
                cut = stages[self.at][0]
                parts = sum_split((self.keep, *arrived), self.last, cut)
                self.keep, sent = parts[0], parts[1:] if cut > 1 else parts
                self.arrived = exchange(stages[self.at], sent)
                return sent[0]
            if self.at == len(stages):
                buffers = (self.keep, *arrived)
                if self.last:
                    count, rest = buffers[0].shape[0], buffers[0].shape[1:]
                    outs = (shaped((count - self.last, *rest), narrow), shaped((self.last, *rest), single))
                    kernel = functools.partial(sum_last_kernel, count=len(buffers), last=self.last)
                    self.held, self.small = small_call(kernel, "sum_last", outs, *buffers)
                else:
                    (self.held,) = sum_split(buffers, 0, 1)
            else:
                self.held = join(self.held, *arrived)
            stage = gather_back[self.at - len(stages)]
            self.arrived = exchange(stage, [self.held] * len(stage[2]))
            return self.held

        def left(self):
            return len(stages) + len(gather_back) - 1 - self.at

    class Group:
        def __init__(self):
            self.shares, self.at = [], 0

        def step(self, *others):
            self.at += 1
            if self.at == 1:
                operands = tied(self.shares, *others)
                half = shaped((seq_size // 4, slots, len(self.shares) * 2 * PAIR), narrow)
                self.keep, send = small_call(group_split_kernel, "group_split", (half, half), *operands)
            else:
                self.keep, send = sum_split((self.keep, tied(self.arrived, *others)), 0, 2)
            self.arrived = lax.ppermute(send, *unseen[self.at])
            return send

        def left(self):
            return len(unseen) - 1 - self.at

    conv_tiles = TAPS * width // pieces // TILE
    blocks_wide = width // COLUMNS
    first_tiles, tail_tiles = (
        conv_tiles * (group * 2 * PAIR // COLUMNS) + count * blocks_wide for group, count in zip(GROUPS, (1, 3))
    )

    sums = {"feed": Sum(keep, send, 1)}
    first_group, second_group = Group(), Group()
    waits = [sums["feed"].step(delta)]
    state_back = {"grads": []}

    def advance(name, kept=0):
        if name in sums and sums[name].left() > kept:
            waits.append(sums[name].step(*waits))

    def advance_group(group):
        if group.left() > 0:
            waits.append(group.step(*waits))

    def add_share(group, kept, arrived):
        (total,) = sum_split(tied((kept, arrived), *waits), 0, 1)
        waits.append(total)
        group.shares.append(total)

    partial_q, pending = [], None
    for pair in range(head_pairs):
        in_first = pair < GROUPS[0]
        grads, kept, sent = back(pair, tied(qm, *waits))
        waits = [grads]
        partial_q.append(grads)
        if pair < head_pairs - 1:
            advance("feed", 1)
        if pending is not None:
            add_share(*pending)
        pending = (first_group if in_first else second_group, kept, lax.ppermute(sent, *unseen[0]))
        if pair >= GROUPS[0]:
            advance_group(first_group)
    def own_block(first, count):
        return call(
            f"attend_back_own_{first}",
            functools.partial(attend_back_own_kernel, first=first),
            (shaped((rows, count * PAIR), single), shaped((slots, count * 2 * PAIR), single)),
            operands=(tied(qm, *waits), dm, lse, delta, kv[None], *partial_q[first : first + count]),
            mib=12,
            flops=1e11,
        )

    later_q, second_own = own_block(GROUPS[0], GROUPS[1])
    waits = [later_q]
    add_share(*pending)
    advance_group(second_group)
    advance("feed", 1)
    while first_group.left() > 0:
        advance_group(first_group)
    half = shaped((pieces // 2 * first_tiles, TILE, COLUMNS), narrow)
    grad_k, grad_v, early_q, keep0, send0 = call(
        "middle",
        functools.partial(middle_kernel, pieces=pieces, inverse_at=inverse_at),
        (token_wide, token_wide, shaped((rows, GROUPS[0] * PAIR), single), half, half),
        table=table,
        operands=(
            tied(qm, *waits), dm, lse, delta, kv[None], tk, tv, first_group.keep[0], first_group.arrived[0],
            grad_w_out_here, ck, cv, *partial_q[: GROUPS[0]],
        ),
        away_outs=2,
        scratch=[
            pltpu.VMEM((pieces * first_tiles, TILE, COLUMNS), narrow),
            pltpu.VMEM((slots, GROUPS[0] * 2 * PAIR), single),
            pltpu.SemaphoreType.DMA((3,)),
        ],
        mib=24,
        flops=1e11,
    )
    sums["first"] = Sum(keep0, send0, 0)
    waits = [grad_k]
    advance("feed", 1)
    advance_group(second_group)
    grad_hidden, grad_wq_here = call(
        "tail_query",
        tail_query_kernel,
        (token_wide, shaped((width, width), narrow)),
        operands=(tied(hidden, *waits), tk, own_ds, w_query, early_q, later_q),
        mib=16,
        flops=1e11,
    )
    waits = [grad_hidden]
    while second_group.left() > 0:
        advance_group(second_group)
    advance("first")
    half = shaped((pieces // 2 * tail_tiles + 1, TILE, COLUMNS), narrow)
    grad_x, keep1, send1 = call(
        "tail",
        functools.partial(tail_kernel, pieces=pieces, inverse_at=inverse_at),
        (token_low, half, half),
        table=table,
        operands=(
            xp, hidden, q, tk, tv, grad_attended, grad_middle, own_prob, own_ds, grad_hidden, grad_k, grad_v,
            tied(second_group.keep[0], *waits), second_group.arrived[0], second_own, grad_wq_here,
            w_key, w_value, ck, cv, row(ln1_gain),
        ),
        away_outs=2,
        scratch=[
            pltpu.VMEM((pieces * tail_tiles + 1, TILE, COLUMNS), narrow),
            pltpu.VMEM((rows, width), single),
            pltpu.VMEM((rows, width), single),
            pltpu.SemaphoreType.DMA((3,)),
        ],
        mib=26,
        flops=1e11,
    )
    sums["second"] = Sum(keep1, send1, 1)
    waits = [grad_x]

    def unpack(name, parts, heads, weights, bufs, *known, small=()):
        count = len(parts) * pieces // 2
        outs = [shaped((width, width), single)] * weights + [shaped(ck.shape, single)] * 2
        first = [shaped((1, width), single)] * (2 * len(small))
        return call(
            name,
            functools.partial(
                unpack_kernel,
                parts=parts,
                half=pieces // 2,
                piece_at=piece_at,
                first_column=heads[0] * PAIR,
                outs=len(outs),
                small=len(small),
            ),
            first + outs,
            table=table,
            operands=(*bufs, *small),
            away=known,
            away_outs=len(outs),
            in_place=len(known),
            scratch=[
                pltpu.VMEM((count, 2, conv_tiles * TILE, heads[1] * PAIR), single),
                pltpu.VMEM((count, weights, TILE, width), single),
                pltpu.SemaphoreType.DMA((count, len(outs))),
            ],
            mib=20,
            flops=1e11,
        )

    def finish_feed(*others):
        vector = shaped((1, width), single)
        return call(
            "unpack_feed",
            functools.partial(unpack_feed_kernel, pieces=pieces, piece_at=piece_at),
            (shaped((ff, width), single), shaped((width, ff), single), vector, vector, shaped((1, ff), single), vector),
            table=table,
            operands=(sums["feed"].held, tied(sums["feed"].arrived[0], *others), sums["feed"].small),
            mib=16,
            flops=2e10,
        )

    places = (GROUPS[0], GROUPS[1])
    for action in "F0R010010101F0111F01Uu1":
        if action in "01F":
            advance({"0": "first", "1": "second", "F": "feed"}[action])
            waits = waits[-1:]
        elif action == "R":
            output, grad_x = call(
                "reorder",
                reorder_kernel,
                (token_low, token_low),
                operands=(output, tied(grad_x, *waits)),
                mib=8,
                flops=1e11,
            )
            waits.append(grad_x)
        elif action == "U":
            while sums["feed"].left() > 0:
                advance("feed")
            grad_w_down, grad_w_up, *small_feed = finish_feed(*waits)
            waits.append(grad_w_up)
        elif action == "u":
            while sums["first"].left() > 0:
                advance("first")
            while sums["second"].left() > 1:
                advance("second")
            grad_w_out, *convs = unpack(
                "unpack_first",
                (0, 1),
                (0, GROUPS[0]),
                1,
                (sums["first"].held, tied(sums["first"].arrived[0], *waits)),
            )
            waits.append(grad_w_out)
    last = sums["second"]
    small_first, small_second, *found = unpack(
        "unpack_own", (0,), places, 3, (last.held,), *tied(convs, *waits), small=(last.small,)
    )
    grad_wq, grad_wk, grad_wv, grad_ck, grad_cv = unpack(
        "unpack_last", (1,), places, 3, (last.arrived[0],), *found
    )
    return (
        output[None],
        grad_x[None],
        small_first[0],
        small_second[0],
        grad_wq,
        grad_wk,
        grad_wv,
        grad_ck.reshape(conv_key.shape),
        grad_cv.reshape(conv_value.shape),
        grad_w_out,
        small_feed[0][0],
        small_feed[1][0],
        grad_w_up,
        small_feed[2][0],
        grad_w_down,
        small_feed[3][0],
    )


def solution(mesh):
    placed = (P("batch", "seq", None),) * 2 + (P(),) * 14
    return jax.shard_map(
        functools.partial(per_device, mesh.shape["seq"], mesh.shape["batch"]),
        mesh=mesh,
        in_specs=placed,
        out_specs=placed,
        check_vma=False,
    )
```

```python
import functools

import jax
import jax.numpy as jnp
import numpy as np
from jax import lax
from jax.experimental import pallas as pl
from jax.experimental.pallas import tpu as pltpu
from jax.sharding import PartitionSpec as P

HEADS = 8
HEAD_DIM = 64
PAIR = 2 * HEAD_DIM
TAPS = 3
TILE = 16
COLUMNS = 512
GROUPS = (2, 2)

epsilon = 1e-05
narrow = jnp.bfloat16
single = jnp.float32
scale = HEAD_DIM ** (-0.5)

vmem = pl.BlockSpec(memory_space=pltpu.VMEM)
smem = pl.BlockSpec(memory_space=pltpu.SMEM)
anywhere = pl.BlockSpec(memory_space=pl.ANY)
hbm = pl.BlockSpec(memory_space=pltpu.HBM)


def params(mib):
    return pltpu.CompilerParams(vmem_limit_bytes=mib * 2**20)


def cost(flops, moved):
    return pl.CostEstimate(flops=int(flops), bytes_accessed=int(moved), transcendentals=0)


class Loads:
    def __init__(self, sources, held, sems):
        self.held, self.waited = held, set()
        self.copies = [pltpu.make_async_copy(a, b, sems.at[i]) for i, (a, b) in enumerate(zip(sources, held))]
        for copy in self.copies:
            copy.start()

    def __getitem__(self, i):
        if i not in self.waited:
            self.copies[i].wait()
            self.waited.add(i)
        return self.held[i]


def call(
    name, body, outs, *, loads=(), table=None, operands=(), away=(), away_outs=0, in_place=0, scratch=(), mib, flops
):
    count = len(loads)
    inputs = count + (table is not None) + len(operands) + len(away)

    def kernel(*refs):
        sources, rest = refs[:count], refs[count:]
        if count == 0:
            return body(*rest)
        held, sems = rest[-count - 1 : -1], rest[-1]
        return body(Loads(sources, held, sems), *rest[: -count - 1])

    moved = sum(v.size * 2 for v in (*loads, *operands, *away, *outs))
    scratch = list(scratch)
    if count:
        scratch += [pltpu.VMEM(v.shape, v.dtype) for v in loads] + [pltpu.SemaphoreType.DMA((count,))]
    return pl.pallas_call(
        kernel,
        out_shape=tuple(outs),
        in_specs=[hbm] * count + [smem] * (table is not None) + [vmem] * len(operands) + [anywhere] * len(away),
        out_specs=(vmem,) * (len(outs) - away_outs) + (anywhere,) * away_outs,
        scratch_shapes=scratch,
        input_output_aliases={inputs - in_place + i: len(outs) - in_place + i for i in range(in_place)},
        compiler_params=params(mib),
        cost_estimate=cost(flops, moved),
        name=name,
    )(
        *[pltpu.with_memory_space_constraint(v, pltpu.HBM) for v in loads],
        *([] if table is None else [table]),
        *operands,
        *away,
    )


def tied(values, *others):
    return lax.optimization_barrier((values, others))[0]


def nn(a, b):
    return lax.dot_general(a, b, (((1,), (0,)), ((), ())), preferred_element_type=single)


def nt(a, b):
    return lax.dot_general(a, b, (((1,), (1,)), ((), ())), preferred_element_type=single)


def tn(a, b):
    return lax.dot_general(a, b, (((0,), (0,)), ((), ())), preferred_element_type=single)


def bit_masks(size):
    return [1 << b for b in range(size.bit_length() - 1)]


def seq_masks(size, core):
    masks = bit_masks(size)[1:]
    return masks if core == 0 else masks[::-1]


def seq_swap(size, stage):
    return [(i, i ^ seq_masks(size, i & 1)[stage]) for i in range(size)]


def gather_stages(seq_size):
    found = [("seq", seq_swap(seq_size, j)) for j in range(len(bit_masks(seq_size)) - 1)]
    return found + [("seq", [(i, i ^ 1) for i in range(seq_size)])]


def reduce_stages(seq_size, batch_size, split_bits):
    found = [(2, "seq", [[(i, i ^ 1) for i in range(seq_size)]])]
    found += [(2, "seq", [seq_swap(seq_size, j)]) for j in range(len(bit_masks(seq_size)) - 1)]
    split = split_bits - len(found)
    for j, mask in enumerate(bit_masks(batch_size)):
        found.append((2 if j < split else 1, "batch", [[(i, i ^ mask) for i in range(batch_size)]]))
    return found


def gather_origin(seq_size, me, block):
    count = len(bit_masks(seq_size)) - 1
    core_bit = (block >> count) & 1
    other = me ^ core_bit
    masks = seq_masks(seq_size, other & 1)
    for j in range(count):
        if (block >> j) & 1:
            other ^= masks[j]
    return other


def piece_of(seq_size, batch_size, split_bits, me_seq, me_batch, place):
    bits = [(place >> (split_bits - 1 - j)) & 1 for j in range(split_bits)]
    s = me_seq ^ bits[0]
    masks = seq_masks(seq_size, s & 1)
    z = me_batch
    for j, b in enumerate(bits[1:]):
        if j < len(masks):
            s ^= masks[j] * b
        else:
            z ^= (1 << (j - len(masks))) * b
    low_batch = z & ((1 << (split_bits - len(bit_masks(seq_size)))) - 1)
    return s + seq_size * low_batch


def gather_plan(seq_size):
    stages = gather_stages(seq_size)
    count = len(stages) - 1
    rounds = [[] for _ in range(count + 1)]
    for block in range(1, 1 << count):
        last = block.bit_length() - 1
        rounds[bin(block).count("1")].append((block, block ^ (1 << last), stages[last]))
    for found in rounds:
        blocks = [entry[0] for entry in found] or [0]
        found += [(block | (1 << count), block, stages[-1]) for block in blocks]
    return rounds


def plan_tables(seq_size, batch_size, split_bits):
    rows = []
    pieces = 1 << split_bits
    for s in range(seq_size):
        origins = [gather_origin(seq_size, s, k) for k in range(seq_size)]
        seen = [int(origin < s) for origin in origins]
        visible = [k for k in range(seq_size) if origins[k] < s]
        lists = [len(visible)] + visible + [k for k in range(seq_size) if origins[k] > s]
        for z in range(batch_size):
            places = [piece_of(seq_size, batch_size, split_bits, s, z, k) for k in range(pieces)]
            inverse = [places.index(p) for p in range(pieces)]
            rows.append(seen + lists + places + inverse)
    return np.asarray(rows, np.int32)


def token_order(rows):
    slots = rows // TAPS
    r = lax.broadcasted_iota(jnp.int32, (rows, rows), 0)
    c = lax.broadcasted_iota(jnp.int32, (rows, rows), 1)
    return jnp.where(c == TAPS * (r % slots) + r // slots, 1.0, 0.0).astype(narrow)


def head_rows(width):
    r = lax.broadcasted_iota(jnp.int32, (HEADS, width), 0)
    c = lax.broadcasted_iota(jnp.int32, (HEADS, width), 1)
    return jnp.where(c // HEAD_DIM == r, 1.0, 0.0).astype(narrow)


def head_sums(values):
    marks = head_rows(values.shape[1])
    high = values.astype(narrow)
    rest = values - high.astype(single)
    middle = rest.astype(narrow)
    low = (rest - middle.astype(single)).astype(narrow)
    return nt(marks, high) + nt(marks, middle) + nt(marks, low)


def standardized(values):
    centred = values - jnp.mean(values, -1, keepdims=True)
    spread = lax.rsqrt(jnp.mean(centred * centred, -1, keepdims=True) + epsilon)
    return centred * spread, spread


def norm_back(grad, unit, spread, gain):
    inner = grad * gain
    return spread * (
        inner
        - jnp.mean(inner, -1, keepdims=True)
        - unit * jnp.mean(inner * unit, -1, keepdims=True)
    )


def front_kernel(loads, xp_ref, hid_ref, tk_ref, tv_ref, kv_ref):
    rows, width = xp_ref.shape
    slots = rows // TAPS
    order = token_order(rows)
    x = nn(order, loads[0][...])
    xp_ref[...] = x.astype(narrow)
    unit, _ = standardized(x)
    hidden = (unit * loads[1][...] + loads[2][...]).astype(narrow)
    hid_ref[...] = hidden
    for number, t_ref in enumerate((tk_ref, tv_ref)):
        t = nn(hidden, loads[3 + 2 * number][...]).astype(narrow)
        t_ref[...] = t
        c_ref = loads[4 + 2 * number]
        total = nn(t[:slots], c_ref[:width])
        for i in range(1, TAPS):
            total += nn(t[i * slots : (i + 1) * slots], c_ref[i * width : (i + 1) * width])
        kv_ref[:, number * width : (number + 1) * width] = total.astype(narrow)


def attend_block(kv_ref, number, qm_ref, m_ref, acc_ref, diagonal):
    slots, width = kv_ref.shape[1], qm_ref.shape[2]
    lane = lax.broadcasted_iota(jnp.int32, (1, PAIR), 1)
    for h in range(HEADS):
        cols = slice(PAIR * (h // 2), PAIR * (h // 2 + 1))
        keep = (lane < HEAD_DIM) if h % 2 == 0 else (lane >= HEAD_DIM)
        v = kv_ref[number, :, width + cols.start : width + cols.stop]
        v_ones = jnp.where(keep, v, jnp.ones_like(v))
        s = nt(qm_ref[h % 2, :, cols], kv_ref[number, :, cols])
        if diagonal:
            slot = lax.broadcasted_iota(jnp.int32, s.shape, 1)
            row = lax.broadcasted_iota(jnp.int32, s.shape, 0)
            s = jnp.where(3 * slot + 2 <= 3 * (row % slots) + row // slots, s, -1e30)
        before = m_ref[h]
        after = jnp.maximum(before, jnp.max(s, 1, keepdims=True))
        m_ref[h] = after
        p = jnp.exp(s - jnp.concatenate([after] * (slots // PAIR), 1))
        acc_ref[h] = acc_ref[h] * jnp.exp(before - after) + nn(p.astype(narrow), v_ones)


def split_heads(values, out_ref):
    lanes = lax.broadcasted_iota(jnp.int32, (1, values.shape[1]), 1) % PAIR
    nothing = jnp.zeros_like(values)
    out_ref[0] = jnp.where(lanes < HEAD_DIM, values, nothing)
    out_ref[1] = jnp.where(lanes >= HEAD_DIM, values, nothing)


def attend_own_kernel(loads, hid_ref, tk_ref, tv_ref, kv_ref, q_ref, gp_ref, qm_ref, own_ref, m_ref, acc_ref):
    rows, width = hid_ref.shape
    q_low = nn(hid_ref[...], loads[0][...]).astype(narrow)
    q_ref[...] = q_low
    q = q_low.astype(single)
    split_heads((q * scale).astype(narrow), qm_ref)
    own = head_sums(q * tk_ref[...].astype(single)) * scale
    own_ref[...] = own
    own_cols = own.T
    lane = lax.broadcasted_iota(jnp.int32, (1, PAIR), 1)
    for h in range(HEADS):
        keep = (lane < HEAD_DIM) if h % 2 == 0 else (lane >= HEAD_DIM)
        m_ref[h] = jnp.broadcast_to(own_cols[:, h : h + 1], (rows, PAIR))
        acc_ref[h] = jnp.where(keep, tv_ref[:, PAIR * (h // 2) : PAIR * (h // 2 + 1)].astype(single), 1.0)
    attend_block(kv_ref, 0, qm_ref, m_ref, acc_ref, True)
    gp_ref[...] = nn(token_order(rows), loads[1][...]).astype(narrow)


def attend_seen(tab_ref, blocks, kv_refs, qm_ref, m_ref, acc_ref):
    for block, kv_ref in zip(blocks, kv_refs):

        @pl.when(tab_ref[block] == 1)
        def _(kv_ref=kv_ref):
            attend_block(kv_ref, 0, qm_ref, m_ref, acc_ref, False)


def attend_more_kernel(tab_ref, qm_ref, m_in, acc_in, *rest, blocks):
    kv_refs, (m_ref, acc_ref) = rest[:-2], rest[-2:]
    m_ref[...] = m_in[...]
    acc_ref[...] = acc_in[...]
    attend_seen(tab_ref, blocks, kv_refs, qm_ref, m_ref, acc_ref)


def attend_last_kernel(tab_ref, qm_ref, own_ref, m_in, acc_in, *rest, blocks):
    kv_refs, (att_ref, lse_ref, prob_ref, m_ref, acc_ref) = rest[:-5], rest[-5:]
    m_ref[...] = m_in[...]
    acc_ref[...] = acc_in[...]
    attend_seen(tab_ref, blocks, kv_refs, qm_ref, m_ref, acc_ref)
    lane = lax.broadcasted_iota(jnp.int32, (1, PAIR), 1)
    columns = []
    for p in range(HEADS // 2):
        first, second = acc_ref[2 * p], acc_ref[2 * p + 1]
        sums = pltpu.roll(jnp.where(lane < HEAD_DIM, second, first), HEAD_DIM, 1)
        att_ref[:, PAIR * p : PAIR * (p + 1)] = jnp.where(lane < HEAD_DIM, first, second) / sums
        columns.append(m_ref[2 * p][:, :1] + jnp.log(first[:, HEAD_DIM : HEAD_DIM + 1]))
        columns.append(m_ref[2 * p + 1][:, :1] + jnp.log(second[:, :1]))
    lse = jnp.concatenate(columns, 1).T
    lse_ref[...] = lse
    prob_ref[...] = jnp.exp(own_ref[...] - lse)


def gelu_parts(u):
    bell = jnp.exp(-0.5 * (u * u))
    t = 1.0 / (1.0 + (0.3275911 * 0.5**0.5) * jnp.abs(u))
    series = t * (0.127414796 + t * (-0.142248368 + t * (0.7107068705 + t * (-0.7265760135 + t * 0.5307027145))))
    tail = series * bell
    below = jnp.where(u >= 0.0, 1.0 - tail, tail)
    return u * below, below + u * (bell * 0.3989422804014327)


def feed_kernel(loads, tab_ref, x_ref, att_ref, g_ref, wo_ref, *rest, pieces, inverse_at):
    kv_refs = rest[:-11]
    out_ref, mid_ref, gh_ref, keep_ref, send_ref, kv_all, h_s, ht_s, out_s, buf_ref, sems = rest[-11:]
    copies = [
        pltpu.make_async_copy(kv_ref, kv_all.at[pl.ds(i, 1)], sems.at[3 + i]) for i, kv_ref in enumerate(kv_refs)
    ]
    for copy in copies:
        copy.start()
    rows, width = x_ref.shape
    hidden_rows = loads.held[4].shape[0]
    steps = hidden_rows // width
    down_rows = hidden_rows // pieces
    down_tiles = down_rows // TILE
    tiles = down_tiles + steps
    middle = x_ref[...].astype(single) + nn(att_ref[...].astype(narrow), wo_ref[...])
    mid_ref[...] = middle
    unit, _ = standardized(middle)
    h = (unit * loads[0][...] + loads[1][...]).astype(narrow)
    h_s[...] = h
    ht_s[...] = h.T
    g = g_ref[...]
    wu_ref, ub_ref, wd_ref, db_ref = (loads[i] for i in range(2, 6))
    small = buf_ref.shape[0] - 1
    place = lax.broadcasted_iota(jnp.int32, (TILE, width), 0)
    here = pieces // steps
    out_s[...] = middle + db_ref[...]
    gh_ref[...] = jnp.zeros_like(middle)

    def step(i, sums):
        cols = pl.ds(pl.multiple_of(i * width, width), width)
        act, slope = gelu_parts(nn(h_s[...], wu_ref[:, cols]) + ub_ref[:, cols])
        act = act.astype(narrow)
        out_s[...] += nn(act, wd_ref[cols, :])
        gu = (nt(g_ref[...], wd_ref[cols, :]) * slope).astype(narrow)
        gh_ref[...] += nt(gu, wu_ref[:, cols])
        grad_down = tn(act, g_ref[...]).astype(narrow)
        for j in range(here):
            at = tab_ref[inverse_at + i * here + j] * tiles
            store_tiles(buf_ref, at, grad_down[j * down_rows : (j + 1) * down_rows])
        grad_up = nn(ht_s[...], gu).astype(narrow)
        for j in range(pieces):
            buf_ref[tab_ref[inverse_at + j] * tiles + down_tiles + i] = grad_up[j * TILE : (j + 1) * TILE]
        return jnp.where(place == 1 + i, jnp.sum(gu.astype(single), 0, keepdims=True), sums)

    sums = lax.fori_loop(0, steps, step, jnp.zeros((TILE, width), single))
    unit, _ = standardized(mid_ref[...])
    gh = gh_ref[...]
    for row, value in ((0, g.astype(single)), (1 + steps, gh * unit), (2 + steps, gh)):
        sums = jnp.where(place == row, jnp.sum(value, 0, keepdims=True), sums)
    buf_ref[small] = sums.astype(narrow)
    out_ref[...] = out_s[...].astype(narrow)
    split_out(buf_ref, keep_ref, send_ref, sems, 1)
    for copy in copies:
        copy.wait()


def branch_kernel(
    loads, mid_ref, gh_ref, g_ref, att_ref, tv_ref, own_ref, wo_ref, gm_ref, gw_ref, ga_ref, dm_ref, delta_ref, ods_ref
):
    unit, spread = standardized(mid_ref[...])
    gm = g_ref[...].astype(single) + norm_back(gh_ref[...], unit, spread, loads[0][...])
    gm_ref[...] = gm
    branch = gm.astype(narrow)
    att = att_ref[...]
    ga = nt(branch, wo_ref[...]).astype(narrow)
    ga_ref[...] = ga
    split_heads(ga, dm_ref)
    wide = ga.astype(single)
    delta = head_sums(wide * att)
    delta_ref[...] = delta
    dprob = head_sums(wide * tv_ref[...].astype(single))
    ods_ref[...] = (own_ref[...] * (dprob - delta)).astype(narrow)
    gw_ref[...] = tn(att.astype(narrow), branch).astype(narrow)


def reorder_kernel(out_ref, gx_ref, to_out_ref, to_gx_ref):
    order = token_order(out_ref.shape[0])
    to_out_ref[...] = tn(order, out_ref[...]).astype(narrow)
    to_gx_ref[...] = tn(order, gx_ref[...]).astype(narrow)


def back_block(kv_ref, number, pair, qm_ref, dm_ref, lse_ref, delta_ref, diagonal):
    slots, width = kv_ref.shape[1], qm_ref.shape[2]
    cols = slice(PAIR * pair, PAIR * (pair + 1))
    k = kv_ref[number, :, cols]
    v = kv_ref[number, :, width + cols.start : width + cols.stop]
    lane = lax.broadcasted_iota(jnp.int32, (1, PAIR), 1)
    scores, probs = [], []
    for half in range(2):
        h = 2 * pair + half
        prob = jnp.exp(nt(k, qm_ref[half, :, cols]) - lse_ref[h : h + 1, :])
        dprob = nt(v, dm_ref[half, :, cols])
        if diagonal:
            slot = lax.broadcasted_iota(jnp.int32, prob.shape, 0)
            row = lax.broadcasted_iota(jnp.int32, prob.shape, 1)
            prob = jnp.where(3 * slot + 2 <= 3 * (row % slots) + row // slots, prob, 0.0)
        scores.append((prob * (dprob - delta_ref[h : h + 1, :])).astype(narrow))
        probs.append(prob.astype(narrow))
    dk = nn(scores[0], qm_ref[0, :, cols]) + nn(scores[1], qm_ref[1, :, cols])
    dv = nn(probs[0], dm_ref[0, :, cols]) + nn(probs[1], dm_ref[1, :, cols])
    nothing = jnp.zeros_like(k)
    split_k = jnp.concatenate([jnp.where(lane < HEAD_DIM, k, nothing), jnp.where(lane >= HEAD_DIM, k, nothing)], 0)
    return dk, dv, tn(jnp.concatenate(scores, 0), split_k)


def attend_back_kernel(
    tab_ref, qm_ref, dm_ref, lse_ref, delta_ref, kv_ref, dq_ref, keep_ref, send_ref, *, list_at, pair
):
    half, slots, _ = keep_ref.shape

    def store(number, dk, dv):
        @pl.when(number < half)
        def _():
            keep_ref[number, :, :PAIR] = dk
            keep_ref[number, :, PAIR:] = dv

        @pl.when(number >= half)
        def _():
            send_ref[number - half, :, :PAIR] = dk
            send_ref[number - half, :, PAIR:] = dv

    def step(i, carry):
        number = tab_ref[list_at + 1 + i]
        dk, dv, dq = back_block(kv_ref, number, pair, qm_ref, dm_ref, lse_ref, delta_ref, False)
        dq_ref[...] += dq
        store(number, dk.astype(narrow), dv.astype(narrow))
        return carry

    def clear(i, carry):
        nothing = jnp.zeros((slots, PAIR), narrow)
        store(tab_ref[list_at + 1 + i], nothing, nothing)
        return carry

    dq_ref[...] = jnp.zeros(dq_ref.shape, single)
    keep_ref[0] = jnp.zeros((slots, 2 * PAIR), narrow)
    lax.fori_loop(0, tab_ref[list_at], step, 0)
    lax.fori_loop(tab_ref[list_at], 2 * half - 1, clear, 0)


def attend_back_own_kernel(qm_ref, dm_ref, lse_ref, delta_ref, kv_ref, *rest, first):
    dq_in, (dq_ref, out_ref) = rest[:-2], rest[-2:]
    group = out_ref.shape[1] // 2
    for i, ref in enumerate(dq_in):
        dk, dv, dq = back_block(kv_ref, 0, first + i, qm_ref, dm_ref, lse_ref, delta_ref, True)
        cols = slice(PAIR * i, PAIR * (i + 1))
        dq_ref[:, cols] = ref[...] + dq
        out_ref[:, cols] = dk
        out_ref[:, group + PAIR * i : group + PAIR * (i + 1)] = dv


def sum_split_kernel(*refs, count, last):
    total = refs[0][...].astype(single)
    for ref in refs[1:count]:
        total += ref[...].astype(single)
    total = total.astype(narrow)
    outs = refs[count:]
    size = (total.shape[0] - last) // len(outs)
    for i, out_ref in enumerate(outs):
        if i == len(outs) - 1:
            out_ref[...] = total[i * size :]
        else:
            out_ref[pl.ds(0, size)] = total[i * size : (i + 1) * size]
            if last:
                out_ref[pl.ds(size, last)] = total[len(outs) * size :]


def sum_last_kernel(*refs, count, last):
    total = refs[0][...].astype(single)
    for ref in refs[1:count]:
        total += ref[...].astype(single)
    size = total.shape[0] - last
    refs[count][...] = total[:size].astype(narrow)
    refs[count + 1][...] = total[size:]


def join_kernel(*refs):
    parts, out_ref = refs[:-1], refs[-1]
    size = parts[0].shape[0]
    for i, ref in enumerate(parts):
        out_ref[pl.ds(i * size, size)] = ref[...]


def group_split_kernel(*refs):
    totals, (keep_ref, send_ref) = refs[:-2], refs[-2:]
    pairs = len(totals)
    half = keep_ref.shape[0]
    for pair, ref in enumerate(totals):
        for number in range(2):
            cols = slice(number * PAIR, (number + 1) * PAIR)
            first = (number * pairs + pair) * PAIR
            keep_ref[:, :, first : first + PAIR] = ref[pl.ds(0, half), :, cols]
            send_ref[:, :, first : first + PAIR] = ref[pl.ds(half, half), :, cols]


def store_tiles(buf_ref, first, values):
    for t in range(values.shape[0] // TILE):
        buf_ref[first + t] = values[t * TILE : (t + 1) * TILE]


def start_split(buf_ref, keep_ref, send_ref, sems, last):
    half = (buf_ref.shape[0] - last) // 2
    copies = [
        pltpu.make_async_copy(buf_ref.at[pl.ds(0, half)], keep_ref.at[pl.ds(0, half)], sems.at[0]),
        pltpu.make_async_copy(buf_ref.at[pl.ds(half, half + last)], send_ref, sems.at[1]),
    ]
    if last:
        copies.append(
            pltpu.make_async_copy(buf_ref.at[pl.ds(2 * half, last)], keep_ref.at[pl.ds(half, last)], sems.at[2])
        )
    for copy in copies:
        copy.start()
    return copies


def split_out(buf_ref, keep_ref, send_ref, sems, last):
    for copy in start_split(buf_ref, keep_ref, send_ref, sems, last):
        copy.wait()


def conv_grads(tab_ref, buf_ref, tk_ref, tv_ref, grad, tiles, pieces, inverse_at):
    width = tk_ref.shape[1]
    slots = grad.shape[0]
    group = grad.shape[1] // 2
    conv_tiles = TAPS * width // pieces // TILE
    for i in range(TAPS):
        own = slice(i * slots, (i + 1) * slots)
        both = jnp.concatenate([tn(tk_ref[own], grad[:, :group]), tn(tv_ref[own], grad[:, group:])], 1).astype(narrow)
        for j in range(width // TILE):
            tile = i * (width // TILE) + j
            at = tab_ref[inverse_at + tile // conv_tiles] * tiles + tile % conv_tiles
            for c in range(2 * group // COLUMNS):
                buf_ref[at + c * conv_tiles] = both[j * TILE : (j + 1) * TILE, c * COLUMNS : (c + 1) * COLUMNS]


def weight_grads(tab_ref, buf_ref, grad, first, tiles, pieces, inverse_at):
    for j in range(pieces):
        at = tab_ref[inverse_at + j] * tiles + first
        for c in range(grad.shape[1] // COLUMNS):
            buf_ref[at + c] = grad[j * TILE : (j + 1) * TILE, c * COLUMNS : (c + 1) * COLUMNS]


def middle_kernel(
    tab_ref, qm_ref, dm_ref, lse_ref, delta_ref, kv_ref, tk_ref, tv_ref, first_ref, second_ref, gw_out_ref, ck_ref, cv_ref,
    *rest, pieces, inverse_at,
):
    dq_refs, (gk_ref, gv_ref, dq_ref, keep_ref, send_ref, buf_ref, own_s, sems) = rest[:-8], rest[-8:]
    attend_back_own_kernel(qm_ref, dm_ref, lse_ref, delta_ref, kv_ref, *dq_refs, dq_ref, own_s, first=0)
    tiles = buf_ref.shape[0] // pieces
    blocks = gw_out_ref.shape[1] // COLUMNS
    grad = slot_grads(first_ref, second_ref, own_s)
    conv_grads(tab_ref, buf_ref, tk_ref, tv_ref, grad, tiles, pieces, inverse_at)
    weight_grads(tab_ref, buf_ref, gw_out_ref, tiles - blocks, tiles, pieces, inverse_at)
    copies = start_split(buf_ref, keep_ref, send_ref, sems, 0)
    conv_back(grad, ck_ref, cv_ref, 0, gk_ref, gv_ref)
    for copy in copies:
        copy.wait()


def tail_query_kernel(hid_ref, tk_ref, ods_ref, wq_ref, early_ref, later_ref, gh_ref, gw_ref):
    own_ds = tn(ods_ref[...], head_rows(tk_ref.shape[1])) * scale
    dq = jnp.concatenate([early_ref[...], later_ref[...]], 1)
    gq = (dq * scale + own_ds * tk_ref[...].astype(single)).astype(narrow)
    gw_ref[...] = tn(hid_ref[...], gq).astype(narrow)
    gh_ref[...] = nt(gq, wq_ref[...])


def slot_grads(*refs):
    return sum(ref[...].astype(single) for ref in refs).astype(narrow)


def conv_back(grads, ck_ref, cv_ref, first, gk_ref, gv_ref):
    slots, width = grads.shape[0], ck_ref.shape[1]
    group = grads.shape[1] // 2
    for grad, c_ref, out_ref in ((grads[:, :group], ck_ref, gk_ref), (grads[:, group:], cv_ref, gv_ref)):
        for i in range(TAPS):
            out_ref[i * slots : (i + 1) * slots] = nt(grad, c_ref[i * width : (i + 1) * width, first : first + group])


def tail_kernel(
    tab_ref, x_ref, hid_ref, q_ref, tk_ref, tv_ref, ga_ref, gm_ref, own_ref, ods_ref, gh_ref, gk0_ref, gv0_ref,
    first_ref, second_ref, own_grad_ref, gwq_ref, wk_ref, wv_ref, ck_ref, cv_ref, gain_ref, gx_ref, keep_ref, send_ref, buf_ref, gk_s, gv_s, sems, *, pieces, inverse_at,
):
    rows, width = x_ref.shape
    tiles = (buf_ref.shape[0] - 1) // pieces
    blocks = width // COLUMNS
    grad = slot_grads(first_ref, second_ref, own_grad_ref)
    conv_grads(tab_ref, buf_ref, tk_ref, tv_ref, grad, tiles, pieces, inverse_at)
    marks = head_rows(width)
    own_ds = tn(ods_ref[...], marks) * scale
    own_prob = tn(own_ref[...].astype(narrow), marks)
    conv_back(grad, ck_ref, cv_ref, width - grad.shape[1] // 2, gk_s, gv_s)
    gk = (gk_s[...] + gk0_ref[...] + own_ds * q_ref[...].astype(single)).astype(narrow)
    gv = (gv_s[...] + gv0_ref[...] + own_prob * ga_ref[...].astype(single)).astype(narrow)
    weight_grads(tab_ref, buf_ref, gwq_ref, tiles - 3 * blocks, tiles, pieces, inverse_at)
    hidden_t = hid_ref[...].T
    grad_hidden = gh_ref[...]
    for number, grad in enumerate((gk, gv)):
        grad_w = nn(hidden_t, grad).astype(narrow)
        weight_grads(tab_ref, buf_ref, grad_w, tiles - (2 - number) * blocks, tiles, pieces, inverse_at)
        grad_hidden += nt(grad, (wk_ref, wv_ref)[number][...])
    unit, spread = standardized(x_ref[...].astype(single))
    place = lax.broadcasted_iota(jnp.int32, (TILE, COLUMNS), 0)
    sums = jnp.zeros((TILE, COLUMNS), single)
    for first, value in ((0, grad_hidden * unit), (blocks, grad_hidden)):
        total = jnp.sum(value, 0, keepdims=True)
        for c in range(blocks):
            sums = jnp.where(place == first + c, total[:, c * COLUMNS : (c + 1) * COLUMNS], sums)
    buf_ref[buf_ref.shape[0] - 1] = sums.astype(narrow)
    split_out(buf_ref, keep_ref, send_ref, sems, 1)
    gx_ref[...] = (gm_ref[...] + norm_back(grad_hidden, unit, spread, gain_ref[...])).astype(narrow)


def unpack_feed_kernel(
    tab_ref, own_ref, other_ref, small_ref, wd_ref, wu_ref, gain_ref, bias_ref, up_ref, down_ref, *, pieces, piece_at
):
    width = wd_ref.shape[1]
    down_rows = wd_ref.shape[0] // pieces
    down_tiles, up_tiles = down_rows // TILE, wu_ref.shape[1] // width
    tiles = down_tiles + up_tiles
    down_ref[...] = small_ref[0, 0:1, :]
    for t in range(up_tiles):
        up_ref[:, t * width : (t + 1) * width] = small_ref[0, 1 + t : 2 + t, :]
    gain_ref[...] = small_ref[0, 1 + up_tiles : 2 + up_tiles, :]
    bias_ref[...] = small_ref[0, 2 + up_tiles : 3 + up_tiles, :]

    for number, buf_ref in enumerate((own_ref, other_ref)):

        def step(k, carry, number=number, buf_ref=buf_ref):
            piece = tab_ref[piece_at + number * pieces // 2 + k]
            at = k * tiles
            for t in range(down_tiles):
                rows = pl.ds(pl.multiple_of(piece * down_rows + t * TILE, TILE), TILE)
                wd_ref[rows, :] = buf_ref[at + t].astype(single)
            mine = pl.ds(pl.multiple_of(piece * TILE, TILE), TILE)
            for t in range(up_tiles):
                wu_ref[mine, t * width : (t + 1) * width] = buf_ref[at + down_tiles + t].astype(single)
            return carry

        lax.fori_loop(0, pieces // 2, step, 0, unroll=4)


def unpack_kernel(tab_ref, *rest, parts, half, piece_at, first_column, outs, small):
    bufs, rest = rest[: len(parts)], rest[len(parts) :]
    if small:
        small_ref, small_outs, rest = rest[0], rest[-5 - outs : -3 - outs], rest[1:]
        for i, ref in enumerate(small_outs):
            ref[...] = small_ref[0, i : i + 1, :]
    out_refs, (conv_s, weight_s, sems) = rest[-outs - 3 : -3], rest[-3:]
    weight_refs, conv_refs = out_refs[:-2], out_refs[-2:]
    conv_rows, columns = conv_s.shape[2], conv_s.shape[3]
    conv_tiles = conv_rows // TILE
    blocks = weight_s.shape[3] // COLUMNS
    weights_at = conv_tiles * (2 * columns // COLUMNS)
    tiles = weights_at + blocks * len(weight_refs)

    def copies(number, place):
        piece = tab_ref[piece_at + place]
        rows = pl.ds(pl.multiple_of(piece * conv_rows, TILE), conv_rows)
        mine = pl.ds(pl.multiple_of(piece * TILE, TILE), TILE)
        cols = pl.ds(first_column, columns)
        return [
            pltpu.make_async_copy(conv_s.at[number, i], ref.at[rows, cols], sems.at[number, i])
            for i, ref in enumerate(conv_refs)
        ] + [
            pltpu.make_async_copy(weight_s.at[number, i], ref.at[mine], sems.at[number, 2 + i])
            for i, ref in enumerate(weight_refs)
        ]

    for order, (buf_ref, part) in enumerate(zip(bufs, parts)):

        def step(k, carry, order=order, buf_ref=buf_ref, part=part):
            number = order * half + k
            for t in range(conv_tiles):
                for unit in range(2 * columns // PAIR):
                    which, first = unit * PAIR // columns, unit * PAIR % columns
                    block, lanes = unit * PAIR // COLUMNS, unit * PAIR % COLUMNS
                    conv_s[number, which, t * TILE : (t + 1) * TILE, first : first + PAIR] = buf_ref[
                        k * tiles + block * conv_tiles + t, :, lanes : lanes + PAIR
                    ].astype(single)
            for t in range(len(weight_refs)):
                for c in range(blocks):
                    weight_s[number, t, :, c * COLUMNS : (c + 1) * COLUMNS] = buf_ref[
                        k * tiles + weights_at + t * blocks + c
                    ].astype(single)
            for copy in copies(number, part * half + k):
                copy.start()
            return carry

        lax.fori_loop(0, half, step, 0)

    for order, part in enumerate(parts):

        def finish(k, carry, order=order, part=part):
            for copy in copies(order * half + k, part * half + k):
                copy.wait()
            return carry

        lax.fori_loop(0, half, finish, 0)


def shaped(shape, kind):
    return jax.ShapeDtypeStruct(shape, kind)


def per_device(
    seq_size, batch_size,
    inputs, cotangent, ln1_gain, ln1_bias, w_query, w_key, w_value, conv_key, conv_value, w_out,
    ln2_gain, ln2_bias, w_up, up_bias, w_down, down_bias,
):
    x, g = inputs[0], cotangent[0]
    rows, width = x.shape
    slots = rows // TAPS
    ff = w_up.shape[1]
    seq_bits, batch_bits = seq_size.bit_length() - 1, batch_size.bit_length() - 1
    split_bits = min(5, seq_bits + batch_bits)
    pieces = 1 << split_bits
    list_at = seq_size
    piece_at = list_at + seq_size
    inverse_at = piece_at + pieces
    tables = jnp.asarray(plan_tables(seq_size, batch_size, split_bits))
    table = lax.dynamic_index_in_dim(
        tables, lax.axis_index("seq") * batch_size + lax.axis_index("batch"), 0, keepdims=False
    )
    x = tied(x, table)
    row = lambda v: v.reshape(1, -1)
    ck = conv_key.reshape(TAPS * width, width)
    cv = conv_value.reshape(TAPS * width, width)
    token_low, token_wide = shaped((rows, width), narrow), shaped((rows, width), single)
    head_wide, head_low = shaped((HEADS, rows), single), shaped((HEADS, rows), narrow)
    two_low = shaped((2, rows, width), narrow)

    xp, hidden, tk, tv, kv = call(
        "front",
        front_kernel,
        (token_low,) * 4 + (shaped((slots, 2 * width), narrow),),
        loads=(x, row(ln1_gain), row(ln1_bias), w_key, ck, w_value, cv),
        mib=24,
        flops=4e9,
    )

    state = shaped((HEADS, rows, PAIR), single)
    q, gp, qm, own, m, acc = call(
        "attend_own",
        attend_own_kernel,
        (token_low, token_low, two_low, head_wide, state, state),
        loads=(w_query, g),
        operands=(hidden, tk, tv, kv[None]),
        mib=16,
        flops=1e10,
    )
    blocks = {0: kv[None]}
    rounds = gather_plan(seq_size)
    calls = []
    for number, found in enumerate(rounds):
        if number > 0:
            calls.append([entry[0] for entry in rounds[number - 1]])
        held = {source: blocks[source] for _, source, _ in found if source in blocks}
        if number > 1:
            held = tied(held, m)
        for block, source, (axis, pairs) in found:
            if source in held:
                blocks[block] = lax.ppermute(held[source], axis, pairs)
        if number == 0:
            continue
        later = [entry for entry in found if entry[0] not in blocks]
        halves = [[k for k in calls[-1] if k < seq_size // 2], [k for k in calls[-1] if k >= seq_size // 2]]
        for found in halves:
            if not found:
                continue
            m, acc = call(
                f"attend_{found[0]}",
                functools.partial(attend_more_kernel, blocks=found),
                (state, state),
                table=table,
                operands=(qm, m, acc, *[blocks[k] for k in found]),
                mib=8,
                flops=1e11,
            )
            if later:
                for block, source, (axis, pairs) in later:
                    blocks[block] = lax.ppermute(tied(blocks[source], m), axis, pairs)
                later = []
    calls.append([entry[0] for entry in rounds[-1]])
    attended, lse, own_prob = call(
        "attend_last",
        functools.partial(attend_last_kernel, blocks=calls[-1]),
        (token_wide, head_wide, head_wide),
        table=table,
        operands=(qm, own, m, acc, *[blocks[k] for k in calls[-1]]),
        scratch=[pltpu.VMEM(state.shape, single), pltpu.VMEM(state.shape, single)],
        mib=16,
        flops=1e10 * len(calls[-1]),
    )

    steps = ff // width
    tiles = ff // pieces // TILE + steps
    half = shaped((pieces // 2 * tiles + 1, TILE, width), narrow)
    output, middle, grad_normal, keep, send, all_kv = call(
        "feed",
        functools.partial(feed_kernel, pieces=pieces, inverse_at=inverse_at),
        (token_low, token_wide, token_wide, half, half, shaped((seq_size, slots, 2 * width), narrow)),
        loads=(row(ln2_gain), row(ln2_bias), w_up, row(up_bias), w_down, row(down_bias)),
        table=table,
        operands=(xp, attended, gp, w_out),
        away=[blocks[k] for k in range(seq_size)],
        away_outs=3,
        scratch=[
            pltpu.VMEM((rows, width), narrow),
            pltpu.VMEM((width, rows), narrow),
            pltpu.VMEM((rows, width), single),
            pltpu.VMEM((pieces * tiles + 1, TILE, width), narrow),
            pltpu.SemaphoreType.DMA((3 + seq_size,)),
        ],
        mib=30,
        flops=5e10,
    )
    grad_middle, grad_w_out_here, grad_attended, dm, delta, own_ds = call(
        "branch",
        branch_kernel,
        (token_wide, shaped((width, width), narrow), token_low, two_low, head_wide, head_low),
        loads=(row(ln2_gain),),
        operands=(middle, grad_normal, gp, attended, tv, own_prob, w_out),
        mib=16,
        flops=1e11,
    )

    stages = reduce_stages(seq_size, batch_size, split_bits)
    gather_back = [stage for stage in stages if stage[0] > 1][::-1]
    unseen = gather_stages(seq_size)[::-1]
    head_pairs = HEADS // 2

    wide_grant = 12 if seq_size <= 8 else 56
    share = shaped((seq_size // 2, slots, 2 * PAIR), narrow)

    def back(pair, qm):
        return call(
            f"attend_back_{pair}",
            functools.partial(attend_back_kernel, list_at=list_at, pair=pair),
            (shaped((rows, PAIR), single), share, share),
            table=table,
            operands=(qm, dm, lse, delta, all_kv),
            mib=wide_grant,
            flops=1e11,
        )

    def small_call(kernel, name, outs, *operands):
        return call(name, kernel, outs, operands=operands, mib=4, flops=sum(v.size for v in operands) * 600)

    def sum_split(buffers, last, cut):
        count, rest = buffers[0].shape[0], buffers[0].shape[1:]
        outs = (shaped(((count - last) // cut + last, *rest), narrow),) * cut
        kernel = functools.partial(sum_split_kernel, count=len(buffers), last=last)
        return small_call(kernel, "sum_split", outs, *buffers)

    def join(*parts):
        out = shaped((len(parts) * parts[0].shape[0], *parts[0].shape[1:]), narrow)
        return small_call(join_kernel, "join", (out,), *parts)[0]

    def exchange(stage, parts):
        return [lax.ppermute(part, stage[1], pairs) for part, pairs in zip(parts, stage[2])]

    class Sum:
        def __init__(self, keep, send, last):
            self.keep, self.last, self.at = keep, last, 0
            self.arrived = exchange(stages[0], [send])

        def step(self, *others):
            arrived = tied(self.arrived, *others)
            self.at += 1
            if self.at < len(stages):
                cut = stages[self.at][0]
                parts = sum_split((self.keep, *arrived), self.last, cut)
                self.keep, sent = parts[0], parts[1:] if cut > 1 else parts
                self.arrived = exchange(stages[self.at], sent)
                return sent[0]
            if self.at == len(stages):
                buffers = (self.keep, *arrived)
                if self.last:
                    count, rest = buffers[0].shape[0], buffers[0].shape[1:]
                    outs = (shaped((count - self.last, *rest), narrow), shaped((self.last, *rest), single))
                    kernel = functools.partial(sum_last_kernel, count=len(buffers), last=self.last)
                    self.held, self.small = small_call(kernel, "sum_last", outs, *buffers)
                else:
                    (self.held,) = sum_split(buffers, 0, 1)
            else:
                self.held = join(self.held, *arrived)
            stage = gather_back[self.at - len(stages)]
            self.arrived = exchange(stage, [self.held] * len(stage[2]))
            return self.held

        def left(self):
            return len(stages) + len(gather_back) - 1 - self.at

    class Group:
        def __init__(self):
            self.shares, self.at = [], 0

        def step(self, *others):
            self.at += 1
            if self.at == 1:
                operands = tied(self.shares, *others)
                half = shaped((seq_size // 4, slots, len(self.shares) * 2 * PAIR), narrow)
                self.keep, send = small_call(group_split_kernel, "group_split", (half, half), *operands)
            else:
                self.keep, send = sum_split((self.keep, tied(self.arrived, *others)), 0, 2)
            self.arrived = lax.ppermute(send, *unseen[self.at])
            return send

        def left(self):
            return len(unseen) - 1 - self.at

    conv_tiles = TAPS * width // pieces // TILE
    blocks_wide = width // COLUMNS
    first_tiles, tail_tiles = (
        conv_tiles * (group * 2 * PAIR // COLUMNS) + count * blocks_wide for group, count in zip(GROUPS, (1, 3))
    )

    sums = {"feed": Sum(keep, send, 1)}
    first_group, second_group = Group(), Group()
    waits = [sums["feed"].step(delta)]
    state_back = {"grads": []}

    def advance(name, kept=0):
        if name in sums and sums[name].left() > kept:
            waits.append(sums[name].step(*waits))

    def advance_group(group):
        if group.left() > 0:
            waits.append(group.step(*waits))

    def add_share(group, kept, arrived):
        (total,) = sum_split(tied((kept, arrived), *waits), 0, 1)
        waits.append(total)
        group.shares.append(total)

    partial_q, pending = [], None
    for pair in range(head_pairs):
        in_first = pair < GROUPS[0]
        grads, kept, sent = back(pair, tied(qm, *waits))
        waits = [grads]
        partial_q.append(grads)
        if pair < head_pairs - 1:
            advance("feed", 1)
        if pending is not None:
            add_share(*pending)
        pending = (first_group if in_first else second_group, kept, lax.ppermute(sent, *unseen[0]))
        if pair >= GROUPS[0]:
            advance_group(first_group)
    def own_block(first, count):
        return call(
            f"attend_back_own_{first}",
            functools.partial(attend_back_own_kernel, first=first),
            (shaped((rows, count * PAIR), single), shaped((slots, count * 2 * PAIR), single)),
            operands=(tied(qm, *waits), dm, lse, delta, kv[None], *partial_q[first : first + count]),
            mib=12,
            flops=1e11,
        )

    later_q, second_own = own_block(GROUPS[0], GROUPS[1])
    waits = [later_q]
    add_share(*pending)
    advance_group(second_group)
    advance("feed", 1)
    while first_group.left() > 0:
        advance_group(first_group)
    half = shaped((pieces // 2 * first_tiles, TILE, COLUMNS), narrow)
    grad_k, grad_v, early_q, keep0, send0 = call(
        "middle",
        functools.partial(middle_kernel, pieces=pieces, inverse_at=inverse_at),
        (token_wide, token_wide, shaped((rows, GROUPS[0] * PAIR), single), half, half),
        table=table,
        operands=(
            tied(qm, *waits), dm, lse, delta, kv[None], tk, tv, first_group.keep[0], first_group.arrived[0],
            grad_w_out_here, ck, cv, *partial_q[: GROUPS[0]],
        ),
        away_outs=2,
        scratch=[
            pltpu.VMEM((pieces * first_tiles, TILE, COLUMNS), narrow),
            pltpu.VMEM((slots, GROUPS[0] * 2 * PAIR), single),
            pltpu.SemaphoreType.DMA((3,)),
        ],
        mib=24,
        flops=1e11,
    )
    sums["first"] = Sum(keep0, send0, 0)
    waits = [grad_k]
    advance("feed", 1)
    advance_group(second_group)
    grad_hidden, grad_wq_here = call(
        "tail_query",
        tail_query_kernel,
        (token_wide, shaped((width, width), narrow)),
        operands=(tied(hidden, *waits), tk, own_ds, w_query, early_q, later_q),
        mib=16,
        flops=1e11,
    )
    waits = [grad_hidden]
    while second_group.left() > 0:
        advance_group(second_group)
    advance("first")
    half = shaped((pieces // 2 * tail_tiles + 1, TILE, COLUMNS), narrow)
    grad_x, keep1, send1 = call(
        "tail",
        functools.partial(tail_kernel, pieces=pieces, inverse_at=inverse_at),
        (token_low, half, half),
        table=table,
        operands=(
            xp, hidden, q, tk, tv, grad_attended, grad_middle, own_prob, own_ds, grad_hidden, grad_k, grad_v,
            tied(second_group.keep[0], *waits), second_group.arrived[0], second_own, grad_wq_here,
            w_key, w_value, ck, cv, row(ln1_gain),
        ),
        away_outs=2,
        scratch=[
            pltpu.VMEM((pieces * tail_tiles + 1, TILE, COLUMNS), narrow),
            pltpu.VMEM((rows, width), single),
            pltpu.VMEM((rows, width), single),
            pltpu.SemaphoreType.DMA((3,)),
        ],
        mib=26,
        flops=1e11,
    )
    sums["second"] = Sum(keep1, send1, 1)
    waits = [grad_x]

    def unpack(name, parts, heads, weights, bufs, *known, small=()):
        count = len(parts) * pieces // 2
        outs = [shaped((width, width), single)] * weights + [shaped(ck.shape, single)] * 2
        first = [shaped((1, width), single)] * (2 * len(small))
        return call(
            name,
            functools.partial(
                unpack_kernel,
                parts=parts,
                half=pieces // 2,
                piece_at=piece_at,
                first_column=heads[0] * PAIR,
                outs=len(outs),
                small=len(small),
            ),
            first + outs,
            table=table,
            operands=(*bufs, *small),
            away=known,
            away_outs=len(outs),
            in_place=len(known),
            scratch=[
                pltpu.VMEM((count, 2, conv_tiles * TILE, heads[1] * PAIR), single),
                pltpu.VMEM((count, weights, TILE, width), single),
                pltpu.SemaphoreType.DMA((count, len(outs))),
            ],
            mib=20,
            flops=1e11,
        )

    def finish_feed(*others):
        vector = shaped((1, width), single)
        return call(
            "unpack_feed",
            functools.partial(unpack_feed_kernel, pieces=pieces, piece_at=piece_at),
            (shaped((ff, width), single), shaped((width, ff), single), vector, vector, shaped((1, ff), single), vector),
            table=table,
            operands=(sums["feed"].held, tied(sums["feed"].arrived[0], *others), sums["feed"].small),
            mib=16,
            flops=2e10,
        )

    places = (GROUPS[0], GROUPS[1])
    for action in "F0R010010101F011F101Uu1":
        if action in "01F":
            advance({"0": "first", "1": "second", "F": "feed"}[action])
            waits = waits[-1:]
        elif action == "R":
            output, grad_x = call(
                "reorder",
                reorder_kernel,
                (token_low, token_low),
                operands=(output, tied(grad_x, *waits)),
                mib=8,
                flops=1e11,
            )
            waits.append(grad_x)
        elif action == "U":
            while sums["feed"].left() > 0:
                advance("feed")
            grad_w_down, grad_w_up, *small_feed = finish_feed(*waits)
            waits.append(grad_w_up)
        elif action == "u":
            while sums["first"].left() > 0:
                advance("first")
            while sums["second"].left() > 1:
                advance("second")
            grad_w_out, *convs = unpack(
                "unpack_first",
                (0, 1),
                (0, GROUPS[0]),
                1,
                (sums["first"].held, tied(sums["first"].arrived[0], *waits)),
            )
            waits.append(grad_w_out)
    last = sums["second"]
    small_first, small_second, *found = unpack(
        "unpack_own", (0,), places, 3, (last.held,), *tied(convs, *waits), small=(last.small,)
    )
    grad_wq, grad_wk, grad_wv, grad_ck, grad_cv = unpack(
        "unpack_last", (1,), places, 3, (last.arrived[0],), *found
    )
    return (
        output[None],
        grad_x[None],
        small_first[0],
        small_second[0],
        grad_wq,
        grad_wk,
        grad_wv,
        grad_ck.reshape(conv_key.shape),
        grad_cv.reshape(conv_value.shape),
        grad_w_out,
        small_feed[0][0],
        small_feed[1][0],
        grad_w_up,
        small_feed[2][0],
        grad_w_down,
        small_feed[3][0],
    )


def solution(mesh):
    placed = (P("batch", "seq", None),) * 2 + (P(),) * 14
    return jax.shard_map(
        functools.partial(per_device, mesh.shape["seq"], mesh.shape["batch"]),
        mesh=mesh,
        in_specs=placed,
        out_specs=placed,
        check_vma=False,
    )
```

```python
import functools

import jax
import jax.numpy as jnp
import numpy as np
from jax import lax
from jax.experimental import pallas as pl
from jax.experimental.pallas import tpu as pltpu
from jax.sharding import PartitionSpec as P

HEADS = 8
HEAD_DIM = 64
PAIR = 2 * HEAD_DIM
TAPS = 3
TILE = 16
COLUMNS = 512
GROUPS = (2, 2)

epsilon = 1e-05
narrow = jnp.bfloat16
single = jnp.float32
scale = HEAD_DIM ** (-0.5)

vmem = pl.BlockSpec(memory_space=pltpu.VMEM)
smem = pl.BlockSpec(memory_space=pltpu.SMEM)
anywhere = pl.BlockSpec(memory_space=pl.ANY)
hbm = pl.BlockSpec(memory_space=pltpu.HBM)


def params(mib):
    return pltpu.CompilerParams(vmem_limit_bytes=mib * 2**20)


def cost(flops, moved):
    return pl.CostEstimate(flops=int(flops), bytes_accessed=int(moved), transcendentals=0)


class Loads:
    def __init__(self, sources, held, sems):
        self.held, self.waited = held, set()
        self.copies = [pltpu.make_async_copy(a, b, sems.at[i]) for i, (a, b) in enumerate(zip(sources, held))]
        for copy in self.copies:
            copy.start()

    def __getitem__(self, i):
        if i not in self.waited:
            self.copies[i].wait()
            self.waited.add(i)
        return self.held[i]


def call(
    name, body, outs, *, loads=(), table=None, operands=(), away=(), away_outs=0, in_place=0, scratch=(), mib, flops
):
    count = len(loads)
    inputs = count + (table is not None) + len(operands) + len(away)

    def kernel(*refs):
        sources, rest = refs[:count], refs[count:]
        if count == 0:
            return body(*rest)
        held, sems = rest[-count - 1 : -1], rest[-1]
        return body(Loads(sources, held, sems), *rest[: -count - 1])

    moved = sum(v.size * 2 for v in (*loads, *operands, *away, *outs))
    scratch = list(scratch)
    if count:
        scratch += [pltpu.VMEM(v.shape, v.dtype) for v in loads] + [pltpu.SemaphoreType.DMA((count,))]
    return pl.pallas_call(
        kernel,
        out_shape=tuple(outs),
        in_specs=[hbm] * count + [smem] * (table is not None) + [vmem] * len(operands) + [anywhere] * len(away),
        out_specs=(vmem,) * (len(outs) - away_outs) + (anywhere,) * away_outs,
        scratch_shapes=scratch,
        input_output_aliases={inputs - in_place + i: len(outs) - in_place + i for i in range(in_place)},
        compiler_params=params(mib),
        cost_estimate=cost(flops, moved),
        name=name,
    )(
        *[pltpu.with_memory_space_constraint(v, pltpu.HBM) for v in loads],
        *([] if table is None else [table]),
        *operands,
        *away,
    )


def tied(values, *others):
    return lax.optimization_barrier((values, others))[0]


def nn(a, b):
    return lax.dot_general(a, b, (((1,), (0,)), ((), ())), preferred_element_type=single)


def nt(a, b):
    return lax.dot_general(a, b, (((1,), (1,)), ((), ())), preferred_element_type=single)


def tn(a, b):
    return lax.dot_general(a, b, (((0,), (0,)), ((), ())), preferred_element_type=single)


def bit_masks(size):
    return [1 << b for b in range(size.bit_length() - 1)]


def seq_masks(size, core):
    masks = bit_masks(size)[1:]
    return masks if core == 0 else masks[::-1]


def seq_swap(size, stage):
    return [(i, i ^ seq_masks(size, i & 1)[stage]) for i in range(size)]


def gather_stages(seq_size):
    found = [("seq", seq_swap(seq_size, j)) for j in range(len(bit_masks(seq_size)) - 1)]
    return found + [("seq", [(i, i ^ 1) for i in range(seq_size)])]


def reduce_stages(seq_size, batch_size, split_bits):
    found = [(2, "seq", [[(i, i ^ 1) for i in range(seq_size)]])]
    found += [(2, "seq", [seq_swap(seq_size, j)]) for j in range(len(bit_masks(seq_size)) - 1)]
    split = split_bits - len(found)
    for j, mask in enumerate(bit_masks(batch_size)):
        found.append((2 if j < split else 1, "batch", [[(i, i ^ mask) for i in range(batch_size)]]))
    return found


def gather_origin(seq_size, me, block):
    count = len(bit_masks(seq_size)) - 1
    core_bit = (block >> count) & 1
    other = me ^ core_bit
    masks = seq_masks(seq_size, other & 1)
    for j in range(count):
        if (block >> j) & 1:
            other ^= masks[j]
    return other


def piece_of(seq_size, batch_size, split_bits, me_seq, me_batch, place):
    bits = [(place >> (split_bits - 1 - j)) & 1 for j in range(split_bits)]
    s = me_seq ^ bits[0]
    masks = seq_masks(seq_size, s & 1)
    z = me_batch
    for j, b in enumerate(bits[1:]):
        if j < len(masks):
            s ^= masks[j] * b
        else:
            z ^= (1 << (j - len(masks))) * b
    low_batch = z & ((1 << (split_bits - len(bit_masks(seq_size)))) - 1)
    return s + seq_size * low_batch


def gather_plan(seq_size):
    stages = gather_stages(seq_size)
    count = len(stages) - 1
    rounds = [[] for _ in range(count + 1)]
    for block in range(1, 1 << count):
        last = block.bit_length() - 1
        rounds[bin(block).count("1")].append((block, block ^ (1 << last), stages[last]))
    for found in rounds:
        blocks = [entry[0] for entry in found] or [0]
        found += [(block | (1 << count), block, stages[-1]) for block in blocks]
    return rounds


def plan_tables(seq_size, batch_size, split_bits):
    rows = []
    pieces = 1 << split_bits
    for s in range(seq_size):
        origins = [gather_origin(seq_size, s, k) for k in range(seq_size)]
        seen = [int(origin < s) for origin in origins]
        visible = [k for k in range(seq_size) if origins[k] < s]
        lists = [len(visible)] + visible + [k for k in range(seq_size) if origins[k] > s]
        for z in range(batch_size):
            places = [piece_of(seq_size, batch_size, split_bits, s, z, k) for k in range(pieces)]
            inverse = [places.index(p) for p in range(pieces)]
            rows.append(seen + lists + places + inverse)
    return np.asarray(rows, np.int32)


def token_order(rows):
    slots = rows // TAPS
    r = lax.broadcasted_iota(jnp.int32, (rows, rows), 0)
    c = lax.broadcasted_iota(jnp.int32, (rows, rows), 1)
    return jnp.where(c == TAPS * (r % slots) + r // slots, 1.0, 0.0).astype(narrow)


def head_rows(width):
    r = lax.broadcasted_iota(jnp.int32, (HEADS, width), 0)
    c = lax.broadcasted_iota(jnp.int32, (HEADS, width), 1)
    return jnp.where(c // HEAD_DIM == r, 1.0, 0.0).astype(narrow)


def head_sums(values):
    marks = head_rows(values.shape[1])
    high = values.astype(narrow)
    rest = values - high.astype(single)
    middle = rest.astype(narrow)
    low = (rest - middle.astype(single)).astype(narrow)
    return nt(marks, high) + nt(marks, middle) + nt(marks, low)


def standardized(values):
    centred = values - jnp.mean(values, -1, keepdims=True)
    spread = lax.rsqrt(jnp.mean(centred * centred, -1, keepdims=True) + epsilon)
    return centred * spread, spread


def norm_back(grad, unit, spread, gain):
    inner = grad * gain
    return spread * (
        inner
        - jnp.mean(inner, -1, keepdims=True)
        - unit * jnp.mean(inner * unit, -1, keepdims=True)
    )


def front_kernel(loads, xp_ref, hid_ref, tk_ref, tv_ref, kv_ref):
    rows, width = xp_ref.shape
    slots = rows // TAPS
    order = token_order(rows)
    x = nn(order, loads[0][...])
    xp_ref[...] = x.astype(narrow)
    unit, _ = standardized(x)
    hidden = (unit * loads[1][...] + loads[2][...]).astype(narrow)
    hid_ref[...] = hidden
    for number, t_ref in enumerate((tk_ref, tv_ref)):
        t = nn(hidden, loads[3 + 2 * number][...]).astype(narrow)
        t_ref[...] = t
        c_ref = loads[4 + 2 * number]
        total = nn(t[:slots], c_ref[:width])
        for i in range(1, TAPS):
            total += nn(t[i * slots : (i + 1) * slots], c_ref[i * width : (i + 1) * width])
        kv_ref[:, number * width : (number + 1) * width] = total.astype(narrow)


def attend_block(kv_ref, number, qm_ref, m_ref, acc_ref, diagonal):
    slots, width = kv_ref.shape[1], qm_ref.shape[2]
    lane = lax.broadcasted_iota(jnp.int32, (1, PAIR), 1)
    for h in range(HEADS):
        cols = slice(PAIR * (h // 2), PAIR * (h // 2 + 1))
        keep = (lane < HEAD_DIM) if h % 2 == 0 else (lane >= HEAD_DIM)
        v = kv_ref[number, :, width + cols.start : width + cols.stop]
        v_ones = jnp.where(keep, v, jnp.ones_like(v))
        s = nt(qm_ref[h % 2, :, cols], kv_ref[number, :, cols])
        if diagonal:
            slot = lax.broadcasted_iota(jnp.int32, s.shape, 1)
            row = lax.broadcasted_iota(jnp.int32, s.shape, 0)
            s = jnp.where(3 * slot + 2 <= 3 * (row % slots) + row // slots, s, -1e30)
        before = m_ref[h]
        after = jnp.maximum(before, jnp.max(s, 1, keepdims=True))
        m_ref[h] = after
        p = jnp.exp(s - jnp.concatenate([after] * (slots // PAIR), 1))
        acc_ref[h] = acc_ref[h] * jnp.exp(before - after) + nn(p.astype(narrow), v_ones)


def split_heads(values, out_ref):
    lanes = lax.broadcasted_iota(jnp.int32, (1, values.shape[1]), 1) % PAIR
    nothing = jnp.zeros_like(values)
    out_ref[0] = jnp.where(lanes < HEAD_DIM, values, nothing)
    out_ref[1] = jnp.where(lanes >= HEAD_DIM, values, nothing)


def attend_own_kernel(loads, hid_ref, tk_ref, tv_ref, kv_ref, q_ref, gp_ref, qm_ref, own_ref, m_ref, acc_ref):
    rows, width = hid_ref.shape
    q_low = nn(hid_ref[...], loads[0][...]).astype(narrow)
    q_ref[...] = q_low
    q = q_low.astype(single)
    split_heads((q * scale).astype(narrow), qm_ref)
    own = head_sums(q * tk_ref[...].astype(single)) * scale
    own_ref[...] = own
    own_cols = own.T
    lane = lax.broadcasted_iota(jnp.int32, (1, PAIR), 1)
    for h in range(HEADS):
        keep = (lane < HEAD_DIM) if h % 2 == 0 else (lane >= HEAD_DIM)
        m_ref[h] = jnp.broadcast_to(own_cols[:, h : h + 1], (rows, PAIR))
        acc_ref[h] = jnp.where(keep, tv_ref[:, PAIR * (h // 2) : PAIR * (h // 2 + 1)].astype(single), 1.0)
    attend_block(kv_ref, 0, qm_ref, m_ref, acc_ref, True)
    gp_ref[...] = nn(token_order(rows), loads[1][...]).astype(narrow)


def attend_seen(tab_ref, blocks, kv_refs, qm_ref, m_ref, acc_ref):
    for block, kv_ref in zip(blocks, kv_refs):

        @pl.when(tab_ref[block] == 1)
        def _(kv_ref=kv_ref):
            attend_block(kv_ref, 0, qm_ref, m_ref, acc_ref, False)


def attend_more_kernel(tab_ref, qm_ref, m_in, acc_in, *rest, blocks):
    kv_refs, (m_ref, acc_ref) = rest[:-2], rest[-2:]
    m_ref[...] = m_in[...]
    acc_ref[...] = acc_in[...]
    attend_seen(tab_ref, blocks, kv_refs, qm_ref, m_ref, acc_ref)


def attend_last_kernel(tab_ref, qm_ref, own_ref, m_in, acc_in, *rest, blocks):
    kv_refs, (att_ref, lse_ref, prob_ref, m_ref, acc_ref) = rest[:-5], rest[-5:]
    m_ref[...] = m_in[...]
    acc_ref[...] = acc_in[...]
    attend_seen(tab_ref, blocks, kv_refs, qm_ref, m_ref, acc_ref)
    lane = lax.broadcasted_iota(jnp.int32, (1, PAIR), 1)
    columns = []
    for p in range(HEADS // 2):
        first, second = acc_ref[2 * p], acc_ref[2 * p + 1]
        sums = pltpu.roll(jnp.where(lane < HEAD_DIM, second, first), HEAD_DIM, 1)
        att_ref[:, PAIR * p : PAIR * (p + 1)] = jnp.where(lane < HEAD_DIM, first, second) / sums
        columns.append(m_ref[2 * p][:, :1] + jnp.log(first[:, HEAD_DIM : HEAD_DIM + 1]))
        columns.append(m_ref[2 * p + 1][:, :1] + jnp.log(second[:, :1]))
    lse = jnp.concatenate(columns, 1).T
    lse_ref[...] = lse
    prob_ref[...] = jnp.exp(own_ref[...] - lse)


def gelu_parts(u):
    bell = jnp.exp(-0.5 * (u * u))
    t = 1.0 / (1.0 + (0.3275911 * 0.5**0.5) * jnp.abs(u))
    series = t * (0.127414796 + t * (-0.142248368 + t * (0.7107068705 + t * (-0.7265760135 + t * 0.5307027145))))
    tail = series * bell
    below = jnp.where(u >= 0.0, 1.0 - tail, tail)
    return u * below, below + u * (bell * 0.3989422804014327)


def feed_kernel(loads, tab_ref, x_ref, att_ref, g_ref, wo_ref, *rest, pieces, inverse_at):
    kv_refs = rest[:-11]
    out_ref, mid_ref, gh_ref, keep_ref, send_ref, kv_all, h_s, ht_s, out_s, buf_ref, sems = rest[-11:]
    copies = [
        pltpu.make_async_copy(kv_ref, kv_all.at[pl.ds(i, 1)], sems.at[3 + i]) for i, kv_ref in enumerate(kv_refs)
    ]
    for copy in copies:
        copy.start()
    rows, width = x_ref.shape
    hidden_rows = loads.held[4].shape[0]
    steps = hidden_rows // width
    down_rows = hidden_rows // pieces
    down_tiles = down_rows // TILE
    tiles = down_tiles + steps
    middle = x_ref[...].astype(single) + nn(att_ref[...].astype(narrow), wo_ref[...])
    mid_ref[...] = middle
    unit, _ = standardized(middle)
    h = (unit * loads[0][...] + loads[1][...]).astype(narrow)
    h_s[...] = h
    ht_s[...] = h.T
    g = g_ref[...]
    wu_ref, ub_ref, wd_ref, db_ref = (loads[i] for i in range(2, 6))
    small = buf_ref.shape[0] - 1
    place = lax.broadcasted_iota(jnp.int32, (TILE, width), 0)
    here = pieces // steps
    out_s[...] = middle + db_ref[...]
    gh_ref[...] = jnp.zeros_like(middle)

    def step(i, sums):
        cols = pl.ds(pl.multiple_of(i * width, width), width)
        act, slope = gelu_parts(nn(h_s[...], wu_ref[:, cols]) + ub_ref[:, cols])
        act = act.astype(narrow)
        out_s[...] += nn(act, wd_ref[cols, :])
        gu = (nt(g_ref[...], wd_ref[cols, :]) * slope).astype(narrow)
        gh_ref[...] += nt(gu, wu_ref[:, cols])
        grad_down = tn(act, g_ref[...]).astype(narrow)
        for j in range(here):
            at = tab_ref[inverse_at + i * here + j] * tiles
            store_tiles(buf_ref, at, grad_down[j * down_rows : (j + 1) * down_rows])
        grad_up = nn(ht_s[...], gu).astype(narrow)
        for j in range(pieces):
            buf_ref[tab_ref[inverse_at + j] * tiles + down_tiles + i] = grad_up[j * TILE : (j + 1) * TILE]
        return jnp.where(place == 1 + i, jnp.sum(gu.astype(single), 0, keepdims=True), sums)

    sums = lax.fori_loop(0, steps, step, jnp.zeros((TILE, width), single))
    unit, _ = standardized(mid_ref[...])
    gh = gh_ref[...]
    for row, value in ((0, g.astype(single)), (1 + steps, gh * unit), (2 + steps, gh)):
        sums = jnp.where(place == row, jnp.sum(value, 0, keepdims=True), sums)
    buf_ref[small] = sums.astype(narrow)
    out_ref[...] = out_s[...].astype(narrow)
    split_out(buf_ref, keep_ref, send_ref, sems, 1)
    for copy in copies:
        copy.wait()


def branch_kernel(
    loads, mid_ref, gh_ref, g_ref, att_ref, tv_ref, own_ref, wo_ref, gm_ref, gw_ref, ga_ref, dm_ref, delta_ref, ods_ref
):
    unit, spread = standardized(mid_ref[...])
    gm = g_ref[...].astype(single) + norm_back(gh_ref[...], unit, spread, loads[0][...])
    gm_ref[...] = gm
    branch = gm.astype(narrow)
    att = att_ref[...]
    ga = nt(branch, wo_ref[...]).astype(narrow)
    ga_ref[...] = ga
    split_heads(ga, dm_ref)
    wide = ga.astype(single)
    delta = head_sums(wide * att)
    delta_ref[...] = delta
    dprob = head_sums(wide * tv_ref[...].astype(single))
    ods_ref[...] = (own_ref[...] * (dprob - delta)).astype(narrow)
    gw_ref[...] = tn(att.astype(narrow), branch).astype(narrow)


def reorder_kernel(out_ref, gx_ref, to_out_ref, to_gx_ref):
    order = token_order(out_ref.shape[0])
    to_out_ref[...] = tn(order, out_ref[...]).astype(narrow)
    to_gx_ref[...] = tn(order, gx_ref[...]).astype(narrow)


def back_block(kv_ref, number, pair, qm_ref, dm_ref, lse_ref, delta_ref, diagonal):
    slots, width = kv_ref.shape[1], qm_ref.shape[2]
    cols = slice(PAIR * pair, PAIR * (pair + 1))
    k = kv_ref[number, :, cols]
    v = kv_ref[number, :, width + cols.start : width + cols.stop]
    lane = lax.broadcasted_iota(jnp.int32, (1, PAIR), 1)
    scores, probs = [], []
    for half in range(2):
        h = 2 * pair + half
        prob = jnp.exp(nt(k, qm_ref[half, :, cols]) - lse_ref[h : h + 1, :])
        dprob = nt(v, dm_ref[half, :, cols])
        if diagonal:
            slot = lax.broadcasted_iota(jnp.int32, prob.shape, 0)
            row = lax.broadcasted_iota(jnp.int32, prob.shape, 1)
            prob = jnp.where(3 * slot + 2 <= 3 * (row % slots) + row // slots, prob, 0.0)
        scores.append((prob * (dprob - delta_ref[h : h + 1, :])).astype(narrow))
        probs.append(prob.astype(narrow))
    dk = nn(scores[0], qm_ref[0, :, cols]) + nn(scores[1], qm_ref[1, :, cols])
    dv = nn(probs[0], dm_ref[0, :, cols]) + nn(probs[1], dm_ref[1, :, cols])
    nothing = jnp.zeros_like(k)
    split_k = jnp.concatenate([jnp.where(lane < HEAD_DIM, k, nothing), jnp.where(lane >= HEAD_DIM, k, nothing)], 0)
    return dk, dv, tn(jnp.concatenate(scores, 0), split_k)


def attend_back_kernel(
    tab_ref, qm_ref, dm_ref, lse_ref, delta_ref, kv_ref, dq_ref, keep_ref, send_ref, *, list_at, pair
):
    half, slots, _ = keep_ref.shape

    def store(number, dk, dv):
        @pl.when(number < half)
        def _():
            keep_ref[number, :, :PAIR] = dk
            keep_ref[number, :, PAIR:] = dv

        @pl.when(number >= half)
        def _():
            send_ref[number - half, :, :PAIR] = dk
            send_ref[number - half, :, PAIR:] = dv

    def step(i, carry):
        number = tab_ref[list_at + 1 + i]
        dk, dv, dq = back_block(kv_ref, number, pair, qm_ref, dm_ref, lse_ref, delta_ref, False)
        dq_ref[...] += dq
        store(number, dk.astype(narrow), dv.astype(narrow))
        return carry

    def clear(i, carry):
        nothing = jnp.zeros((slots, PAIR), narrow)
        store(tab_ref[list_at + 1 + i], nothing, nothing)
        return carry

    dq_ref[...] = jnp.zeros(dq_ref.shape, single)
    keep_ref[0] = jnp.zeros((slots, 2 * PAIR), narrow)
    lax.fori_loop(0, tab_ref[list_at], step, 0)
    lax.fori_loop(tab_ref[list_at], 2 * half - 1, clear, 0)


def attend_back_own_kernel(qm_ref, dm_ref, lse_ref, delta_ref, kv_ref, *rest, first):
    dq_in, (dq_ref, out_ref) = rest[:-2], rest[-2:]
    group = out_ref.shape[1] // 2
    for i, ref in enumerate(dq_in):
        dk, dv, dq = back_block(kv_ref, 0, first + i, qm_ref, dm_ref, lse_ref, delta_ref, True)
        cols = slice(PAIR * i, PAIR * (i + 1))
        dq_ref[:, cols] = ref[...] + dq
        out_ref[:, cols] = dk
        out_ref[:, group + PAIR * i : group + PAIR * (i + 1)] = dv


def sum_split_kernel(*refs, count, last):
    total = refs[0][...].astype(single)
    for ref in refs[1:count]:
        total += ref[...].astype(single)
    total = total.astype(narrow)
    outs = refs[count:]
    size = (total.shape[0] - last) // len(outs)
    for i, out_ref in enumerate(outs):
        if i == len(outs) - 1:
            out_ref[...] = total[i * size :]
        else:
            out_ref[pl.ds(0, size)] = total[i * size : (i + 1) * size]
            if last:
                out_ref[pl.ds(size, last)] = total[len(outs) * size :]


def sum_last_kernel(*refs, count, last):
    total = refs[0][...].astype(single)
    for ref in refs[1:count]:
        total += ref[...].astype(single)
    size = total.shape[0] - last
    refs[count][...] = total[:size].astype(narrow)
    refs[count + 1][...] = total[size:]


def join_kernel(*refs):
    parts, out_ref = refs[:-1], refs[-1]
    size = parts[0].shape[0]
    for i, ref in enumerate(parts):
        out_ref[pl.ds(i * size, size)] = ref[...]


def group_split_kernel(*refs):
    totals, (keep_ref, send_ref) = refs[:-2], refs[-2:]
    pairs = len(totals)
    half = keep_ref.shape[0]
    for pair, ref in enumerate(totals):
        for number in range(2):
            cols = slice(number * PAIR, (number + 1) * PAIR)
            first = (number * pairs + pair) * PAIR
            keep_ref[:, :, first : first + PAIR] = ref[pl.ds(0, half), :, cols]
            send_ref[:, :, first : first + PAIR] = ref[pl.ds(half, half), :, cols]


def store_tiles(buf_ref, first, values):
    for t in range(values.shape[0] // TILE):
        buf_ref[first + t] = values[t * TILE : (t + 1) * TILE]


def start_split(buf_ref, keep_ref, send_ref, sems, last):
    half = (buf_ref.shape[0] - last) // 2
    copies = [
        pltpu.make_async_copy(buf_ref.at[pl.ds(0, half)], keep_ref.at[pl.ds(0, half)], sems.at[0]),
        pltpu.make_async_copy(buf_ref.at[pl.ds(half, half + last)], send_ref, sems.at[1]),
    ]
    if last:
        copies.append(
            pltpu.make_async_copy(buf_ref.at[pl.ds(2 * half, last)], keep_ref.at[pl.ds(half, last)], sems.at[2])
        )
    for copy in copies:
        copy.start()
    return copies


def split_out(buf_ref, keep_ref, send_ref, sems, last):
    for copy in start_split(buf_ref, keep_ref, send_ref, sems, last):
        copy.wait()


def conv_grads(tab_ref, buf_ref, tk_ref, tv_ref, grad, tiles, pieces, inverse_at):
    width = tk_ref.shape[1]
    slots = grad.shape[0]
    group = grad.shape[1] // 2
    conv_tiles = TAPS * width // pieces // TILE
    for i in range(TAPS):
        own = slice(i * slots, (i + 1) * slots)
        both = jnp.concatenate([tn(tk_ref[own], grad[:, :group]), tn(tv_ref[own], grad[:, group:])], 1).astype(narrow)
        for j in range(width // TILE):
            tile = i * (width // TILE) + j
            at = tab_ref[inverse_at + tile // conv_tiles] * tiles + tile % conv_tiles
            for c in range(2 * group // COLUMNS):
                buf_ref[at + c * conv_tiles] = both[j * TILE : (j + 1) * TILE, c * COLUMNS : (c + 1) * COLUMNS]


def weight_grads(tab_ref, buf_ref, grad, first, tiles, pieces, inverse_at):
    for j in range(pieces):
        at = tab_ref[inverse_at + j] * tiles + first
        for c in range(grad.shape[1] // COLUMNS):
            buf_ref[at + c] = grad[j * TILE : (j + 1) * TILE, c * COLUMNS : (c + 1) * COLUMNS]


def middle_kernel(
    tab_ref, qm_ref, dm_ref, lse_ref, delta_ref, kv_ref, tk_ref, tv_ref, first_ref, second_ref, gw_out_ref, ck_ref, cv_ref,
    *rest, pieces, inverse_at,
):
    dq_refs, (gk_ref, gv_ref, dq_ref, keep_ref, send_ref, buf_ref, own_s, sems) = rest[:-8], rest[-8:]
    attend_back_own_kernel(qm_ref, dm_ref, lse_ref, delta_ref, kv_ref, *dq_refs, dq_ref, own_s, first=0)
    tiles = buf_ref.shape[0] // pieces
    blocks = gw_out_ref.shape[1] // COLUMNS
    grad = slot_grads(first_ref, second_ref, own_s)
    conv_grads(tab_ref, buf_ref, tk_ref, tv_ref, grad, tiles, pieces, inverse_at)
    weight_grads(tab_ref, buf_ref, gw_out_ref, tiles - blocks, tiles, pieces, inverse_at)
    copies = start_split(buf_ref, keep_ref, send_ref, sems, 0)
    conv_back(grad, ck_ref, cv_ref, 0, gk_ref, gv_ref)
    for copy in copies:
        copy.wait()


def tail_query_kernel(hid_ref, tk_ref, ods_ref, wq_ref, early_ref, later_ref, gh_ref, gw_ref):
    own_ds = tn(ods_ref[...], head_rows(tk_ref.shape[1])) * scale
    dq = jnp.concatenate([early_ref[...], later_ref[...]], 1)
    gq = (dq * scale + own_ds * tk_ref[...].astype(single)).astype(narrow)
    gw_ref[...] = tn(hid_ref[...], gq).astype(narrow)
    gh_ref[...] = nt(gq, wq_ref[...])


def slot_grads(*refs):
    return sum(ref[...].astype(single) for ref in refs).astype(narrow)


def conv_back(grads, ck_ref, cv_ref, first, gk_ref, gv_ref):
    slots, width = grads.shape[0], ck_ref.shape[1]
    group = grads.shape[1] // 2
    for grad, c_ref, out_ref in ((grads[:, :group], ck_ref, gk_ref), (grads[:, group:], cv_ref, gv_ref)):
        for i in range(TAPS):
            out_ref[i * slots : (i + 1) * slots] = nt(grad, c_ref[i * width : (i + 1) * width, first : first + group])


def tail_kernel(
    tab_ref, x_ref, hid_ref, q_ref, tk_ref, tv_ref, ga_ref, gm_ref, own_ref, ods_ref, gh_ref, gk0_ref, gv0_ref,
    first_ref, second_ref, own_grad_ref, gwq_ref, wk_ref, wv_ref, ck_ref, cv_ref, gain_ref, gx_ref, keep_ref, send_ref, buf_ref, gk_s, gv_s, sems, *, pieces, inverse_at,
):
    rows, width = x_ref.shape
    tiles = (buf_ref.shape[0] - 1) // pieces
    blocks = width // COLUMNS
    grad = slot_grads(first_ref, second_ref, own_grad_ref)
    conv_grads(tab_ref, buf_ref, tk_ref, tv_ref, grad, tiles, pieces, inverse_at)
    marks = head_rows(width)
    own_ds = tn(ods_ref[...], marks) * scale
    own_prob = tn(own_ref[...].astype(narrow), marks)
    conv_back(grad, ck_ref, cv_ref, width - grad.shape[1] // 2, gk_s, gv_s)
    gk = (gk_s[...] + gk0_ref[...] + own_ds * q_ref[...].astype(single)).astype(narrow)
    gv = (gv_s[...] + gv0_ref[...] + own_prob * ga_ref[...].astype(single)).astype(narrow)
    weight_grads(tab_ref, buf_ref, gwq_ref, tiles - 3 * blocks, tiles, pieces, inverse_at)
    hidden_t = hid_ref[...].T
    grad_hidden = gh_ref[...]
    for number, grad in enumerate((gk, gv)):
        grad_w = nn(hidden_t, grad).astype(narrow)
        weight_grads(tab_ref, buf_ref, grad_w, tiles - (2 - number) * blocks, tiles, pieces, inverse_at)
        grad_hidden += nt(grad, (wk_ref, wv_ref)[number][...])
    unit, spread = standardized(x_ref[...].astype(single))
    place = lax.broadcasted_iota(jnp.int32, (TILE, COLUMNS), 0)
    sums = jnp.zeros((TILE, COLUMNS), single)
    for first, value in ((0, grad_hidden * unit), (blocks, grad_hidden)):
        total = jnp.sum(value, 0, keepdims=True)
        for c in range(blocks):
            sums = jnp.where(place == first + c, total[:, c * COLUMNS : (c + 1) * COLUMNS], sums)
    buf_ref[buf_ref.shape[0] - 1] = sums.astype(narrow)
    split_out(buf_ref, keep_ref, send_ref, sems, 1)
    gx_ref[...] = (gm_ref[...] + norm_back(grad_hidden, unit, spread, gain_ref[...])).astype(narrow)


def unpack_feed_kernel(
    tab_ref, own_ref, other_ref, small_ref, wd_ref, wu_ref, gain_ref, bias_ref, up_ref, down_ref, *, pieces, piece_at
):
    width = wd_ref.shape[1]
    down_rows = wd_ref.shape[0] // pieces
    down_tiles, up_tiles = down_rows // TILE, wu_ref.shape[1] // width
    tiles = down_tiles + up_tiles
    down_ref[...] = small_ref[0, 0:1, :]
    for t in range(up_tiles):
        up_ref[:, t * width : (t + 1) * width] = small_ref[0, 1 + t : 2 + t, :]
    gain_ref[...] = small_ref[0, 1 + up_tiles : 2 + up_tiles, :]
    bias_ref[...] = small_ref[0, 2 + up_tiles : 3 + up_tiles, :]

    for number, buf_ref in enumerate((own_ref, other_ref)):

        def step(k, carry, number=number, buf_ref=buf_ref):
            piece = tab_ref[piece_at + number * pieces // 2 + k]
            at = k * tiles
            for t in range(down_tiles):
                rows = pl.ds(pl.multiple_of(piece * down_rows + t * TILE, TILE), TILE)
                wd_ref[rows, :] = buf_ref[at + t].astype(single)
            mine = pl.ds(pl.multiple_of(piece * TILE, TILE), TILE)
            for t in range(up_tiles):
                wu_ref[mine, t * width : (t + 1) * width] = buf_ref[at + down_tiles + t].astype(single)
            return carry

        lax.fori_loop(0, pieces // 2, step, 0, unroll=4)


def unpack_kernel(tab_ref, *rest, parts, half, piece_at, first_column, outs, small):
    bufs, rest = rest[: len(parts)], rest[len(parts) :]
    if small:
        small_ref, small_outs, rest = rest[0], rest[-5 - outs : -3 - outs], rest[1:]
        for i, ref in enumerate(small_outs):
            ref[...] = small_ref[0, i : i + 1, :]
    out_refs, (conv_s, weight_s, sems) = rest[-outs - 3 : -3], rest[-3:]
    weight_refs, conv_refs = out_refs[:-2], out_refs[-2:]
    conv_rows, columns = conv_s.shape[2], conv_s.shape[3]
    conv_tiles = conv_rows // TILE
    blocks = weight_s.shape[3] // COLUMNS
    weights_at = conv_tiles * (2 * columns // COLUMNS)
    tiles = weights_at + blocks * len(weight_refs)

    def copies(number, place):
        piece = tab_ref[piece_at + place]
        rows = pl.ds(pl.multiple_of(piece * conv_rows, TILE), conv_rows)
        mine = pl.ds(pl.multiple_of(piece * TILE, TILE), TILE)
        cols = pl.ds(first_column, columns)
        return [
            pltpu.make_async_copy(conv_s.at[number, i], ref.at[rows, cols], sems.at[number, i])
            for i, ref in enumerate(conv_refs)
        ] + [
            pltpu.make_async_copy(weight_s.at[number, i], ref.at[mine], sems.at[number, 2 + i])
            for i, ref in enumerate(weight_refs)
        ]

    for order, (buf_ref, part) in enumerate(zip(bufs, parts)):

        def step(k, carry, order=order, buf_ref=buf_ref, part=part):
            number = order * half + k
            for t in range(conv_tiles):
                for unit in range(2 * columns // PAIR):
                    which, first = unit * PAIR // columns, unit * PAIR % columns
                    block, lanes = unit * PAIR // COLUMNS, unit * PAIR % COLUMNS
                    conv_s[number, which, t * TILE : (t + 1) * TILE, first : first + PAIR] = buf_ref[
                        k * tiles + block * conv_tiles + t, :, lanes : lanes + PAIR
                    ].astype(single)
            for t in range(len(weight_refs)):
                for c in range(blocks):
                    weight_s[number, t, :, c * COLUMNS : (c + 1) * COLUMNS] = buf_ref[
                        k * tiles + weights_at + t * blocks + c
                    ].astype(single)
            for copy in copies(number, part * half + k):
                copy.start()
            return carry

        lax.fori_loop(0, half, step, 0)

    for order, part in enumerate(parts):

        def finish(k, carry, order=order, part=part):
            for copy in copies(order * half + k, part * half + k):
                copy.wait()
            return carry

        lax.fori_loop(0, half, finish, 0)


def shaped(shape, kind):
    return jax.ShapeDtypeStruct(shape, kind)


def per_device(
    seq_size, batch_size,
    inputs, cotangent, ln1_gain, ln1_bias, w_query, w_key, w_value, conv_key, conv_value, w_out,
    ln2_gain, ln2_bias, w_up, up_bias, w_down, down_bias,
):
    x, g = inputs[0], cotangent[0]
    rows, width = x.shape
    slots = rows // TAPS
    ff = w_up.shape[1]
    seq_bits, batch_bits = seq_size.bit_length() - 1, batch_size.bit_length() - 1
    split_bits = min(5, seq_bits + batch_bits)
    pieces = 1 << split_bits
    list_at = seq_size
    piece_at = list_at + seq_size
    inverse_at = piece_at + pieces
    tables = jnp.asarray(plan_tables(seq_size, batch_size, split_bits))
    table = lax.dynamic_index_in_dim(
        tables, lax.axis_index("seq") * batch_size + lax.axis_index("batch"), 0, keepdims=False
    )
    x = tied(x, table)
    row = lambda v: v.reshape(1, -1)
    ck = conv_key.reshape(TAPS * width, width)
    cv = conv_value.reshape(TAPS * width, width)
    token_low, token_wide = shaped((rows, width), narrow), shaped((rows, width), single)
    head_wide, head_low = shaped((HEADS, rows), single), shaped((HEADS, rows), narrow)
    two_low = shaped((2, rows, width), narrow)

    xp, hidden, tk, tv, kv = call(
        "front",
        front_kernel,
        (token_low,) * 4 + (shaped((slots, 2 * width), narrow),),
        loads=(x, row(ln1_gain), row(ln1_bias), w_key, ck, w_value, cv),
        mib=24,
        flops=4e9,
    )

    state = shaped((HEADS, rows, PAIR), single)
    q, gp, qm, own, m, acc = call(
        "attend_own",
        attend_own_kernel,
        (token_low, token_low, two_low, head_wide, state, state),
        loads=(w_query, g),
        operands=(hidden, tk, tv, kv[None]),
        mib=16,
        flops=1e10,
    )
    blocks = {0: kv[None]}
    rounds = gather_plan(seq_size)
    calls = []
    for number, found in enumerate(rounds):
        if number > 0:
            calls.append([entry[0] for entry in rounds[number - 1]])
        held = {source: blocks[source] for _, source, _ in found if source in blocks}
        if number > 1:
            held = tied(held, m)
        for block, source, (axis, pairs) in found:
            if source in held:
                blocks[block] = lax.ppermute(held[source], axis, pairs)
        if number == 0:
            continue
        later = [entry for entry in found if entry[0] not in blocks]
        halves = [[k for k in calls[-1] if k < seq_size // 2], [k for k in calls[-1] if k >= seq_size // 2]]
        for found in halves:
            if not found:
                continue
            m, acc = call(
                f"attend_{found[0]}",
                functools.partial(attend_more_kernel, blocks=found),
                (state, state),
                table=table,
                operands=(qm, m, acc, *[blocks[k] for k in found]),
                mib=8,
                flops=1e11,
            )
            if later:
                for block, source, (axis, pairs) in later:
                    blocks[block] = lax.ppermute(tied(blocks[source], m), axis, pairs)
                later = []
    calls.append([entry[0] for entry in rounds[-1]])
    attended, lse, own_prob = call(
        "attend_last",
        functools.partial(attend_last_kernel, blocks=calls[-1]),
        (token_wide, head_wide, head_wide),
        table=table,
        operands=(qm, own, m, acc, *[blocks[k] for k in calls[-1]]),
        scratch=[pltpu.VMEM(state.shape, single), pltpu.VMEM(state.shape, single)],
        mib=16,
        flops=1e10 * len(calls[-1]),
    )

    steps = ff // width
    tiles = ff // pieces // TILE + steps
    half = shaped((pieces // 2 * tiles + 1, TILE, width), narrow)
    output, middle, grad_normal, keep, send, all_kv = call(
        "feed",
        functools.partial(feed_kernel, pieces=pieces, inverse_at=inverse_at),
        (token_low, token_wide, token_wide, half, half, shaped((seq_size, slots, 2 * width), narrow)),
        loads=(row(ln2_gain), row(ln2_bias), w_up, row(up_bias), w_down, row(down_bias)),
        table=table,
        operands=(xp, attended, gp, w_out),
        away=[blocks[k] for k in range(seq_size)],
        away_outs=3,
        scratch=[
            pltpu.VMEM((rows, width), narrow),
            pltpu.VMEM((width, rows), narrow),
            pltpu.VMEM((rows, width), single),
            pltpu.VMEM((pieces * tiles + 1, TILE, width), narrow),
            pltpu.SemaphoreType.DMA((3 + seq_size,)),
        ],
        mib=30,
        flops=5e10,
    )
    grad_middle, grad_w_out_here, grad_attended, dm, delta, own_ds = call(
        "branch",
        branch_kernel,
        (token_wide, shaped((width, width), narrow), token_low, two_low, head_wide, head_low),
        loads=(row(ln2_gain),),
        operands=(middle, grad_normal, gp, attended, tv, own_prob, w_out),
        mib=16,
        flops=1e11,
    )

    stages = reduce_stages(seq_size, batch_size, split_bits)
    gather_back = [stage for stage in stages if stage[0] > 1][::-1]
    unseen = gather_stages(seq_size)[::-1]
    head_pairs = HEADS // 2

    wide_grant = 12 if seq_size <= 8 else 56
    share = shaped((seq_size // 2, slots, 2 * PAIR), narrow)

    def back(pair, qm):
        return call(
            f"attend_back_{pair}",
            functools.partial(attend_back_kernel, list_at=list_at, pair=pair),
            (shaped((rows, PAIR), single), share, share),
            table=table,
            operands=(qm, dm, lse, delta, all_kv),
            mib=wide_grant,
            flops=1e11,
        )

    def small_call(kernel, name, outs, *operands):
        return call(name, kernel, outs, operands=operands, mib=4, flops=sum(v.size for v in operands) * 600)

    def sum_split(buffers, last, cut):
        count, rest = buffers[0].shape[0], buffers[0].shape[1:]
        outs = (shaped(((count - last) // cut + last, *rest), narrow),) * cut
        kernel = functools.partial(sum_split_kernel, count=len(buffers), last=last)
        return small_call(kernel, "sum_split", outs, *buffers)

    def join(*parts):
        out = shaped((len(parts) * parts[0].shape[0], *parts[0].shape[1:]), narrow)
        return small_call(join_kernel, "join", (out,), *parts)[0]

    def exchange(stage, parts):
        return [lax.ppermute(part, stage[1], pairs) for part, pairs in zip(parts, stage[2])]

    class Sum:
        def __init__(self, keep, send, last):
            self.keep, self.last, self.at = keep, last, 0
            self.arrived = exchange(stages[0], [send])

        def step(self, *others):
            arrived = tied(self.arrived, *others)
            self.at += 1
            if self.at < len(stages):
                cut = stages[self.at][0]
                parts = sum_split((self.keep, *arrived), self.last, cut)
                self.keep, sent = parts[0], parts[1:] if cut > 1 else parts
                self.arrived = exchange(stages[self.at], sent)
                return sent[0]
            if self.at == len(stages):
                buffers = (self.keep, *arrived)
                if self.last:
                    count, rest = buffers[0].shape[0], buffers[0].shape[1:]
                    outs = (shaped((count - self.last, *rest), narrow), shaped((self.last, *rest), single))
                    kernel = functools.partial(sum_last_kernel, count=len(buffers), last=self.last)
                    self.held, self.small = small_call(kernel, "sum_last", outs, *buffers)
                else:
                    (self.held,) = sum_split(buffers, 0, 1)
            else:
                self.held = join(self.held, *arrived)
            stage = gather_back[self.at - len(stages)]
            self.arrived = exchange(stage, [self.held] * len(stage[2]))
            return self.held

        def left(self):
            return len(stages) + len(gather_back) - 1 - self.at

    class Group:
        def __init__(self):
            self.shares, self.at = [], 0

        def step(self, *others):
            self.at += 1
            if self.at == 1:
                operands = tied(self.shares, *others)
                half = shaped((seq_size // 4, slots, len(self.shares) * 2 * PAIR), narrow)
                self.keep, send = small_call(group_split_kernel, "group_split", (half, half), *operands)
            else:
                self.keep, send = sum_split((self.keep, tied(self.arrived, *others)), 0, 2)
            self.arrived = lax.ppermute(send, *unseen[self.at])
            return send

        def left(self):
            return len(unseen) - 1 - self.at

    conv_tiles = TAPS * width // pieces // TILE
    blocks_wide = width // COLUMNS
    first_tiles, tail_tiles = (
        conv_tiles * (group * 2 * PAIR // COLUMNS) + count * blocks_wide for group, count in zip(GROUPS, (1, 3))
    )

    sums = {"feed": Sum(keep, send, 1)}
    first_group, second_group = Group(), Group()
    waits = [sums["feed"].step(delta)]
    state_back = {"grads": []}

    def advance(name, kept=0):
        if name in sums and sums[name].left() > kept:
            waits.append(sums[name].step(*waits))

    def advance_group(group):
        if group.left() > 0:
            waits.append(group.step(*waits))

    def add_share(group, kept, arrived):
        (total,) = sum_split(tied((kept, arrived), *waits), 0, 1)
        waits.append(total)
        group.shares.append(total)

    partial_q, pending = [], None
    for pair in range(head_pairs):
        in_first = pair < GROUPS[0]
        grads, kept, sent = back(pair, tied(qm, *waits))
        waits = [grads]
        partial_q.append(grads)
        if pair < head_pairs - 1:
            advance("feed", 1)
        if pending is not None:
            add_share(*pending)
        pending = (first_group if in_first else second_group, kept, lax.ppermute(sent, *unseen[0]))
        if pair >= GROUPS[0]:
            advance_group(first_group)
    def own_block(first, count):
        return call(
            f"attend_back_own_{first}",
            functools.partial(attend_back_own_kernel, first=first),
            (shaped((rows, count * PAIR), single), shaped((slots, count * 2 * PAIR), single)),
            operands=(tied(qm, *waits), dm, lse, delta, kv[None], *partial_q[first : first + count]),
            mib=12,
            flops=1e11,
        )

    later_q, second_own = own_block(GROUPS[0], GROUPS[1])
    waits = [later_q]
    add_share(*pending)
    advance_group(second_group)
    advance("feed", 1)
    while first_group.left() > 0:
        advance_group(first_group)
    half = shaped((pieces // 2 * first_tiles, TILE, COLUMNS), narrow)
    grad_k, grad_v, early_q, keep0, send0 = call(
        "middle",
        functools.partial(middle_kernel, pieces=pieces, inverse_at=inverse_at),
        (token_wide, token_wide, shaped((rows, GROUPS[0] * PAIR), single), half, half),
        table=table,
        operands=(
            tied(qm, *waits), dm, lse, delta, kv[None], tk, tv, first_group.keep[0], first_group.arrived[0],
            grad_w_out_here, ck, cv, *partial_q[: GROUPS[0]],
        ),
        away_outs=2,
        scratch=[
            pltpu.VMEM((pieces * first_tiles, TILE, COLUMNS), narrow),
            pltpu.VMEM((slots, GROUPS[0] * 2 * PAIR), single),
            pltpu.SemaphoreType.DMA((3,)),
        ],
        mib=24,
        flops=1e11,
    )
    sums["first"] = Sum(keep0, send0, 0)
    waits = [grad_k]
    advance("feed", 1)
    advance_group(second_group)
    grad_hidden, grad_wq_here = call(
        "tail_query",
        tail_query_kernel,
        (token_wide, shaped((width, width), narrow)),
        operands=(tied(hidden, *waits), tk, own_ds, w_query, early_q, later_q),
        mib=16,
        flops=1e11,
    )
    waits = [grad_hidden]
    while second_group.left() > 0:
        advance_group(second_group)
    advance("first")
    half = shaped((pieces // 2 * tail_tiles + 1, TILE, COLUMNS), narrow)
    grad_x, keep1, send1 = call(
        "tail",
        functools.partial(tail_kernel, pieces=pieces, inverse_at=inverse_at),
        (token_low, half, half),
        table=table,
        operands=(
            xp, hidden, q, tk, tv, grad_attended, grad_middle, own_prob, own_ds, grad_hidden, grad_k, grad_v,
            tied(second_group.keep[0], *waits), second_group.arrived[0], second_own, grad_wq_here,
            w_key, w_value, ck, cv, row(ln1_gain),
        ),
        away_outs=2,
        scratch=[
            pltpu.VMEM((pieces * tail_tiles + 1, TILE, COLUMNS), narrow),
            pltpu.VMEM((rows, width), single),
            pltpu.VMEM((rows, width), single),
            pltpu.SemaphoreType.DMA((3,)),
        ],
        mib=26,
        flops=1e11,
    )
    sums["second"] = Sum(keep1, send1, 1)
    waits = [grad_x]

    def unpack(name, parts, heads, weights, bufs, *known, small=()):
        count = len(parts) * pieces // 2
        outs = [shaped((width, width), single)] * weights + [shaped(ck.shape, single)] * 2
        first = [shaped((1, width), single)] * (2 * len(small))
        return call(
            name,
            functools.partial(
                unpack_kernel,
                parts=parts,
                half=pieces // 2,
                piece_at=piece_at,
                first_column=heads[0] * PAIR,
                outs=len(outs),
                small=len(small),
            ),
            first + outs,
            table=table,
            operands=(*bufs, *small),
            away=known,
            away_outs=len(outs),
            in_place=len(known),
            scratch=[
                pltpu.VMEM((count, 2, conv_tiles * TILE, heads[1] * PAIR), single),
                pltpu.VMEM((count, weights, TILE, width), single),
                pltpu.SemaphoreType.DMA((count, len(outs))),
            ],
            mib=20,
            flops=1e11,
        )

    def finish_feed(*others):
        vector = shaped((1, width), single)
        return call(
            "unpack_feed",
            functools.partial(unpack_feed_kernel, pieces=pieces, piece_at=piece_at),
            (shaped((ff, width), single), shaped((width, ff), single), vector, vector, shaped((1, ff), single), vector),
            table=table,
            operands=(sums["feed"].held, tied(sums["feed"].arrived[0], *others), sums["feed"].small),
            mib=16,
            flops=2e10,
        )

    places = (GROUPS[0], GROUPS[1])
    for action in "F0R010010101F011F110Uu1":
        if action in "01F":
            advance({"0": "first", "1": "second", "F": "feed"}[action])
            waits = waits[-1:]
        elif action == "R":
            output, grad_x = call(
                "reorder",
                reorder_kernel,
                (token_low, token_low),
                operands=(output, tied(grad_x, *waits)),
                mib=8,
                flops=1e11,
            )
            waits.append(grad_x)
        elif action == "U":
            while sums["feed"].left() > 0:
                advance("feed")
            grad_w_down, grad_w_up, *small_feed = finish_feed(*waits)
            waits.append(grad_w_up)
        elif action == "u":
            while sums["first"].left() > 0:
                advance("first")
            while sums["second"].left() > 1:
                advance("second")
            grad_w_out, *convs = unpack(
                "unpack_first",
                (0, 1),
                (0, GROUPS[0]),
                1,
                (sums["first"].held, tied(sums["first"].arrived[0], *waits)),
            )
            waits.append(grad_w_out)
    last = sums["second"]
    small_first, small_second, *found = unpack(
        "unpack_own", (0,), places, 3, (last.held,), *tied(convs, *waits), small=(last.small,)
    )
    grad_wq, grad_wk, grad_wv, grad_ck, grad_cv = unpack(
        "unpack_last", (1,), places, 3, (last.arrived[0],), *found
    )
    return (
        output[None],
        grad_x[None],
        small_first[0],
        small_second[0],
        grad_wq,
        grad_wk,
        grad_wv,
        grad_ck.reshape(conv_key.shape),
        grad_cv.reshape(conv_value.shape),
        grad_w_out,
        small_feed[0][0],
        small_feed[1][0],
        grad_w_up,
        small_feed[2][0],
        grad_w_down,
        small_feed[3][0],
    )


def solution(mesh):
    placed = (P("batch", "seq", None),) * 2 + (P(),) * 14
    return jax.shard_map(
        functools.partial(per_device, mesh.shape["seq"], mesh.shape["batch"]),
        mesh=mesh,
        in_specs=placed,
        out_specs=placed,
        check_vma=False,
    )
```
